32 devices in a mesh: groups: 2 (over x), rows: 16 (over z, y, core).
Axes of the slice: x: 2, y: 2, z: 4, core: 2. Of those that a mesh axis runs over, the one named last changes fastest.
Arguments:
- grid_inputs: bfloat16 [474, 4096], P(None, ('groups', 'rows')), parts along dimension 1, may hold values from -6 to 6
- link_features: float32 [4, 4096], P(None, 'rows'), may hold values from -6 to 6
- link_partition: int32 [2048, 2], P('rows'), may hold values from 0 to 15, all different within a row; in each aligned block of 128 rows (0 to 127, 128 to 255, ...) at most 32 rows name the same one
- link_node: int32 [2048, 2], P('rows'), may hold values from 0 to 383
- mesh_start: bfloat16 [6144, 512], P('rows'), may hold values from -6 to 6
- edge_features: float32 [4, 49152], P(None, 'rows'), may hold values from -6 to 6
- edge_senders: int32 [6144, 8], P('rows'), may hold values from 0 to 639, as said below
- halo_lists: int32 [16, 16, 16], P('rows'), may hold values from -1 to 383, as said below
- embed_first: bfloat16 [474, 512], replicated, may hold values from -0.25 to 0.25
- embed_second: bfloat16 [512, 512], replicated, may hold values from -0.25 to 0.25
- link_embed: float32 [4, 512], replicated, may hold values from -3 to 3
- link_first: bfloat16 [1536, 512], replicated, may hold values from -0.15625 to 0.15625
- link_second: bfloat16 [512, 512], replicated, may hold values from -0.25 to 0.25
- update_first: bfloat16 [1024, 512], replicated, may hold values from -0.1875 to 0.1875
- update_second: bfloat16 [512, 512], replicated, may hold values from -0.25 to 0.25
- edge_embed: float32 [4, 512], replicated, may hold values from -3 to 3
- process_first: bfloat16 [2, 1536, 512], replicated, may hold values from -0.15625 to 0.15625
- process_second: bfloat16 [2, 512, 512], replicated, may hold values from -0.25 to 0.25
- process_update_first: bfloat16 [2, 1024, 512], replicated, may hold values from -0.1875 to 0.1875
- process_update_second: bfloat16 [2, 512, 512], replicated, may hold values from -0.25 to 0.25
- update_gain: float32 [3, 512], replicated, may hold values from 0.5 to 1.5
Outputs:
- mesh_state: bfloat16 [12288, 512], P(('groups', 'rows')), parts along dimension 0
The draws below stay inside these ranges and needn't reach their ends.
There are 2 independent parts, one for each index of `groups`. The reference program is written for one: setup_inputs(seed, part) draws one part's arguments, and reference() takes and returns one part's arrays. A program takes and returns all parts, laid end to end along the dimension named above; an argument that names none is the same for every part. Nothing has to cross between parts.
Inputs may be any that keep to these rules, and one draw needn't show every extreme that they name: `link_partition`: the 2 partitions named by one cell differ. Among the cells of one slab no partition is named more than 32 times, and some slab names some partition exactly 32 times. Every partition is named. `halo_lists`: each entry is a node index of the owning device o, or -1 for an empty slot; filled slots come first in every list. The lists of o to the devices o + 1 and o - 1 (modulo 16) are full; its list to o + 8 holds exactly 4 nodes; any other list to another device holds at most 4; the list to itself is empty. `edge_senders`: an entry s below 384 is node s of the receiving node's own partition d; an entry s = 384 + o * 16 + t names slot t of halo_lists[o, d], which is filled. Every filled slot of a list to d is named by some edge of a node of d.
All inputs are finite; a program needn't handle non-finite values.
Results may differ from the reference program's by a relative error of at most 0.015.
Values may be sent and summed in bfloat16 or wider, within the bound.
No kernel may reach another device: no remote copies, remote signals or barrier semaphores. Data moves between devices by JAX's collectives and lax.ppermute only.
A program may use at most 128 MiB of HBM per device.

```python
import math
import jax
import jax.numpy as jnp
import numpy as np
from jax import lax

LAT = 512
CIN = 474
EF = 4
K = 2
DEG = 8
HCAP = 16
FARCAP = 4
STEPS = 2
G_DEV = 128
M_DEV = 384
GRID = 2048
MESH = 6144
CAP = 32
N_ROWS = 16


def halo_layout(key):
    count_key, node_key = jax.random.split(key)
    owners = jnp.arange(N_ROWS, dtype=jnp.int32)[:, None]
    readers = jnp.arange(N_ROWS, dtype=jnp.int32)[None, :]
    offset = (readers - owners) % N_ROWS
    drawn = jax.random.randint(count_key, (N_ROWS, N_ROWS), 0, FARCAP + 1)
    filled = jnp.where(offset == N_ROWS // 2, FARCAP, drawn)
    filled = jnp.where((offset == 1) | (offset == N_ROWS - 1), HCAP, filled)
    filled = jnp.where(offset == 0, 0, filled).astype(jnp.int32)
    node_ids = jax.random.randint(node_key, (N_ROWS, N_ROWS, HCAP), 0, M_DEV)
    places = jnp.arange(HCAP, dtype=jnp.int32)[None, None, :]
    lists = jnp.where(places < filled[:, :, None], node_ids, -1).astype(jnp.int32)
    return (lists, filled)


def draw_halo_lists(key, part):
    lists, filled = halo_layout(key)
    return lists


def draw_edge_senders(key, part):
    lists, filled = halo_layout(key)
    key = jax.random.fold_in(key, 7)
    edge_total = M_DEV * DEG
    slot_total = N_ROWS * HCAP

    def one_device(device_key, device):
        order_key, place_key, pick_key, kind_key, local_key = jax.random.split(device_key, 5)
        arrived = filled[:, device]
        valid = (jnp.arange(HCAP, dtype=jnp.int32)[None, :] < arrived[:, None]).reshape(-1)
        extended = M_DEV + jnp.arange(slot_total, dtype=jnp.int32)
        ranking = jnp.where(valid, 0, 1) * 1048576 + jax.random.randint(order_key, (slot_total,), 0, 1048576)
        ranked = extended[jnp.argsort(ranking, stable=True)]
        valid_total = jnp.sum(valid.astype(jnp.int32))
        placed = jax.random.permutation(place_key, edge_total).astype(jnp.int32)
        picked = ranked[jax.random.randint(pick_key, (edge_total,), 0, 1048576) % valid_total]
        choose_kind = jax.random.randint(kind_key, (edge_total,), 0, 4)
        local_ids = jax.random.randint(local_key, (edge_total,), 0, M_DEV)
        leading = ranked[jnp.clip(placed, 0, slot_total - 1)]
        chosen = jnp.where(placed < valid_total, leading, jnp.where(choose_kind == 0, picked, local_ids))
        return chosen.reshape(M_DEV, DEG).astype(jnp.int32)
    devices = jnp.arange(N_ROWS, dtype=jnp.int32)
    device_keys = jax.vmap(lambda device: jax.random.fold_in(key, device))(devices)
    result = jax.vmap(one_device)(device_keys, devices)
    return result.reshape(N_ROWS * M_DEV, DEG)


def touch_ends(entries, rng, least, largest):
    spot = [jax.random.randint(jax.random.fold_in(rng, axis), (), 0, length) for axis, length in enumerate(entries.shape)]
    widest = entries.shape.index(max(entries.shape))
    neighbour = spot[:widest] + [(spot[widest] + 1) % entries.shape[widest]] + spot[widest + 1:]
    return entries.at[tuple(spot)].set(least).at[tuple(neighbour)].set(largest)


def block_scale(stream_key, shape, cuts, smallest, largest):
    def one(dim, shards_of):
        draws = jax.random.uniform(jax.random.fold_in(jax.random.fold_in(stream_key, 6), dim), (shards_of,), jnp.float32, smallest / len(cuts), largest / len(cuts))
        return jnp.repeat(jnp.exp(draws), shape[dim] // shards_of).reshape((-1,) + (1,) * (len(shape) - dim - 1))

    loudness = one(*cuts[0])
    for cut in cuts[1:]:
        loudness = loudness * one(*cut)
    return loudness


def assign_block(stream_key, own, number, rows, amount, top, reach, slope):
    order = jax.random.permutation(stream_key, amount)
    heavy_load, ordinary = shares(amount, rows * top, reach, slope, True), shares(amount, rows * top, reach, slope, False)
    places = jnp.arange(amount)

    def named(tallies, rotation):
        used = int((tallies > 0).sum())
        fixed = max(1, used // 4)
        passed = fixed + (places - fixed + rotation * (used - fixed)) % max(1, amount - fixed)
        return jnp.zeros((amount,), jnp.int32).at[order[jnp.where(places < fixed, places, passed)]].set(jnp.asarray(tallies, jnp.int32))

    tallies = jnp.where(number % 4 == 0, named(heavy_load, number // 4), named(ordinary, number - number // 4 - 1))
    mixed = jax.random.permutation(jax.random.fold_in(own, 3), amount)
    source_of, sink = mixed[0:amount // 2 * 2:2], mixed[1:amount // 2 * 2:2]
    slack = jnp.minimum(tallies[source_of] - 1, reach - tallies[sink]) // 2
    slack = jnp.where((source_of == order[0]) | (sink == order[0]) | (tallies[sink] == 0), 0, jnp.maximum(slack, 0))
    passed = jax.random.randint(jax.random.fold_in(own, 4), (amount // 2,), 0, 1 << 20) % (slack + 1)
    tallies = tallies.at[source_of].add(-passed).at[sink].add(passed)
    members = jnp.searchsorted(jnp.cumsum(tallies), jnp.arange(rows * top), side="right").astype(jnp.int32)
    table = members.reshape(top, rows).T
    table = table[jax.random.permutation(jax.random.fold_in(own, 1), rows)]
    rotation = jax.random.randint(jax.random.fold_in(own, 2), (rows, 1), 0, top)
    return jnp.take_along_axis(table, (jnp.arange(top)[None, :] + rotation) % top, axis=1)


def shares(number_of, total, bound, slope, full):
    weights = [(1 << 20) // math.isqrt(grade ** slope) + 1 for grade in range(1, number_of + 1)]
    largest = bound if full else min(bound, max(-(-total // number_of), total * weights[0] // sum(weights)))
    least = 1 if total - largest >= number_of - 1 else 0
    given, surplus = [largest] + [least] * (number_of - 1), total - largest - least * (number_of - 1)
    while surplus > 0:
        movable = [i for i in range(1, number_of) if given[i] < largest] or [i for i in range(1, number_of) if given[i] < bound]
        mass, remaining = sum([weights[i] for i in movable]), surplus
        for i in movable:
            extra = min(bound - given[i], max(1, remaining * weights[i] // mass), surplus)
            given[i] = given[i] + extra
            surplus = surplus - extra
    return np.array(given)


def noise(key, extent, width, reach, pieces=(), kind=jnp.bfloat16):
    values = width * jax.random.normal(key, extent, jnp.float32)
    if pieces:
        values = values * block_scale(key, extent, pieces, -0.22, 0.18)
    return jnp.clip(values, -reach, reach).astype(kind)


def setup_inputs(seed: int = 0, part: int = 0) -> dict:
    streams_of = jax.random.split(jax.random.key(seed), 22)
    part_splits = jax.random.split(jax.random.fold_in(streams_of[21], part), 22)
    grid_inputs = noise(part_splits[0], (CIN, GRID), 1.0, 6.0, ((1, 16),))
    link_features = noise(streams_of[1], (EF, GRID * K), 1.0, 6.0, ((1, 16),), jnp.float32)
    link_partition_keys = jax.random.split(jax.random.fold_in(streams_of[2], 1), GRID // G_DEV)
    link_partition_turns = jax.random.permutation(jax.random.fold_in(streams_of[2], 3), GRID // G_DEV)
    link_partition = jax.vmap(lambda own, number: assign_block(jax.random.fold_in(streams_of[2], 2), own, number, G_DEV, N_ROWS, K, CAP, 2))(link_partition_keys, link_partition_turns).reshape((GRID, K))
    link_node = touch_ends(jax.random.randint(streams_of[3], (GRID, K), 0, M_DEV), jax.random.fold_in(streams_of[3], 1), 0, M_DEV - 1).astype(jnp.int32)
    mesh_start = noise(streams_of[4], (MESH, LAT), 1.0, 6.0, ((0, 16),))
    edge_features = noise(streams_of[5], (EF, MESH * DEG), 1.0, 6.0, ((1, 16),), jnp.float32)
    edge_senders = draw_edge_senders(jax.random.fold_in(streams_of[21], 71), part)
    halo_lists = draw_halo_lists(jax.random.fold_in(streams_of[21], 71), part)
    embed_first = noise(streams_of[8], (CIN, LAT), CIN ** -0.5, 0.25)
    embed_second = noise(streams_of[9], (LAT, LAT), LAT ** -0.5, 0.25)
    link_embed = noise(streams_of[10], (EF, LAT), EF ** -0.5, 3.0, (), jnp.float32)
    link_first = noise(streams_of[11], (3 * LAT, LAT), (3 * LAT) ** -0.5, 0.15625)
    link_second = noise(streams_of[12], (LAT, LAT), LAT ** -0.5, 0.25)
    update_first = noise(streams_of[13], (2 * LAT, LAT), (2 * LAT) ** -0.5, 0.1875)
    update_second = noise(streams_of[14], (LAT, LAT), LAT ** -0.5, 0.25)
    edge_embed = noise(streams_of[15], (EF, LAT), EF ** -0.5, 3.0, (), jnp.float32)
    process_first = noise(streams_of[16], (STEPS, 3 * LAT, LAT), (3 * LAT) ** -0.5, 0.15625)
    process_second = noise(streams_of[17], (STEPS, LAT, LAT), LAT ** -0.5, 0.25)
    process_update_first = noise(streams_of[18], (STEPS, 2 * LAT, LAT), (2 * LAT) ** -0.5, 0.1875)
    process_update_second = noise(streams_of[19], (STEPS, LAT, LAT), LAT ** -0.5, 0.25)
    update_gain = jnp.clip(1.0 + 0.1 * jax.random.normal(streams_of[20], (STEPS + 1, LAT), jnp.float32), 0.5, 1.5)
    return dict(grid_inputs=grid_inputs, link_features=link_features, link_partition=link_partition, link_node=link_node, mesh_start=mesh_start, edge_features=edge_features, edge_senders=edge_senders, halo_lists=halo_lists, embed_first=embed_first, embed_second=embed_second, link_embed=link_embed, link_first=link_first, link_second=link_second, update_first=update_first, update_second=update_second, edge_embed=edge_embed, process_first=process_first, process_second=process_second, process_update_first=process_update_first, process_update_second=process_update_second, update_gain=update_gain)


epsilon = 1e-05

def normalize(values):
    center = values - lax.optimization_barrier(jnp.mean(values, axis=-1, keepdims=True))
    spread = lax.optimization_barrier(jnp.mean(center * center, axis=-1, keepdims=True))
    return center * lax.rsqrt(spread + epsilon)

def product(left, right):
    return jnp.dot(left, right, preferred_element_type=jnp.float32)

def embed_links(features, table):
    linear = jnp.einsum('fe,fl->el', features, table, precision=lax.Precision.HIGHEST)
    return normalize(jax.nn.silu(linear)).astype(jnp.bfloat16)

def finish_message(summand, second):
    hidden = jax.nn.silu(summand).astype(jnp.bfloat16)
    return normalize(product(hidden, second)).astype(jnp.bfloat16)

def node_update(state, summed, first, second, gain):
    summand = product(state, first[:LAT]) + product(summed, first[LAT:])
    hidden = jax.nn.silu(summand).astype(jnp.bfloat16)
    return (state.astype(jnp.float32) + gain * normalize(product(hidden, second))).astype(jnp.bfloat16)

def reference(grid_inputs, link_features, link_partition, link_node, mesh_start, edge_features, edge_senders, halo_lists, embed_first, embed_second, link_embed, link_first, link_second, update_first, update_second, edge_embed, process_first, process_second, process_update_first, process_update_second, update_gain):
    receiver_terms = product(mesh_start, link_first[LAT:2 * LAT]).astype(jnp.bfloat16)

    def slab(total, index):
        cells = lax.dynamic_slice_in_dim(grid_inputs, index * G_DEV, G_DEV, 1)
        hidden = jax.nn.silu(lax.dot_general(cells, embed_first, (((0,), (0,)), ((), ())), preferred_element_type=jnp.float32)).astype(jnp.bfloat16)
        grid_state = normalize(product(hidden, embed_second)).astype(jnp.bfloat16)
        sender_terms = product(grid_state, link_first[:LAT]).astype(jnp.bfloat16)
        features = lax.dynamic_slice_in_dim(link_features, index * G_DEV * K, G_DEV * K, 1)
        link_state = embed_links(features, link_embed)
        edge_part = product(link_state, link_first[2 * LAT:]).reshape(G_DEV, K, LAT)
        link_terms = (edge_part + sender_terms.astype(jnp.float32)[:, None, :]).reshape(G_DEV * K, LAT).astype(jnp.bfloat16)
        parts = lax.dynamic_slice_in_dim(link_partition, index * G_DEV, G_DEV, 0).reshape(-1)
        nodes = lax.dynamic_slice_in_dim(link_node, index * G_DEV, G_DEV, 0).reshape(-1)
        target = (parts * M_DEV + nodes).astype(jnp.int32)
        message = finish_message(link_terms.astype(jnp.float32) + receiver_terms[target].astype(jnp.float32), link_second)
        return (total.at[target].add(message.astype(jnp.float32)), None)
    total, _ = lax.scan(slab, jnp.zeros((MESH, LAT), jnp.float32), jnp.arange(N_ROWS, dtype=jnp.int32))
    state = node_update(mesh_start, total.astype(jnp.bfloat16), update_first, update_second, update_gain[0])
    owner_device = (jnp.arange(MESH, dtype=jnp.int32) // M_DEV)[:, None] + jnp.zeros((1, DEG), jnp.int32)
    is_local = edge_senders < M_DEV
    offset = jnp.clip(edge_senders - M_DEV, 0, N_ROWS * HCAP - 1).astype(jnp.int32)
    owner = offset // HCAP
    place = offset % HCAP
    remote = halo_lists[owner, owner_device, place]
    source = jnp.where(is_local, owner_device * M_DEV + edge_senders, owner * M_DEV + remote).astype(jnp.int32)
    saved = []
    for step in range(STEPS):
        weights = process_first[step]
        sent = product(state, weights[:LAT]).astype(jnp.bfloat16)
        kept = product(state, weights[LAT:2 * LAT]).astype(jnp.bfloat16)
        saved.append((sent, kept))

        def block(index, saved_terms=tuple(saved), last=step):
            features = lax.dynamic_slice_in_dim(edge_features, index * M_DEV * DEG, M_DEV * DEG, 1)
            edge_state = embed_links(features, edge_embed)
            senders = lax.dynamic_slice_in_dim(source, index * M_DEV, M_DEV, 0).reshape(-1)
            message = None
            for earlier in range(last + 1):
                sender_part, receiver_part = saved_terms[earlier]
                local_receivers = lax.dynamic_slice_in_dim(receiver_part, index * M_DEV, M_DEV, 0)
                summand = sender_part[senders].astype(jnp.float32).reshape(M_DEV, DEG, LAT)
                summand = summand + local_receivers.astype(jnp.float32)[:, None, :]
                summand = summand + product(edge_state, process_first[earlier][2 * LAT:]).reshape(M_DEV, DEG, LAT)
                message = finish_message(summand.reshape(-1, LAT), process_second[earlier])
                if earlier < last:
                    edge_state = (edge_state.astype(jnp.float32) + message.astype(jnp.float32)).astype(jnp.bfloat16)
            return lax.optimization_barrier(jnp.sum(message.reshape(M_DEV, DEG, LAT).astype(jnp.float32), axis=1)).astype(jnp.bfloat16)
        summed = lax.map(block, jnp.arange(N_ROWS, dtype=jnp.int32)).reshape(MESH, LAT)
        state = node_update(state, summed, process_update_first[step], process_update_second[step], update_gain[step + 1])
    return state
```

```python
import functools

import jax
import jax.numpy as jnp
from jax import lax
from jax.experimental import pallas as pl
from jax.experimental.pallas import tpu as pltpu
from jax.sharding import PartitionSpec as P

epsilon = 1e-05
f32 = jnp.float32
bf16 = jnp.bfloat16
MIB = 2**20
EXTRA = 32


def dot(left, right, left_dim=1, right_dim=0):
    return lax.dot_general(
        left, right, (((left_dim,), (right_dim,)), ((), ())), preferred_element_type=f32
    )


def silu(values):
    half = 0.5 * values
    return half + half * jnp.tanh(half)


def normalize(values):
    scale = 1.0 / values.shape[-1]
    center = values - jnp.sum(values, axis=-1, keepdims=True) * scale
    spread = jnp.sum(center * center, axis=-1, keepdims=True) * scale
    return center * lax.rsqrt(spread + epsilon)


def iota(shape, dim):
    return lax.broadcasted_iota(jnp.int32, shape, dim)


def split3(values):
    high = values.astype(bf16).astype(f32)
    rest = values - high
    middle = rest.astype(bf16).astype(f32)
    return high, middle, rest - middle


def store_pieces(ref, values, order, base=0):
    pieces = split3(values)
    rows = values.shape[0]
    for place, piece in enumerate(order):
        ref[base + place * rows : base + (place + 1) * rows, :] = pieces[piece]


LEFT_ORDER = (0, 0, 0, 1, 1, 2)
RIGHT_ORDER = (0, 1, 2, 0, 1, 0)


def pack_kernel(devices, grid_ref, features_ref, partition_ref, node_ref, sent_ref, columns, extra):
    channels, cells = grid_ref.shape
    fanout = partition_ref.shape[1]
    links = cells * fanout
    width = sent_ref.shape[1]
    slots = sent_ref.shape[0]
    capacity = slots // devices
    cell_of = iota((cells, links), 0)
    link_of = iota((cells, links), 1)
    target = jnp.zeros((1, links), f32)
    node = jnp.zeros((1, links), f32)
    repeat = jnp.zeros((cells, links), f32)
    for k in range(fanout):
        mine = jnp.where(link_of == cell_of * fanout + k, 1.0, 0.0)
        repeat = repeat + mine
        target = target + jnp.sum(
            mine * partition_ref[:, k : k + 1].astype(f32), axis=0, keepdims=True
        )
        node = node + jnp.sum(
            mine * (node_ref[:, k : k + 1] + 1).astype(f32), axis=0, keepdims=True
        )
    target = target.astype(jnp.int32)
    node = node.astype(jnp.int32)
    matches = jnp.where(iota((devices, links), 0) == target, 1.0, 0.0)
    upper = jnp.where(iota((links, links), 0) <= iota((links, links), 1), 1.0, 0.0)
    counts = dot(matches.astype(bf16), upper.astype(bf16))
    rank = jnp.sum(counts * matches, axis=0, keepdims=True).astype(jnp.int32) - 1
    slot = target * capacity + rank
    select = jnp.where(iota((slots, links), 0) == slot, 1.0, 0.0).astype(bf16)
    extra[...] = jnp.zeros_like(extra)
    store_pieces(extra, features_ref[...], LEFT_ORDER)
    extra[24:25, :] = (node >> 4).astype(f32)
    extra[25:26, :] = (node & 15).astype(f32)
    columns[width - EXTRA - 16 : width - EXTRA, :] = jnp.zeros((16, links), bf16)
    columns[0:channels, :] = dot(grid_ref[...], repeat.astype(bf16)).astype(bf16)
    columns[width - EXTRA : width, :] = extra[...].astype(bf16)
    sent_ref[...] = dot(select, columns[...], 1, 1).astype(bf16)


def side_kernel(
    devices,
    features_ref,
    senders_ref,
    lists_ref,
    start_ref,
    table_ref,
    link_first_ref,
    update_first_ref,
    process_first_ref,
    state_ref,
    part_ref,
    local_ref,
    halo_ref,
    receiver_ref,
    base_ref,
    select_ref,
    pieces,
    turned,
    table,
):
    owned, width = start_ref.shape
    degree = senders_ref.shape[1]
    slots = lists_ref.shape[2]
    receiver_ref[...] = dot(start_ref[...], link_first_ref[width : 2 * width, :]).astype(bf16)
    base_ref[...] = dot(start_ref[...], update_first_ref[0:width, :])
    lists = lists_ref[0]
    rows = select_ref.shape[0]
    picks = jnp.where(
        iota((rows, devices), 0) // slots == iota((rows, devices), 1), 1.0, 0.0
    ).astype(bf16)
    high = dot(picks, (lists >> 4).astype(f32).astype(bf16))
    low = dot(picks, (lists & 15).astype(f32).astype(bf16))
    chosen = high * 16.0 + low
    place = iota((rows, slots), 0) % slots == iota((rows, slots), 1)
    column = jnp.sum(jnp.where(place, chosen, 0.0), axis=1, keepdims=True).astype(jnp.int32)
    select_ref[...] = jnp.where(iota((rows, owned), 1) == column, 1.0, 0.0).astype(bf16)
    pieces[...] = jnp.zeros_like(pieces)
    store_pieces(pieces, features_ref[...], LEFT_ORDER)
    turned[...] = jnp.zeros_like(turned)
    turned[:, 0:EXTRA] = jnp.transpose(pieces[...])
    table[...] = jnp.zeros_like(table)
    store_pieces(table, table_ref[...], RIGHT_ORDER)
    matrix = table[...].astype(bf16)
    weights = process_first_ref[0, 2 * width :, :]
    for j in range(degree):
        column = senders_ref[:, j : j + 1]
        local_ref[j] = jnp.where(iota((owned, owned), 1) == column, 1.0, 0.0).astype(bf16)
        halo_ref[j] = jnp.where(iota((owned, rows), 1) == column - owned, 1.0, 0.0).astype(bf16)
        left = turned[pl.ds(j, owned, stride=degree), :].astype(bf16)
        state = normalize(silu(dot(left, matrix))).astype(bf16)
        state_ref[j] = state
        part_ref[j] = dot(state, weights)


def update(state, summand, second, gain):
    hidden = silu(summand).astype(bf16)
    return (state.astype(f32) + gain * normalize(dot(hidden, second))).astype(bf16)


def link_kernel(
    terms_ref,
    receiver_ref,
    base_ref,
    start_ref,
    select_ref,
    embed_first_ref,
    embed_second_ref,
    link_embed_ref,
    link_first_ref,
    link_second_ref,
    update_first_ref,
    update_second_ref,
    gain_ref,
    process_first_ref,
    state_ref,
    sent_ref,
    out_ref,
    first,
    table,
    messages,
):
    owned, width = start_ref.shape
    slots = terms_ref.shape[0]
    channels = embed_first_ref.shape[0]
    first[...] = jnp.zeros_like(first)
    first[0:channels, :] = embed_first_ref[...]
    table[...] = jnp.zeros_like(table)
    store_pieces(table, link_embed_ref[...], RIGHT_ORDER, table.shape[0] - EXTRA)
    matrix = table[...].astype(bf16)
    tail = table.shape[0]
    chunk = 256
    lanes = iota((8, tail), 1)
    weights = jnp.where(
        lanes == tail - EXTRA + 24, 16.0, jnp.where(lanes == tail - EXTRA + 25, 1.0, 0.0)
    ).astype(bf16)
    for start in range(0, slots, chunk):
        rows = slice(start, start + chunk)
        terms = terms_ref[rows, :]
        extra = terms_ref[rows, width - tail :]
        hidden = silu(dot(terms, first[...])).astype(bf16)
        grid_state = normalize(dot(hidden, embed_second_ref[...])).astype(bf16)
        sender = dot(grid_state, link_first_ref[0:width, :]).astype(bf16).astype(f32)
        link_state = normalize(silu(dot(extra, matrix))).astype(bf16)
        link_terms = (sender + dot(link_state, link_first_ref[2 * width :, :])).astype(bf16)
        parts = extra.astype(f32)
        node = (
            parts[:, tail - EXTRA + 24 : tail - EXTRA + 25] * 16.0
            + parts[:, tail - EXTRA + 25 : tail - EXTRA + 26]
        ).astype(jnp.int32)
        pick = jnp.where(iota((chunk, owned), 1) == node - 1, 1.0, 0.0).astype(bf16)
        summand = link_terms.astype(f32) + dot(pick, receiver_ref[...])
        message = normalize(dot(silu(summand).astype(bf16), link_second_ref[...]))
        messages[rows, :] = message.astype(bf16)
    nodes = dot(weights, terms_ref[:, width - tail :], 1, 1)[0:1, :].astype(jnp.int32)
    collect = jnp.where(iota((owned, slots), 0) == nodes - 1, 1.0, 0.0).astype(bf16)
    summed = dot(collect, messages[...]).astype(bf16)
    summand = base_ref[...] + dot(summed, update_first_ref[width:, :])
    state = update(start_ref[...], summand, update_second_ref[...], gain_ref[0:1, :])
    state_ref[...] = state
    sent = dot(state, process_first_ref[0, 0:width, :]).astype(bf16)
    sent_ref[...] = sent
    out_ref[...] = dot(select_ref[...], sent).astype(bf16)


def local_kernel(step, state_ref, sent_ref, local_ref, part_ref, process_first_ref, sum_ref):
    width = state_ref.shape[1]
    kept = dot(state_ref[...], process_first_ref[step, width : 2 * width, :])
    kept = kept.astype(bf16).astype(f32)
    for j in range(local_ref.shape[0]):
        part = part_ref[j]
        if step:
            part = dot(part, process_first_ref[step, 2 * width :, :])
        sum_ref[j] = part + kept + dot(local_ref[j], sent_ref[...])


def edge_kernel(
    step,
    last,
    sum_ref,
    halo_ref,
    incoming_ref,
    edge_ref,
    state_ref,
    select_ref,
    process_first_ref,
    process_second_ref,
    first_ref,
    second_ref,
    gain_ref,
    *out_refs,
):
    width = state_ref.shape[1]
    total = jnp.zeros(state_ref.shape, f32)
    for j in range(sum_ref.shape[0]):
        summand = sum_ref[j] + dot(halo_ref[j], incoming_ref[...])
        hidden = silu(summand).astype(bf16)
        message = normalize(dot(hidden, process_second_ref[step])).astype(bf16).astype(f32)
        total = total + message
        if not last:
            out_refs[3][j] = (edge_ref[j].astype(f32) + message).astype(bf16)
    summed = total.astype(bf16)
    summand = dot(state_ref[...], first_ref[step, 0:width, :]) + dot(
        summed, first_ref[step, width:, :]
    )
    state = update(
        state_ref[...], summand, second_ref[step], gain_ref[step + 1 : step + 2, :]
    )
    out_refs[0][...] = state
    if not last:
        sent = dot(state, process_first_ref[step + 1, 0:width, :]).astype(bf16)
        out_refs[1][...] = sent
        out_refs[2][...] = dot(select_ref[...], sent).astype(bf16)


def call(kernel, name, outs, args, scratch=(), flops=10**9, limit=20):
    spec = pl.BlockSpec(memory_space=pltpu.VMEM)
    return pl.pallas_call(
        kernel,
        out_shape=[jax.ShapeDtypeStruct(*out) for out in outs],
        in_specs=[spec] * len(args),
        out_specs=[spec] * len(outs),
        scratch_shapes=list(scratch),
        compiler_params=pltpu.CompilerParams(vmem_limit_bytes=limit * MIB),
        cost_estimate=pl.CostEstimate(flops=flops, bytes_accessed=8 * MIB, transcendentals=0),
        name=name,
    )(*args)


def body(
    grid_inputs,
    link_features,
    link_partition,
    link_node,
    mesh_start,
    edge_features,
    edge_senders,
    halo_lists,
    embed_first,
    embed_second,
    link_embed,
    link_first,
    link_second,
    update_first,
    update_second,
    edge_embed,
    process_first,
    process_second,
    process_update_first,
    process_update_second,
    update_gain,
):
    owned, width = mesh_start.shape
    devices = lax.axis_size("rows")
    cells = grid_inputs.shape[1]
    links = cells * link_partition.shape[1]
    slots = 2 * links
    degree = edge_senders.shape[1]
    edges = owned * degree
    halo_slots = halo_lists.shape[2]
    halo_rows = devices * halo_slots

    def exchange(values):
        values = values.reshape(devices, -1, width)
        return lax.all_to_all(values, "rows", split_axis=0, concat_axis=0, tiled=True).reshape(
            -1, width
        )

    (packed,) = call(
        functools.partial(pack_kernel, devices),
        "pack",
        [((slots, width), bf16)],
        (grid_inputs, link_features, link_partition, link_node),
        [pltpu.VMEM((width, links), bf16), pltpu.VMEM((EXTRA, links), f32)],
    )
    terms = exchange(packed)
    edge_state, part, local, halo, receiver, base, select = call(
        functools.partial(side_kernel, devices),
        "side",
        [
            ((degree, owned, width), bf16),
            ((degree, owned, width), f32),
            ((degree, owned, owned), bf16),
            ((degree, owned, halo_rows), bf16),
            ((owned, width), bf16),
            ((owned, width), f32),
            ((halo_rows, owned), bf16),
        ],
        (
            edge_features,
            edge_senders,
            halo_lists,
            mesh_start,
            edge_embed,
            link_first,
            update_first,
            process_first,
        ),
        [
            pltpu.VMEM((EXTRA, edges), f32),
            pltpu.VMEM((edges, 128), f32),
            pltpu.VMEM((128, width), f32),
        ],
        flops=10**10,
    )
    state, sent, outgoing = call(
        link_kernel,
        "link",
        [((owned, width), bf16), ((owned, width), bf16), ((halo_rows, width), bf16)],
        (
            terms,
            receiver,
            base,
            mesh_start,
            select,
            embed_first,
            embed_second,
            link_embed,
            link_first,
            link_second,
            update_first,
            update_second,
            update_gain,
            process_first,
        ),
        [
            pltpu.VMEM((width, width), bf16),
            pltpu.VMEM((128, width), f32),
            pltpu.VMEM((slots, width), bf16),
        ],
    )
    steps = process_first.shape[0]
    for step in range(steps):
        last = step + 1 == steps
        incoming = exchange(outgoing)
        (summand,) = call(
            functools.partial(local_kernel, step),
            f"local{step}",
            [((degree, owned, width), f32)],
            (state, sent, local, part, process_first),
            flops=10**10,
        )
        outs = [((owned, width), bf16)]
        if not last:
            outs += [
                ((owned, width), bf16),
                ((halo_rows, width), bf16),
                ((degree, owned, width), bf16),
            ]
        results = call(
            functools.partial(edge_kernel, step, last),
            f"edge{step}",
            outs,
            (
                summand,
                halo,
                incoming,
                edge_state,
                state,
                select,
                process_first,
                process_second,
                process_update_first,
                process_update_second,
                update_gain,
            ),
        )
        if last:
            return results[0]
        state, sent, outgoing, edge_state = results
        part = edge_state


def solution(mesh):
    return jax.shard_map(
        body,
        mesh=mesh,
        in_specs=(
            P(None, ("groups", "rows")),
            P(None, "rows"),
            P("rows", None),
            P("rows", None),
            P("rows", None),
            P(None, "rows"),
            P("rows", None),
            P("rows", None, None),
        )
        + (P(),) * 13,
        out_specs=P(("groups", "rows"), None),
        check_vma=False,
    )
```

```python
import functools

import jax
import jax.numpy as jnp
from jax import lax
from jax.experimental import pallas as pl
from jax.experimental.pallas import tpu as pltpu
from jax.sharding import PartitionSpec as P

epsilon = 1e-05
f32 = jnp.float32
bf16 = jnp.bfloat16
MIB = 2**20
EXTRA = 32


def dot(left, right, left_dim=1, right_dim=0):
    return lax.dot_general(
        left, right, (((left_dim,), (right_dim,)), ((), ())), preferred_element_type=f32
    )


def silu(values):
    half = 0.5 * values
    return half + half * jnp.tanh(half)


def normalize(values):
    scale = 1.0 / values.shape[-1]
    center = values - jnp.sum(values, axis=-1, keepdims=True) * scale
    spread = jnp.sum(center * center, axis=-1, keepdims=True) * scale
    return center * lax.rsqrt(spread + epsilon)


def iota(shape, dim):
    return lax.broadcasted_iota(jnp.int32, shape, dim)


def split3(values):
    high = values.astype(bf16).astype(f32)
    rest = values - high
    middle = rest.astype(bf16).astype(f32)
    return high, middle, rest - middle


def store_pieces(ref, values, order, base=0):
    pieces = split3(values)
    rows = values.shape[0]
    for place, piece in enumerate(order):
        ref[base + place * rows : base + (place + 1) * rows, :] = pieces[piece]


LEFT_ORDER = (0, 0, 0, 1, 1, 2)
RIGHT_ORDER = (0, 1, 2, 0, 1, 0)


class Load:
    def __init__(self, source, target, semaphore):
        self.copy = pltpu.make_async_copy(source, target, semaphore)
        self.target = target
        self.waiting = True
        self.copy.start()

    def __call__(self):
        if self.waiting:
            self.copy.wait()
            self.waiting = False
        return self.target


def run(kernel, name, outs, args, scratch=(), flops=10**9):
    plans = []
    for arg in args:
        if not isinstance(arg, tuple):
            arg = (arg, None, 1)
        array, take, count = arg
        if take is None:
            shape = array.shape
        else:
            shape = jax.eval_shape(lambda x, take=take: take(x, 0), array).shape
        plans.append((array, take, count, shape))
    n_in, n_out = len(plans), len(outs)
    starts, total = [], 0
    for plan in plans:
        starts.append(total)
        total += plan[2]
    out_starts, out_total = [], 0
    for out in outs:
        out_starts.append(out_total)
        out_total += out[2]
    arrays, places = [], []
    for plan in plans:
        known = [i for i, array in enumerate(arrays) if array is plan[0]]
        if known:
            places.append(known[0])
        else:
            places.append(len(arrays))
            arrays.append(plan[0])

    def whole(*refs):
        ins = refs[: len(arrays)]
        out_refs = refs[len(arrays) : len(arrays) + n_out]
        rest = refs[len(arrays) + n_out :]
        in_vmem, out_vmem = rest[:n_in], rest[n_in : n_in + n_out]
        in_sems, out_sems = rest[n_in + n_out : n_in + n_out + 2]
        loads = []
        for i, (array, take, count, shape) in enumerate(plans):
            source = ins[places[i]]
            pieces = []
            for piece in range(count):
                view = source if take is None else take(source.at, piece)
                target = in_vmem[i] if count == 1 else in_vmem[i].at[piece]
                pieces.append(Load(view, target, in_sems.at[starts[i] + piece]))
            loads.append(pieces[0] if count == 1 else pieces)
        pending = []

        def store(i, value, piece=None):
            target = out_vmem[i] if piece is None else out_vmem[i].at[piece]
            out = out_refs[i] if piece is None else out_refs[i].at[piece]
            target[...] = value
            copy = pltpu.make_async_copy(target, out, out_sems.at[out_starts[i] + (piece or 0)])
            copy.start()
            pending.append(copy)

        kernel(loads, store, *rest[n_in + n_out + 2 :])
        for pieces in loads:
            for load in pieces if isinstance(pieces, list) else [pieces]:
                load()
        for copy in pending:
            copy.wait()

    spec = pl.BlockSpec(memory_space=pl.ANY)
    in_scratch = [
        pltpu.VMEM(shape if count == 1 else (count,) + shape, array.dtype)
        for array, _, count, shape in plans
    ]
    return pl.pallas_call(
        whole,
        out_shape=[jax.ShapeDtypeStruct(out[0], out[1]) for out in outs],
        in_specs=[spec] * len(arrays),
        out_specs=[spec] * n_out,
        scratch_shapes=in_scratch
        + [pltpu.VMEM(out[0], out[1]) for out in outs]
        + [pltpu.SemaphoreType.DMA((total,)), pltpu.SemaphoreType.DMA((out_total,))]
        + list(scratch),
        compiler_params=pltpu.CompilerParams(vmem_limit_bytes=60 * MIB),
        cost_estimate=pl.CostEstimate(flops=flops, bytes_accessed=8 * MIB, transcendentals=0),
        name=name,
    )(*arrays)


def rows_of(start, stop, step=None):
    if step is None:
        return lambda ref, i: ref[start:stop]
    return lambda ref, i: ref[step, start:stop]


def piece_of(ref, i):
    return ref[i]


def fixed(step):
    return lambda ref, i: ref[step]


def pack_kernel(devices, loads, store, columns, extra):
    grid, features, partition, node = loads
    channels, cells = grid.target.shape
    fanout = partition.target.shape[0]
    links = cells * fanout
    width = columns.shape[0]
    slots = 2 * links
    capacity = slots // devices
    place = iota((cells, links), 1)
    repeat = jnp.where(
        functools.reduce(
            jnp.logical_or,
            [place == iota((cells, links), 0) + k * cells for k in range(fanout)],
        ),
        1.0,
        0.0,
    ).astype(bf16)
    order = iota((links, links), 0)
    turn = iota((links, links), 1)
    upper = jnp.where(order <= turn, 1.0, 0.0).astype(bf16)
    spread = jnp.where(order == turn % cells * fanout + turn // cells, 1.0, 0.0).astype(bf16)
    extra[...] = jnp.zeros_like(extra)
    columns[width - EXTRA - 16 : width - EXTRA, :] = jnp.zeros((16, links), bf16)
    store_pieces(extra, features()[...], LEFT_ORDER)
    target = jnp.concatenate([partition()[k : k + 1, :] for k in range(fanout)], axis=1)
    nodes = jnp.concatenate([node()[k : k + 1, :] for k in range(fanout)], axis=1) + 1
    extra[...] = dot(extra[...].astype(bf16), spread)
    extra[24:25, :] = (nodes >> 4).astype(f32)
    extra[25:26, :] = (nodes & 15).astype(f32)
    matches = jnp.where(iota((devices, links), 0) == target, 1.0, 0.0)
    counts = dot(matches.astype(bf16), upper)
    rank = jnp.sum(counts * matches, axis=0, keepdims=True).astype(jnp.int32) - 1
    slot = target * capacity + rank
    select = jnp.where(iota((slots, links), 0) == slot, 1.0, 0.0).astype(bf16)
    columns[0:channels, :] = dot(grid()[...], repeat).astype(bf16)
    columns[width - EXTRA : width, :] = extra[...].astype(bf16)
    store(0, dot(select, columns[...], 1, 1).astype(bf16))


def side_kernel(far, loads, store, pieces, turned, table):
    features, embed, start, link_receiver, update_start, lists = loads
    owned, width = start.target.shape
    edges = features.target.shape[1]
    degree = edges // owned
    devices, slots = lists.target.shape[1:]
    pieces[...] = jnp.zeros_like(pieces)
    turned[...] = jnp.zeros_like(turned)
    table[...] = jnp.zeros_like(table)
    store_pieces(pieces, features()[...], LEFT_ORDER)
    turned[:, 0:EXTRA] = jnp.transpose(pieces[...])
    store_pieces(table, embed()[...], RIGHT_ORDER)
    matrix = table[...].astype(bf16)
    for j in range(degree):
        left = turned[pl.ds(j, owned, stride=degree), :].astype(bf16)
        store(0, normalize(silu(dot(left, matrix))).astype(bf16), j)
    store(1, dot(start()[...], link_receiver()[...]).astype(bf16))
    store(2, dot(start()[...], update_start()[...]))
    lists = lists()[0]
    me = lax.axis_index("rows")
    rows = devices * far + 2 * slots
    row = iota((rows, 1), 0)
    near = row - devices * far
    after = (me + 1) % devices
    before = (me + devices - 1) % devices
    reader = jnp.where(near < 0, row // far, jnp.where(near < slots, after, before))
    place = jnp.where(near < 0, row % far, near % slots)
    picks = jnp.where(iota((rows, devices), 1) == reader, 1.0, 0.0).astype(bf16)
    high = dot(picks, (lists >> 4).astype(f32).astype(bf16))
    low = dot(picks, (lists & 15).astype(f32).astype(bf16))
    chosen = jnp.where(iota((rows, slots), 1) == place, high * 16.0 + low, 0.0)
    column = jnp.sum(chosen, axis=1, keepdims=True).astype(jnp.int32)
    store(3, jnp.where(iota((rows, owned), 1) == column, 1.0, 0.0).astype(bf16))


def update(state, summand, second, gain):
    hidden = silu(summand).astype(bf16)
    return (state.astype(f32) + gain * normalize(dot(hidden, second))).astype(bf16)


def send(store, base, state, sender, select, devices, far, slots):
    sent = dot(state, sender).astype(bf16)
    outgoing = dot(select, sent).astype(bf16)
    count = devices * far
    store(base + 1, outgoing[0:count])
    store(base + 2, outgoing[count : count + slots])
    store(base + 3, outgoing[count + slots : count + 2 * slots])
    store(base, sent)


def link_kernel(sizes, loads, store, first, table, messages):
    (
        terms,
        embed_first,
        embed_second,
        link_embed,
        link_sender,
        link_edge,
        receiver,
        link_second,
        base,
        update_first,
        update_second,
        gain,
        start,
        sender_first,
        select,
    ) = loads
    owned, width = start.target.shape
    slots = terms.target.shape[0]
    channels = embed_first.target.shape[0]
    tail = table.shape[0]
    first[...] = jnp.zeros_like(first)
    table[...] = jnp.zeros_like(table)
    lanes = iota((8, tail), 1)
    weights = jnp.where(
        lanes == tail - EXTRA + 24, 16.0, jnp.where(lanes == tail - EXTRA + 25, 1.0, 0.0)
    ).astype(bf16)
    chunk = 256
    first[0:channels, :] = embed_first()[...]
    store_pieces(table, link_embed()[...], RIGHT_ORDER, tail - EXTRA)
    matrix = table[...].astype(bf16)
    terms = terms()
    for begin in range(0, slots, chunk):
        rows = slice(begin, begin + chunk)
        extra = terms[rows, width - tail :]
        hidden = silu(dot(terms[rows, :], first[...])).astype(bf16)
        grid_state = normalize(dot(hidden, embed_second()[...])).astype(bf16)
        sender = dot(grid_state, link_sender()[...]).astype(bf16).astype(f32)
        link_state = normalize(silu(dot(extra, matrix))).astype(bf16)
        link_terms = (sender + dot(link_state, link_edge()[...])).astype(bf16)
        parts = extra.astype(f32)
        node = (
            parts[:, tail - EXTRA + 24 : tail - EXTRA + 25] * 16.0
            + parts[:, tail - EXTRA + 25 : tail - EXTRA + 26]
        ).astype(jnp.int32)
        pick = jnp.where(iota((chunk, owned), 1) == node - 1, 1.0, 0.0).astype(bf16)
        summand = link_terms.astype(f32) + dot(pick, receiver()[...])
        message = normalize(dot(silu(summand).astype(bf16), link_second()[...]))
        messages[rows, :] = message.astype(bf16)
    nodes = dot(weights, terms[:, width - tail :], 1, 1)[0:1, :].astype(jnp.int32)
    collect = jnp.where(iota((owned, slots), 0) == nodes - 1, 1.0, 0.0).astype(bf16)
    summed = dot(collect, messages[...]).astype(bf16)
    summand = base()[...] + dot(summed, update_first()[...])
    state = update(start()[...], summand, update_second()[...], gain()[0:1, :])
    store(0, state)
    send(store, 1, state, sender_first()[...], select()[...], *sizes)


def local_kernel(loads, store):
    senders, state, receiver_first, sent, edge_first, edges = loads
    degree, owned = senders.target.shape
    columns = jnp.transpose(senders()[...].astype(f32)).astype(jnp.int32)
    kept = dot(state()[...], receiver_first()[...]).astype(bf16).astype(f32)
    for j in range(degree):
        local = jnp.where(iota((owned, owned), 1) == columns[:, j : j + 1], 1.0, 0.0)
        part = dot(local.astype(bf16), sent()[...]) + dot(edges[j]()[...], edge_first()[...])
        store(0, part + kept, j)


def edge_kernel(step, last, sizes, loads, store, table):
    (senders, far_rows, from_before, from_after, second, sums) = loads[:6]
    (state, state_first, summed_first, update_second, gain) = loads[6:11]
    if not last:
        edges, sender_first, select = loads[11:]
    devices, far, slots = sizes
    degree, owned = senders.target.shape
    count = devices * far
    rows = table.shape[0]
    me = lax.axis_index("rows")
    after = (me + 1) % devices
    before = (me + devices - 1) % devices
    senders = senders()[...]
    halo = senders - owned
    owner = halo // slots
    place = halo % slots
    index = jnp.where(
        owner == before,
        count + place,
        jnp.where(owner == after, count + slots + place, owner * far + place),
    )
    index = jnp.where(halo < 0, -1, index)
    columns = jnp.transpose(index.astype(f32)).astype(jnp.int32)
    table[count + 2 * slots :, :] = jnp.zeros((rows - count - 2 * slots, table.shape[1]), bf16)
    table[0:count, :] = far_rows()[...]
    table[count : count + slots, :] = from_before()[...]
    table[count + slots : count + 2 * slots, :] = from_after()[...]
    total = jnp.zeros(state.target.shape, f32)
    for j in range(degree):
        pick = jnp.where(iota((owned, rows), 1) == columns[:, j : j + 1], 1.0, 0.0)
        summand = sums[j]()[...] + dot(pick.astype(bf16), table[...])
        hidden = silu(summand).astype(bf16)
        message = normalize(dot(hidden, second()[...])).astype(bf16).astype(f32)
        total = total + message
        if not last:
            store(5, (edges[j]()[...].astype(f32) + message).astype(bf16), j)
    summand = dot(state()[...], state_first()[...]) + dot(
        total.astype(bf16), summed_first()[...]
    )
    state = update(
        state()[...], summand, update_second()[...], gain()[step + 1 : step + 2, :]
    )
    store(0, state)
    if not last:
        send(store, 1, state, sender_first()[...], select()[...], *sizes)


def body(
    grid_inputs,
    link_features,
    link_partition,
    link_node,
    mesh_start,
    edge_features,
    edge_senders,
    halo_lists,
    embed_first,
    embed_second,
    link_embed,
    link_first,
    link_second,
    update_first,
    update_second,
    edge_embed,
    process_first,
    process_second,
    process_update_first,
    process_update_second,
    update_gain,
):
    owned, width = mesh_start.shape
    devices = lax.axis_size("rows")
    cells = grid_inputs.shape[1]
    links = cells * link_partition.shape[1]
    slots = 2 * links
    degree = edge_senders.shape[1]
    edges = owned * degree
    halo_slots = halo_lists.shape[2]
    far = 8
    sizes = (devices, far, halo_slots)
    halo_rows = devices * far + 2 * halo_slots
    senders = edge_senders.T

    def exchange(values):
        values = values.reshape(devices, -1, width)
        return lax.all_to_all(values, "rows", split_axis=0, concat_axis=0, tiled=True).reshape(
            -1, width
        )

    def halo(outgoing):
        up = [(i, (i + 1) % devices) for i in range(devices)]
        down = [(i, (i + devices - 1) % devices) for i in range(devices)]
        from_before = lax.ppermute(outgoing[1], "rows", up)
        from_after = lax.ppermute(outgoing[2], "rows", down)
        return exchange(outgoing[0]), from_before, from_after

    sending = [
        ((owned, width), bf16, 1),
        ((devices * far, width), bf16, 1),
        ((halo_slots, width), bf16, 1),
        ((halo_slots, width), bf16, 1),
    ]
    (packed,) = run(
        functools.partial(pack_kernel, devices),
        "pack",
        [((slots, width), bf16, 1)],
        (grid_inputs, link_features, link_partition.T, link_node.T),
        [pltpu.VMEM((width, links), bf16), pltpu.VMEM((EXTRA, links), f32)],
    )
    terms = exchange(packed)
    edge_state, receiver, base, select = run(
        functools.partial(side_kernel, far),
        "side",
        [
            ((degree, owned, width), bf16, degree),
            ((owned, width), bf16, 1),
            ((owned, width), f32, 1),
            ((halo_rows, owned), bf16, 1),
        ],
        (
            edge_features,
            edge_embed,
            mesh_start,
            (link_first, rows_of(width, 2 * width), 1),
            (update_first, rows_of(0, width), 1),
            halo_lists,
        ),
        [
            pltpu.VMEM((EXTRA, edges), f32),
            pltpu.VMEM((edges, 128), f32),
            pltpu.VMEM((128, width), f32),
        ],
        flops=10**10,
    )
    state, sent, *outgoing = run(
        functools.partial(link_kernel, sizes),
        "link",
        [((owned, width), bf16, 1)] + sending,
        (
            terms,
            embed_first,
            embed_second,
            link_embed,
            (link_first, rows_of(0, width), 1),
            (link_first, rows_of(2 * width, 3 * width), 1),
            receiver,
            link_second,
            base,
            (update_first, rows_of(width, 2 * width), 1),
            update_second,
            update_gain,
            mesh_start,
            (process_first, rows_of(0, width, 0), 1),
            select,
        ),
        [
            pltpu.VMEM((width, width), bf16),
            pltpu.VMEM((128, width), f32),
            pltpu.VMEM((slots, width), bf16),
        ],
    )
    steps = process_first.shape[0]
    for step in range(steps):
        last = step + 1 == steps
        incoming = halo(outgoing)
        (sums,) = run(
            local_kernel,
            f"local{step}",
            [((degree, owned, width), f32, degree)],
            (
                senders,
                state,
                (process_first, rows_of(width, 2 * width, step), 1),
                sent,
                (process_first, rows_of(2 * width, 3 * width, step), 1),
                (edge_state, piece_of, degree),
            ),
            flops=10**10,
        )
        outs = [((owned, width), bf16, 1)]
        extra = []
        if not last:
            outs += sending + [((degree, owned, width), bf16, degree)]
            extra = [
                (edge_state, piece_of, degree),
                (process_first, rows_of(0, width, step + 1), 1),
                select,
            ]
        results = run(
            functools.partial(edge_kernel, step, last, sizes),
            f"edge{step}",
            outs,
            [
                senders,
                *incoming,
                (process_second, fixed(step), 1),
                (sums, piece_of, degree),
                state,
                (process_update_first, rows_of(0, width, step), 1),
                (process_update_first, rows_of(width, 2 * width, step), 1),
                (process_update_second, fixed(step), 1),
                update_gain,
            ]
            + extra,
            [pltpu.VMEM((-(-halo_rows // 128) * 128, width), bf16)],
        )
        if last:
            return results[0]
        state, sent, *outgoing, edge_state = results


def solution(mesh):
    return jax.shard_map(
        body,
        mesh=mesh,
        in_specs=(
            P(None, ("groups", "rows")),
            P(None, "rows"),
            P("rows", None),
            P("rows", None),
            P("rows", None),
            P(None, "rows"),
            P("rows", None),
            P("rows", None, None),
        )
        + (P(),) * 13,
        out_specs=P(("groups", "rows"), None),
        check_vma=False,
    )
```

```python
import functools

import jax
import jax.numpy as jnp
from jax import lax
from jax.experimental import pallas as pl
from jax.experimental.pallas import tpu as pltpu
from jax.sharding import PartitionSpec as P

epsilon = 1e-05
f32 = jnp.float32
bf16 = jnp.bfloat16
MIB = 2**20
EXTRA = 32


def dot(left, right, left_dim=1, right_dim=0):
    return lax.dot_general(
        left, right, (((left_dim,), (right_dim,)), ((), ())), preferred_element_type=f32
    )


def silu(values):
    half = 0.5 * values
    return half + half * jnp.tanh(half)


def normalize(values):
    scale = 1.0 / values.shape[-1]
    center = values - jnp.sum(values, axis=-1, keepdims=True) * scale
    spread = jnp.sum(center * center, axis=-1, keepdims=True) * scale
    return center * lax.rsqrt(spread + epsilon)


def iota(shape, dim):
    return lax.broadcasted_iota(jnp.int32, shape, dim)


def split3(values):
    high = values.astype(bf16).astype(f32)
    rest = values - high
    middle = rest.astype(bf16).astype(f32)
    return high, middle, rest - middle


def store_pieces(ref, values, order, base=0):
    pieces = split3(values)
    rows = values.shape[0]
    for place, piece in enumerate(order):
        ref[base + place * rows : base + (place + 1) * rows, :] = pieces[piece]


LEFT_ORDER = (0, 0, 0, 1, 1, 2)
RIGHT_ORDER = (0, 1, 2, 0, 1, 0)


class Load:
    def __init__(self, source, target, semaphore):
        self.copy = pltpu.make_async_copy(source, target, semaphore)
        self.target = target
        self.waiting = True
        self.copy.start()

    def __call__(self):
        if self.waiting:
            self.copy.wait()
            self.waiting = False
        return self.target


def run(kernel, name, outs, args, scratch=(), flops=10**9):
    plans = []
    for arg in args:
        if not isinstance(arg, tuple):
            arg = (arg, None, 1)
        array, take, count = arg
        if take is None:
            shape = array.shape
        else:
            shape = jax.eval_shape(lambda x, take=take: take(x, 0), array).shape
        plans.append((array, take, count, shape))
    n_in, n_out = len(plans), len(outs)
    starts, total = [], 0
    for plan in plans:
        starts.append(total)
        total += plan[2]
    out_starts, out_total = [], 0
    for out in outs:
        out_starts.append(out_total)
        out_total += out[2]
    start_order = [(i, 0) for i in range(n_in) if plans[i][2] == 1]
    split = [i for i in range(n_in) if plans[i][2] > 1]
    if split:
        at = len([i for i in range(split[0]) if plans[i][2] == 1])
        pieces = [(i, piece) for piece in range(plans[split[0]][2]) for i in split]
        start_order[at:at] = pieces
    arrays, places = [], []
    for plan in plans:
        known = [i for i, array in enumerate(arrays) if array is plan[0]]
        if known:
            places.append(known[0])
        else:
            places.append(len(arrays))
            arrays.append(plan[0])

    def whole(*refs):
        ins = refs[: len(arrays)]
        out_refs = refs[len(arrays) : len(arrays) + n_out]
        rest = refs[len(arrays) + n_out :]
        in_vmem, out_vmem = rest[:n_in], rest[n_in : n_in + n_out]
        in_sems, out_sems = rest[n_in + n_out : n_in + n_out + 2]
        loads = [[None] * count for _, _, count, _ in plans]
        for i, piece in start_order:
            _, take, count, _ = plans[i]
            source = ins[places[i]]
            view = source if take is None else take(source.at, piece)
            target = in_vmem[i] if count == 1 else in_vmem[i].at[piece]
            loads[i][piece] = Load(view, target, in_sems.at[starts[i] + piece])
        loads = [pieces if len(pieces) > 1 else pieces[0] for pieces in loads]
        pending = []

        def store(i, value, piece=None):
            target = out_vmem[i] if piece is None else out_vmem[i].at[piece]
            out = out_refs[i] if piece is None else out_refs[i].at[piece]
            target[...] = value
            copy = pltpu.make_async_copy(target, out, out_sems.at[out_starts[i] + (piece or 0)])
            copy.start()
            pending.append(copy)

        kernel(loads, store, *rest[n_in + n_out + 2 :])
        for pieces in loads:
            for load in pieces if isinstance(pieces, list) else [pieces]:
                load()
        for copy in pending:
            copy.wait()

    spec = pl.BlockSpec(memory_space=pltpu.HBM)
    in_scratch = [
        pltpu.VMEM(shape if count == 1 else (count,) + shape, array.dtype)
        for array, _, count, shape in plans
    ]
    return pl.pallas_call(
        whole,
        out_shape=[jax.ShapeDtypeStruct(out[0], out[1]) for out in outs],
        in_specs=[spec] * len(arrays),
        out_specs=[spec] * n_out,
        scratch_shapes=in_scratch
        + [pltpu.VMEM(out[0], out[1]) for out in outs]
        + [pltpu.SemaphoreType.DMA((total,)), pltpu.SemaphoreType.DMA((out_total,))]
        + list(scratch),
        compiler_params=pltpu.CompilerParams(vmem_limit_bytes=60 * MIB),
        cost_estimate=pl.CostEstimate(flops=flops, bytes_accessed=8 * MIB, transcendentals=0),
        name=name,
    )(*arrays)


def rows_of(start, stop, step=None):
    if step is None:
        return lambda ref, i: ref[start:stop]
    return lambda ref, i: ref[step, start:stop]


def piece_of(ref, i):
    return ref[i]


def fixed(step):
    return lambda ref, i: ref[step]


def pack_kernel(devices, loads, store, columns, extra):
    grid, features, partition, node = loads
    channels, cells = grid.target.shape
    fanout = partition.target.shape[0]
    links = cells * fanout
    width = columns.shape[0]
    slots = 2 * links
    capacity = slots // devices
    place = iota((cells, links), 1)
    repeat = jnp.where(
        functools.reduce(
            jnp.logical_or,
            [place == iota((cells, links), 0) + k * cells for k in range(fanout)],
        ),
        1.0,
        0.0,
    ).astype(bf16)
    order = iota((links, links), 0)
    turn = iota((links, links), 1)
    upper = jnp.where(order <= turn, 1.0, 0.0).astype(bf16)
    spread = jnp.where(order == turn % cells * fanout + turn // cells, 1.0, 0.0).astype(bf16)
    extra[...] = jnp.zeros_like(extra)
    columns[width - EXTRA - 16 : width - EXTRA, :] = jnp.zeros((16, links), bf16)
    store_pieces(extra, features()[...], LEFT_ORDER)
    target = jnp.concatenate([partition()[k : k + 1, :] for k in range(fanout)], axis=1)
    nodes = jnp.concatenate([node()[k : k + 1, :] for k in range(fanout)], axis=1) + 1
    extra[...] = dot(extra[...].astype(bf16), spread)
    extra[24:25, :] = (nodes >> 4).astype(f32)
    extra[25:26, :] = (nodes & 15).astype(f32)
    matches = jnp.where(iota((devices, links), 0) == target, 1.0, 0.0)
    counts = dot(matches.astype(bf16), upper)
    rank = jnp.sum(counts * matches, axis=0, keepdims=True).astype(jnp.int32) - 1
    slot = target * capacity + rank
    select = jnp.where(iota((slots, links), 0) == slot, 1.0, 0.0).astype(bf16)
    columns[0:channels, :] = dot(grid()[...], repeat).astype(bf16)
    columns[width - EXTRA : width, :] = extra[...].astype(bf16)
    store(0, dot(select, columns[...], 1, 1).astype(bf16))


def side_kernel(loads, store, pieces, turned, table):
    features, embed, edge_first, start, link_receiver, update_start, lists = loads
    owned, width = start.target.shape
    edges = features.target.shape[1]
    degree = edges // owned
    devices, slots = lists.target.shape[1:]
    pieces[...] = jnp.zeros_like(pieces)
    turned[...] = jnp.zeros_like(turned)
    table[...] = jnp.zeros_like(table)
    store_pieces(pieces, features()[...], LEFT_ORDER)
    turned[:, 0:EXTRA] = jnp.transpose(pieces[...])
    store_pieces(table, embed()[...], RIGHT_ORDER)
    matrix = table[...].astype(bf16)
    for j in range(degree):
        left = turned[pl.ds(j, owned, stride=degree), :].astype(bf16)
        edge_state = normalize(silu(dot(left, matrix))).astype(bf16)
        store(0, edge_state, j)
        store(1, dot(edge_state, edge_first()[...]).astype(bf16), j)
    store(2, dot(start()[...], link_receiver()[...]).astype(bf16))
    store(3, dot(start()[...], update_start()[...]))
    lists = lists()[0]
    rows = devices * slots
    row = iota((rows, 1), 0)
    picks = jnp.where(iota((rows, devices), 1) == row // slots, 1.0, 0.0).astype(bf16)
    high = dot(picks, (lists >> 4).astype(f32).astype(bf16))
    low = dot(picks, (lists & 15).astype(f32).astype(bf16))
    chosen = jnp.where(iota((rows, slots), 1) == row % slots, high * 16.0 + low, 0.0)
    column = jnp.sum(chosen, axis=1, keepdims=True).astype(jnp.int32)
    store(4, jnp.where(iota((rows, owned), 1) == column, 1.0, 0.0).astype(bf16))


def update(state, summand, second, gain):
    hidden = silu(summand).astype(bf16)
    return (state.astype(f32) + gain * normalize(dot(hidden, second))).astype(bf16)


def send(store, base, state, sender, select):
    sent = dot(state, sender).astype(bf16)
    store(base, dot(select, sent).astype(bf16))
    store(base + 1, sent)


def link_kernel(loads, store, first, table, messages):
    (
        terms,
        embed_first,
        embed_second,
        link_embed,
        link_sender,
        link_edge,
        receiver,
        link_second,
        base,
        update_first,
        update_second,
        gain,
        start,
        sender_first,
        select,
    ) = loads
    owned, width = start.target.shape
    slots = terms.target.shape[0]
    channels = embed_first.target.shape[0]
    tail = table.shape[0]
    first[...] = jnp.zeros_like(first)
    table[...] = jnp.zeros_like(table)
    lanes = iota((8, tail), 1)
    weights = jnp.where(
        lanes == tail - EXTRA + 24, 16.0, jnp.where(lanes == tail - EXTRA + 25, 1.0, 0.0)
    ).astype(bf16)
    chunk = 256
    first[0:channels, :] = embed_first()[...]
    store_pieces(table, link_embed()[...], RIGHT_ORDER, tail - EXTRA)
    matrix = table[...].astype(bf16)
    terms = terms()
    for begin in range(0, slots, chunk):
        rows = slice(begin, begin + chunk)
        extra = terms[rows, width - tail :]
        hidden = silu(dot(terms[rows, :], first[...])).astype(bf16)
        grid_state = normalize(dot(hidden, embed_second()[...])).astype(bf16)
        sender = dot(grid_state, link_sender()[...]).astype(bf16).astype(f32)
        link_state = normalize(silu(dot(extra, matrix))).astype(bf16)
        link_terms = (sender + dot(link_state, link_edge()[...])).astype(bf16)
        parts = extra.astype(f32)
        node = (
            parts[:, tail - EXTRA + 24 : tail - EXTRA + 25] * 16.0
            + parts[:, tail - EXTRA + 25 : tail - EXTRA + 26]
        ).astype(jnp.int32)
        pick = jnp.where(iota((chunk, owned), 1) == node - 1, 1.0, 0.0).astype(bf16)
        summand = link_terms.astype(f32) + dot(pick, receiver()[...])
        message = normalize(dot(silu(summand).astype(bf16), link_second()[...]))
        messages[rows, :] = message.astype(bf16)
    nodes = dot(weights, terms[:, width - tail :], 1, 1)[0:1, :].astype(jnp.int32)
    collect = jnp.where(iota((owned, slots), 0) == nodes - 1, 1.0, 0.0).astype(bf16)
    summed = dot(collect, messages[...]).astype(bf16)
    summand = base()[...] + dot(summed, update_first()[...])
    state = update(start()[...], summand, update_second()[...], gain()[0:1, :])
    store(0, state)
    send(store, 1, state, sender_first()[...], select()[...])


def local_kernel(step, loads, store):
    senders, state, receiver_first, sent = loads[:4]
    parts = loads[-1]
    degree, owned = senders.target.shape
    columns = jnp.transpose(senders()[...].astype(f32)).astype(jnp.int32)
    kept = dot(state()[...], receiver_first()[...]).astype(bf16).astype(f32)
    for j in range(degree):
        local = jnp.where(iota((owned, owned), 1) == columns[:, j : j + 1], 1.0, 0.0)
        part = parts[j]()[...]
        if step:
            part = dot(part, loads[4]()[...])
        part = dot(local.astype(bf16), sent()[...]) + part.astype(f32)
        store(0, (part + kept).astype(bf16), j)


def edge_kernel(step, last, loads, store):
    senders, incoming, second, sums = loads[:4]
    (state, state_first, summed_first, update_second, gain) = loads[4:9]
    if not last:
        edges, sender_first, select = loads[9:]
    degree, owned = senders.target.shape
    rows = incoming.target.shape[0]
    columns = jnp.transpose((senders()[...] - owned).astype(f32)).astype(jnp.int32)
    total = jnp.zeros(state.target.shape, f32)
    for j in range(degree):
        pick = jnp.where(iota((owned, rows), 1) == columns[:, j : j + 1], 1.0, 0.0)
        summand = sums[j]()[...].astype(f32) + dot(pick.astype(bf16), incoming()[...])
        hidden = silu(summand).astype(bf16)
        message = normalize(dot(hidden, second()[...])).astype(bf16).astype(f32)
        total = total + message
        if not last:
            store(3, (edges[j]()[...].astype(f32) + message).astype(bf16), j)
    summand = dot(state()[...], state_first()[...]) + dot(
        total.astype(bf16), summed_first()[...]
    )
    state = update(
        state()[...], summand, update_second()[...], gain()[step + 1 : step + 2, :]
    )
    store(0, state)
    if not last:
        send(store, 1, state, sender_first()[...], select()[...])


def body(
    grid_inputs,
    link_features,
    link_partition,
    link_node,
    mesh_start,
    edge_features,
    edge_senders,
    halo_lists,
    embed_first,
    embed_second,
    link_embed,
    link_first,
    link_second,
    update_first,
    update_second,
    edge_embed,
    process_first,
    process_second,
    process_update_first,
    process_update_second,
    update_gain,
):
    owned, width = mesh_start.shape
    devices = lax.axis_size("rows")
    cells = grid_inputs.shape[1]
    links = cells * link_partition.shape[1]
    slots = 2 * links
    degree = edge_senders.shape[1]
    edges = owned * degree
    halo_slots = halo_lists.shape[2]
    halo_rows = devices * halo_slots
    senders = edge_senders.T

    def exchange(values):
        values = values.reshape(devices, -1, width)
        return lax.all_to_all(values, "rows", split_axis=0, concat_axis=0, tiled=True).reshape(
            -1, width
        )

    sending = [((halo_rows, width), bf16, 1), ((owned, width), bf16, 1)]
    (packed,) = run(
        functools.partial(pack_kernel, devices),
        "pack",
        [((slots, width), bf16, 1)],
        (grid_inputs, link_features, link_partition.T, link_node.T),
        [pltpu.VMEM((width, links), bf16), pltpu.VMEM((EXTRA, links), f32)],
    )
    terms = exchange(packed)
    edge_state, parts, receiver, base, select = run(
        side_kernel,
        "side",
        [
            ((degree, owned, width), bf16, degree),
            ((degree, owned, width), bf16, degree),
            ((owned, width), bf16, 1),
            ((owned, width), f32, 1),
            ((halo_rows, owned), bf16, 1),
        ],
        (
            edge_features,
            edge_embed,
            (process_first, rows_of(2 * width, 3 * width, 0), 1),
            mesh_start,
            (link_first, rows_of(width, 2 * width), 1),
            (update_first, rows_of(0, width), 1),
            halo_lists,
        ),
        [
            pltpu.VMEM((EXTRA, edges), f32),
            pltpu.VMEM((edges, 128), f32),
            pltpu.VMEM((128, width), f32),
        ],
        flops=10**10,
    )
    state, outgoing, sent = run(
        link_kernel,
        "link",
        [((owned, width), bf16, 1)] + sending,
        (
            terms,
            embed_first,
            embed_second,
            link_embed,
            (link_first, rows_of(0, width), 1),
            (link_first, rows_of(2 * width, 3 * width), 1),
            receiver,
            link_second,
            base,
            (update_first, rows_of(width, 2 * width), 1),
            update_second,
            update_gain,
            mesh_start,
            (process_first, rows_of(0, width, 0), 1),
            select,
        ),
        [
            pltpu.VMEM((width, width), bf16),
            pltpu.VMEM((128, width), f32),
            pltpu.VMEM((slots, width), bf16),
        ],
    )
    steps = process_first.shape[0]
    for step in range(steps):
        last = step + 1 == steps
        incoming = exchange(outgoing)
        extra = [] if step == 0 else [(process_first, rows_of(2 * width, 3 * width, step), 1)]
        (sums,) = run(
            functools.partial(local_kernel, step),
            f"local{step}",
            [((degree, owned, width), bf16, degree)],
            [
                senders,
                state,
                (process_first, rows_of(width, 2 * width, step), 1),
                sent,
            ]
            + extra
            + [(parts, piece_of, degree)],
            flops=10**10,
        )
        outs = [((owned, width), bf16, 1)]
        extra = []
        if not last:
            outs += sending + [((degree, owned, width), bf16, degree)]
            extra = [
                (edge_state, piece_of, degree),
                (process_first, rows_of(0, width, step + 1), 1),
                select,
            ]
        results = run(
            functools.partial(edge_kernel, step, last),
            f"edge{step}",
            outs,
            [
                senders,
                incoming,
                (process_second, fixed(step), 1),
                (sums, piece_of, degree),
                state,
                (process_update_first, rows_of(0, width, step), 1),
                (process_update_first, rows_of(width, 2 * width, step), 1),
                (process_update_second, fixed(step), 1),
                update_gain,
            ]
            + extra,
        )
        if last:
            return results[0]
        state, outgoing, sent, edge_state = results
        parts = edge_state


def solution(mesh):
    return jax.shard_map(
        body,
        mesh=mesh,
        in_specs=(
            P(None, ("groups", "rows")),
            P(None, "rows"),
            P("rows", None),
            P("rows", None),
            P("rows", None),
            P(None, "rows"),
            P("rows", None),
            P("rows", None, None),
        )
        + (P(),) * 13,
        out_specs=P(("groups", "rows"), None),
        check_vma=False,
    )
```

```python
import functools

import jax
import jax.numpy as jnp
from jax import lax
from jax.experimental import pallas as pl
from jax.experimental.pallas import tpu as pltpu
from jax.sharding import PartitionSpec as P

epsilon = 1e-05
f32 = jnp.float32
bf16 = jnp.bfloat16
MIB = 2**20
EXTRA = 32
CHUNK = 32


def dot(left, right, left_dim=1, right_dim=0):
    return lax.dot_general(
        left, right, (((left_dim,), (right_dim,)), ((), ())), preferred_element_type=f32
    )


def silu(values):
    half = 0.5 * values
    return half + half * jnp.tanh(half)


def normalize(values):
    scale = 1.0 / values.shape[-1]
    center = values - jnp.sum(values, axis=-1, keepdims=True) * scale
    spread = jnp.sum(center * center, axis=-1, keepdims=True) * scale
    return center * lax.rsqrt(spread + epsilon)


def iota(shape, dim):
    return lax.broadcasted_iota(jnp.int32, shape, dim)


def split3(values):
    high = values.astype(bf16).astype(f32)
    rest = values - high
    middle = rest.astype(bf16).astype(f32)
    return high, middle, rest - middle


def store_pieces(ref, values, order, base=0):
    pieces = split3(values)
    rows = values.shape[0]
    for place, piece in enumerate(order):
        ref[base + place * rows : base + (place + 1) * rows, :] = pieces[piece]


LEFT_ORDER = (0, 0, 0, 1, 1, 2)
RIGHT_ORDER = (0, 1, 2, 0, 1, 0)


class Load:
    def __init__(self, source, target, semaphore):
        self.copy = pltpu.make_async_copy(source, target, semaphore)
        self.target = target
        self.waiting = True
        self.copy.start()

    def __call__(self):
        if self.waiting:
            self.copy.wait()
            self.waiting = False
        return self.target


def run(kernel, name, outs, args, scratch=(), flops=10**9):
    plans = []
    for arg in args:
        if not isinstance(arg, tuple):
            arg = (arg, None, 1)
        array, take, count = arg
        if take is None:
            shape = array.shape
        else:
            shape = jax.eval_shape(lambda x, take=take: take(x, 0), array).shape
        plans.append((array, take, count, shape))
    n_in, n_out = len(plans), len(outs)
    starts, total = [], 0
    for plan in plans:
        starts.append(total)
        total += plan[2]
    out_starts, out_total = [], 0
    for out in outs:
        out_starts.append(out_total)
        out_total += out[2]
    start_order = [(i, 0) for i in range(n_in) if plans[i][2] == 1]
    split = [i for i in range(n_in) if plans[i][2] > 1]
    if split:
        at = len([i for i in range(split[0]) if plans[i][2] == 1])
        pieces = [(i, piece) for piece in range(plans[split[0]][2]) for i in split]
        start_order[at:at] = pieces
    arrays, places = [], []
    for plan in plans:
        known = [i for i, array in enumerate(arrays) if array is plan[0]]
        if known:
            places.append(known[0])
        else:
            places.append(len(arrays))
            arrays.append(plan[0])

    def whole(*refs):
        ins = refs[: len(arrays)]
        out_refs = refs[len(arrays) : len(arrays) + n_out]
        rest = refs[len(arrays) + n_out :]
        in_vmem, out_vmem = rest[:n_in], rest[n_in : n_in + n_out]
        in_sems, out_sems = rest[n_in + n_out : n_in + n_out + 2]
        loads = [[None] * count for _, _, count, _ in plans]
        for i, piece in start_order:
            _, take, count, _ = plans[i]
            source = ins[places[i]]
            view = source if take is None else take(source.at, piece)
            target = in_vmem[i] if count == 1 else in_vmem[i].at[piece]
            loads[i][piece] = Load(view, target, in_sems.at[starts[i] + piece])
        loads = [pieces if len(pieces) > 1 else pieces[0] for pieces in loads]
        pending = []

        def store(i, value, piece=None):
            target = out_vmem[i] if piece is None else out_vmem[i].at[piece]
            out = out_refs[i] if piece is None else out_refs[i].at[piece]
            if callable(value):
                value(target)
            else:
                target[...] = value
            copy = pltpu.make_async_copy(target, out, out_sems.at[out_starts[i] + (piece or 0)])
            copy.start()
            pending.append(copy)

        kernel(loads, store, *rest[n_in + n_out + 2 :])
        for pieces in loads:
            for load in pieces if isinstance(pieces, list) else [pieces]:
                load()
        for copy in pending:
            copy.wait()

    spec = pl.BlockSpec(memory_space=pltpu.HBM)
    in_scratch = [
        pltpu.VMEM(shape if count == 1 else (count,) + shape, array.dtype)
        for array, _, count, shape in plans
    ]
    return pl.pallas_call(
        whole,
        out_shape=[jax.ShapeDtypeStruct(out[0], out[1]) for out in outs],
        in_specs=[spec] * len(arrays),
        out_specs=[spec] * n_out,
        scratch_shapes=in_scratch
        + [pltpu.VMEM(out[0], out[1]) for out in outs]
        + [pltpu.SemaphoreType.DMA((total,)), pltpu.SemaphoreType.DMA((out_total,))]
        + list(scratch),
        compiler_params=pltpu.CompilerParams(vmem_limit_bytes=60 * MIB),
        cost_estimate=pl.CostEstimate(flops=flops, bytes_accessed=8 * MIB, transcendentals=0),
        name=name,
    )(*arrays)


def rows_of(start, stop, step=None):
    if step is None:
        return lambda ref, i: ref[start:stop]
    return lambda ref, i: ref[step, start:stop]


def piece_of(ref, i):
    return ref[i]


def fixed(step):
    return lambda ref, i: ref[step]


def pack_kernel(devices, loads, store, columns, extra):
    grid, features, partition, node = loads
    channels, cells = grid.target.shape
    fanout = partition.target.shape[0]
    links = cells * fanout
    width = columns.shape[0]
    slots = 2 * links
    capacity = slots // devices
    place = iota((cells, links), 1)
    repeat = jnp.where(
        functools.reduce(
            jnp.logical_or,
            [place == iota((cells, links), 0) + k * cells for k in range(fanout)],
        ),
        1.0,
        0.0,
    ).astype(bf16)
    order = iota((links, links), 0)
    turn = iota((links, links), 1)
    upper = jnp.where(order <= turn, 1.0, 0.0).astype(bf16)
    spread = jnp.where(order == turn % cells * fanout + turn // cells, 1.0, 0.0).astype(bf16)
    extra[...] = jnp.zeros_like(extra)
    columns[width - EXTRA - 16 : width - EXTRA, :] = jnp.zeros((16, links), bf16)
    store_pieces(extra, features()[...], LEFT_ORDER)
    target = jnp.concatenate([partition()[k : k + 1, :] for k in range(fanout)], axis=1)
    nodes = jnp.concatenate([node()[k : k + 1, :] for k in range(fanout)], axis=1) + 1
    extra[...] = dot(extra[...].astype(bf16), spread)
    extra[24:25, :] = (nodes >> 4).astype(f32)
    extra[25:26, :] = (nodes & 15).astype(f32)
    matches = jnp.where(iota((devices, links), 0) == target, 1.0, 0.0)
    counts = dot(matches.astype(bf16), upper)
    rank = jnp.sum(counts * matches, axis=0, keepdims=True).astype(jnp.int32) - 1
    slot = target * capacity + rank
    select = jnp.where(iota((slots, links), 0) == slot, 1.0, 0.0).astype(bf16)
    columns[0:channels, :] = dot(grid()[...], repeat).astype(bf16)
    columns[width - EXTRA : width, :] = extra[...].astype(bf16)
    store(0, dot(select, columns[...], 1, 1).astype(bf16))


def side_kernel(loads, store, pieces, turned, table):
    features, embed, edge_first, start, link_receiver, update_start, lists = loads
    owned, width = start.target.shape
    edges = features.target.shape[1]
    degree = edges // owned
    devices, slots = lists.target.shape[1:]
    pieces[...] = jnp.zeros_like(pieces)
    turned[...] = jnp.zeros_like(turned)
    table[...] = jnp.zeros_like(table)
    store_pieces(pieces, features()[...], LEFT_ORDER)
    turned[:, 0:EXTRA] = jnp.transpose(pieces[...])
    store_pieces(table, embed()[...], RIGHT_ORDER)
    matrix = table[...].astype(bf16)
    for j in range(degree):
        left = turned[pl.ds(j, owned, stride=degree), :].astype(bf16)
        edge_state = normalize(silu(dot(left, matrix))).astype(bf16)
        store(0, edge_state, j)
        store(1, dot(edge_state, edge_first()[...]).astype(bf16), j)
    store(2, dot(start()[...], link_receiver()[...]).astype(bf16))
    store(3, dot(start()[...], update_start()[...]))
    lists = lists()[0]
    rows = devices * slots
    row = iota((rows, 1), 0)
    picks = jnp.where(iota((rows, devices), 1) == row // slots, 1.0, 0.0).astype(bf16)
    high = dot(picks, (lists >> 4).astype(f32).astype(bf16))
    low = dot(picks, (lists & 15).astype(f32).astype(bf16))
    chosen = jnp.where(iota((rows, slots), 1) == row % slots, high * 16.0 + low, 0.0)
    column = jnp.sum(chosen, axis=1, keepdims=True).astype(jnp.int32)
    store(4, jnp.where(iota((rows, owned), 1) == column, 1.0, 0.0).astype(bf16))


def update(state, summand, second, gain):
    hidden = silu(summand).astype(bf16)
    return (state.astype(f32) + gain * normalize(dot(hidden, second))).astype(bf16)


def send(store, base, state, sender, select):
    sent = dot(state, sender).astype(bf16)
    store(base, dot(select, sent).astype(bf16))
    store(base + 1, sent)


def link_kernel(loads, store, first, table, messages):
    (
        terms,
        embed_first,
        embed_second,
        link_embed,
        link_sender,
        link_edge,
        receiver,
        link_second,
        base,
        update_first,
        update_second,
        gain,
        start,
        sender_first,
        select,
    ) = loads
    owned, width = start.target.shape
    slots = terms.target.shape[0]
    channels = embed_first.target.shape[0]
    tail = table.shape[0]
    first[...] = jnp.zeros_like(first)
    table[...] = jnp.zeros_like(table)
    lanes = iota((8, tail), 1)
    weights = jnp.where(
        lanes == tail - EXTRA + 24, 16.0, jnp.where(lanes == tail - EXTRA + 25, 1.0, 0.0)
    ).astype(bf16)
    chunk = 256
    first[0:channels, :] = embed_first()[...]
    store_pieces(table, link_embed()[...], RIGHT_ORDER, tail - EXTRA)
    matrix = table[...].astype(bf16)
    terms = terms()
    for begin in range(0, slots, chunk):
        rows = slice(begin, begin + chunk)
        extra = terms[rows, width - tail :]
        hidden = silu(dot(terms[rows, :], first[...])).astype(bf16)
        grid_state = normalize(dot(hidden, embed_second()[...])).astype(bf16)
        sender = dot(grid_state, link_sender()[...]).astype(bf16).astype(f32)
        link_state = normalize(silu(dot(extra, matrix))).astype(bf16)
        link_terms = (sender + dot(link_state, link_edge()[...])).astype(bf16)
        parts = extra.astype(f32)
        node = (
            parts[:, tail - EXTRA + 24 : tail - EXTRA + 25] * 16.0
            + parts[:, tail - EXTRA + 25 : tail - EXTRA + 26]
        ).astype(jnp.int32)
        pick = jnp.where(iota((chunk, owned), 1) == node - 1, 1.0, 0.0).astype(bf16)
        summand = link_terms.astype(f32) + dot(pick, receiver()[...])
        message = normalize(dot(silu(summand).astype(bf16), link_second()[...]))
        messages[rows, :] = message.astype(bf16)
    nodes = dot(weights, terms[:, width - tail :], 1, 1)[0:1, :].astype(jnp.int32)
    collect = jnp.where(iota((owned, slots), 0) == nodes - 1, 1.0, 0.0).astype(bf16)
    summed = dot(collect, messages[...]).astype(bf16)
    summand = base()[...] + dot(summed, update_first()[...])
    state = update(start()[...], summand, update_second()[...], gain()[0:1, :])
    store(0, state)
    send(store, 1, state, sender_first()[...], select()[...])


def local_kernel(step, last, loads, store):
    senders, state, receiver_first, sent = loads[:4]
    parts = loads[5 if step else 4]
    degree, owned = senders.target.shape
    columns = jnp.transpose(senders()[...].astype(f32)).astype(jnp.int32)
    kept = dot(state()[...], receiver_first()[...]).astype(bf16).astype(f32)
    for j in range(degree):
        local = jnp.where(iota((owned, owned), 1) == columns[:, j : j + 1], 1.0, 0.0)
        part = parts[j]()[...]
        if step:
            edge_state = (part.astype(f32) + loads[6][j]()[...].astype(f32)).astype(bf16)
            if not last:
                store(1, edge_state, j)
            part = dot(edge_state, loads[4]()[...])
        part = dot(local.astype(bf16), sent()[...]) + part.astype(f32)
        store(0, (part + kept).astype(bf16), j)


def edge_kernel(step, last, loads, store, summands, hiddens, results, total):
    senders, incoming, second, sums = loads[:4]
    (state, state_first, summed_first, update_second, gain) = loads[4:9]
    degree, owned = senders.target.shape
    rows = incoming.target.shape[0]
    columns = jnp.transpose((senders()[...] - owned).astype(f32)).astype(jnp.int32)

    def lead(j):
        pick = jnp.where(iota((owned, rows), 1) == columns[:, j : j + 1], 1.0, 0.0)
        summands[j % 2] = dot(pick.astype(bf16), incoming()[...])

    def middle(j):
        part = sums[j]()
        for begin in range(0, owned, CHUNK):
            some = slice(begin, begin + CHUNK)
            summand = part[some, :].astype(f32) + summands[j % 2, some, :]
            hiddens[j % 2, some, :] = silu(summand).astype(bf16)
        results[j % 2] = dot(hiddens[j % 2], second()[...])

    def tail(j):
        def fill(target):
            for begin in range(0, owned, CHUNK):
                some = slice(begin, begin + CHUNK)
                message = normalize(results[j % 2, some, :]).astype(bf16)
                if target is not None:
                    target[some, :] = message
                message = message.astype(f32)
                total[some, :] = message if j == 0 else total[some, :] + message

        if last:
            fill(None)
        else:
            store(3, fill, j)

    lead(0)
    middle(0)
    for j in range(degree):
        if j + 1 < degree:
            lead(j + 1)
            middle(j + 1)
        tail(j)
    summand = dot(state()[...], state_first()[...]) + dot(
        total[...].astype(bf16), summed_first()[...]
    )
    state = update(
        state()[...], summand, update_second()[...], gain()[step + 1 : step + 2, :]
    )
    store(0, state)
    if not last:
        sender_first, select = loads[9:]
        send(store, 1, state, sender_first()[...], select()[...])


def body(
    grid_inputs,
    link_features,
    link_partition,
    link_node,
    mesh_start,
    edge_features,
    edge_senders,
    halo_lists,
    embed_first,
    embed_second,
    link_embed,
    link_first,
    link_second,
    update_first,
    update_second,
    edge_embed,
    process_first,
    process_second,
    process_update_first,
    process_update_second,
    update_gain,
):
    owned, width = mesh_start.shape
    devices = lax.axis_size("rows")
    cells = grid_inputs.shape[1]
    links = cells * link_partition.shape[1]
    slots = 2 * links
    degree = edge_senders.shape[1]
    edges = owned * degree
    halo_slots = halo_lists.shape[2]
    halo_rows = devices * halo_slots
    senders = edge_senders.T

    def exchange(values):
        values = values.reshape(devices, -1, width)
        return lax.all_to_all(values, "rows", split_axis=0, concat_axis=0, tiled=True).reshape(
            -1, width
        )

    sending = [((halo_rows, width), bf16, 1), ((owned, width), bf16, 1)]
    (packed,) = run(
        functools.partial(pack_kernel, devices),
        "pack",
        [((slots, width), bf16, 1)],
        (grid_inputs, link_features, link_partition.T, link_node.T),
        [pltpu.VMEM((width, links), bf16), pltpu.VMEM((EXTRA, links), f32)],
    )
    terms = exchange(packed)
    edge_state, parts, receiver, base, select = run(
        side_kernel,
        "side",
        [
            ((degree, owned, width), bf16, degree),
            ((degree, owned, width), bf16, degree),
            ((owned, width), bf16, 1),
            ((owned, width), f32, 1),
            ((halo_rows, owned), bf16, 1),
        ],
        (
            edge_features,
            edge_embed,
            (process_first, rows_of(2 * width, 3 * width, 0), 1),
            mesh_start,
            (link_first, rows_of(width, 2 * width), 1),
            (update_first, rows_of(0, width), 1),
            halo_lists,
        ),
        [
            pltpu.VMEM((EXTRA, edges), f32),
            pltpu.VMEM((edges, 128), f32),
            pltpu.VMEM((128, width), f32),
        ],
        flops=10**10,
    )
    state, outgoing, sent = run(
        link_kernel,
        "link",
        [((owned, width), bf16, 1)] + sending,
        (
            terms,
            embed_first,
            embed_second,
            link_embed,
            (link_first, rows_of(0, width), 1),
            (link_first, rows_of(2 * width, 3 * width), 1),
            receiver,
            link_second,
            base,
            (update_first, rows_of(width, 2 * width), 1),
            update_second,
            update_gain,
            mesh_start,
            (process_first, rows_of(0, width, 0), 1),
            select,
        ),
        [
            pltpu.VMEM((width, width), bf16),
            pltpu.VMEM((128, width), f32),
            pltpu.VMEM((slots, width), bf16),
        ],
    )
    steps = process_first.shape[0]
    for step in range(steps):
        last = step + 1 == steps
        incoming = exchange(outgoing)
        extra = []
        if step:
            extra = [(process_first, rows_of(2 * width, 3 * width, step), 1)]
            parts = edge_state
        (sums, *kept) = run(
            functools.partial(local_kernel, step, last),
            f"local{step}",
            [((degree, owned, width), bf16, degree)] * (1 if last or step == 0 else 2),
            [
                senders,
                state,
                (process_first, rows_of(width, 2 * width, step), 1),
                sent,
            ]
            + extra
            + [(parts, piece_of, degree)]
            + ([(message, piece_of, degree)] if step else []),
            flops=10**10,
        )
        if kept:
            edge_state = kept[0]
        outs = [((owned, width), bf16, 1)]
        extra = []
        if not last:
            outs += sending + [((degree, owned, width), bf16, degree)]
            extra = [(process_first, rows_of(0, width, step + 1), 1), select]
        results = run(
            functools.partial(edge_kernel, step, last),
            f"edge{step}",
            outs,
            [
                senders,
                incoming,
                (process_second, fixed(step), 1),
                (sums, piece_of, degree),
                state,
                (process_update_first, rows_of(0, width, step), 1),
                (process_update_first, rows_of(width, 2 * width, step), 1),
                (process_update_second, fixed(step), 1),
                update_gain,
            ]
            + extra,
            [
                pltpu.VMEM((2, owned, width), f32),
                pltpu.VMEM((2, owned, width), bf16),
                pltpu.VMEM((2, owned, width), f32),
                pltpu.VMEM((owned, width), f32),
            ],
        )
        if last:
            return results[0]
        state, outgoing, sent, message = results


def solution(mesh):
    return jax.shard_map(
        body,
        mesh=mesh,
        in_specs=(
            P(None, ("groups", "rows")),
            P(None, "rows"),
            P("rows", None),
            P("rows", None),
            P("rows", None),
            P(None, "rows"),
            P("rows", None),
            P("rows", None, None),
        )
        + (P(),) * 13,
        out_specs=P(("groups", "rows"), None),
        check_vma=False,
    )
```

```python
import functools

import jax
import jax.numpy as jnp
from jax import lax
from jax.experimental import pallas as pl
from jax.experimental.pallas import tpu as pltpu
from jax.sharding import PartitionSpec as P

epsilon = 1e-05
f32 = jnp.float32
bf16 = jnp.bfloat16
MIB = 2**20
EXTRA = 32
CHUNK = 32


def dot(left, right, left_dim=1, right_dim=0):
    return lax.dot_general(
        left, right, (((left_dim,), (right_dim,)), ((), ())), preferred_element_type=f32
    )


def silu(values):
    half = 0.5 * values
    return half + half * jnp.tanh(half)


def normalize(values):
    scale = 1.0 / values.shape[-1]
    center = values - jnp.sum(values, axis=-1, keepdims=True) * scale
    spread = jnp.sum(center * center, axis=-1, keepdims=True) * scale
    return center * lax.rsqrt(spread + epsilon)


def iota(shape, dim):
    return lax.broadcasted_iota(jnp.int32, shape, dim)


def split3(values):
    high = values.astype(bf16).astype(f32)
    rest = values - high
    middle = rest.astype(bf16).astype(f32)
    return high, middle, rest - middle


def store_pieces(ref, values, order, base=0):
    pieces = split3(values)
    rows = values.shape[0]
    for place, piece in enumerate(order):
        ref[base + place * rows : base + (place + 1) * rows, :] = pieces[piece]


LEFT_ORDER = (0, 0, 0, 1, 1, 2)
RIGHT_ORDER = (0, 1, 2, 0, 1, 0)


class Held:
    def __init__(self, target):
        self.target = target

    def __call__(self):
        return self.target


class Load:
    def __init__(self, source, target, semaphore):
        self.copy = pltpu.make_async_copy(source, target, semaphore)
        self.target = target
        self.waiting = True
        self.copy.start()

    def __call__(self):
        if self.waiting:
            self.copy.wait()
            self.waiting = False
        return self.target


def run(kernel, name, outs, args, scratch=(), flops=10**9):
    plans = []
    for arg in args:
        if not isinstance(arg, tuple):
            arg = (arg, None, 1)
        array, take, count = arg
        if take is None:
            shape = array.shape
        else:
            shape = jax.eval_shape(lambda x, take=take: take(x, 0), array).shape
        plans.append((array, take, count, shape))
    n_in, n_out = len(plans), len(outs)
    starts, total = [], 0
    for plan in plans:
        starts.append(total)
        total += plan[2]
    out_starts, out_total = [], 0
    for out in outs:
        out_starts.append(out_total)
        out_total += out[2]
    start_order = [(i, 0) for i in range(n_in) if plans[i][2] == 1]
    split = [i for i in range(n_in) if plans[i][2] > 1]
    if split:
        at = len([i for i in range(split[0]) if plans[i][2] == 1])
        pieces = [(i, piece) for piece in range(plans[split[0]][2]) for i in split]
        start_order[at:at] = pieces
    arrays, places = [], []
    for plan in plans:
        known = [i for i, array in enumerate(arrays) if array is plan[0]]
        if known:
            places.append(known[0])
        else:
            places.append(len(arrays))
            arrays.append(plan[0])

    def whole(*refs):
        ins = refs[: len(arrays)]
        out_refs = refs[len(arrays) : len(arrays) + n_out]
        rest = refs[len(arrays) + n_out :]
        in_vmem, out_vmem = rest[:n_in], rest[n_in : n_in + n_out]
        in_sems, out_sems = rest[n_in + n_out : n_in + n_out + 2]
        loads = [[None] * max(count, 1) for _, _, count, _ in plans]
        for i, (_, _, count, _) in enumerate(plans):
            if count == 0:
                loads[i][0] = Held(ins[places[i]])
        for i, piece in start_order:
            _, take, count, _ = plans[i]
            source = ins[places[i]]
            view = source if take is None else take(source.at, piece)
            target = in_vmem[i] if count == 1 else in_vmem[i].at[piece]
            loads[i][piece] = Load(view, target, in_sems.at[starts[i] + piece])
        loads = [pieces if len(pieces) > 1 else pieces[0] for pieces in loads]
        pending = []

        def store(i, value, piece=None):
            target = out_vmem[i] if piece is None else out_vmem[i].at[piece]
            out = out_refs[i] if piece is None else out_refs[i].at[piece]
            if outs[i][2] == 0:
                target = out
            if callable(value):
                value(target)
            else:
                target[...] = value
            if outs[i][2] == 0:
                return
            copy = pltpu.make_async_copy(target, out, out_sems.at[out_starts[i] + (piece or 0)])
            copy.start()
            pending.append(copy)

        kernel(loads, store, *rest[n_in + n_out + 2 :])
        for pieces in loads:
            for load in pieces if isinstance(pieces, list) else [pieces]:
                load()
        for copy in pending:
            copy.wait()

    hbm = pl.BlockSpec(memory_space=pltpu.HBM)
    vmem = pl.BlockSpec(memory_space=pltpu.VMEM)
    held = [
        any(place == i and plan[2] == 0 for place, plan in zip(places, plans))
        for i in range(len(arrays))
    ]

    def room(shape, dtype, count):
        if count == 0:
            return pltpu.VMEM((8, 128), f32)
        return pltpu.VMEM(shape if count == 1 else (count,) + shape, dtype)

    in_scratch = [room(shape, array.dtype, count) for array, _, count, shape in plans]
    return pl.pallas_call(
        whole,
        out_shape=[jax.ShapeDtypeStruct(out[0], out[1]) for out in outs],
        in_specs=[vmem if here else hbm for here in held],
        out_specs=[hbm if out[2] else vmem for out in outs],
        scratch_shapes=in_scratch
        + [room(out[0], out[1], min(out[2], 1)) for out in outs]
        + [
            pltpu.SemaphoreType.DMA((max(total, 1),)),
            pltpu.SemaphoreType.DMA((max(out_total, 1),)),
        ]
        + list(scratch),
        compiler_params=pltpu.CompilerParams(vmem_limit_bytes=60 * MIB),
        cost_estimate=pl.CostEstimate(flops=flops, bytes_accessed=8 * MIB, transcendentals=0),
        name=name,
    )(*arrays)


def rows_of(start, stop, step=None):
    if step is None:
        return lambda ref, i: ref[start:stop]
    return lambda ref, i: ref[step, start:stop]


def piece_of(ref, i):
    return ref[i]


def fixed(step):
    return lambda ref, i: ref[step]


def pack_kernel(devices, loads, store, columns, extra):
    grid, features, partition, node = loads
    channels, cells = grid.target.shape
    fanout = partition.target.shape[0]
    links = cells * fanout
    width = columns.shape[0]
    slots = 2 * links
    capacity = slots // devices
    place = iota((cells, links), 1)
    repeat = jnp.where(
        functools.reduce(
            jnp.logical_or,
            [place == iota((cells, links), 0) + k * cells for k in range(fanout)],
        ),
        1.0,
        0.0,
    ).astype(bf16)
    order = iota((links, links), 0)
    turn = iota((links, links), 1)
    upper = jnp.where(order <= turn, 1.0, 0.0).astype(bf16)
    spread = jnp.where(order == turn % cells * fanout + turn // cells, 1.0, 0.0).astype(bf16)
    extra[...] = jnp.zeros_like(extra)
    columns[width - EXTRA - 16 : width - EXTRA, :] = jnp.zeros((16, links), bf16)
    store_pieces(extra, features()[...], LEFT_ORDER)
    target = jnp.concatenate([partition()[k : k + 1, :] for k in range(fanout)], axis=1)
    nodes = jnp.concatenate([node()[k : k + 1, :] for k in range(fanout)], axis=1) + 1
    extra[...] = dot(extra[...].astype(bf16), spread)
    extra[24:25, :] = (nodes >> 4).astype(f32)
    extra[25:26, :] = (nodes & 15).astype(f32)
    matches = jnp.where(iota((devices, links), 0) == target, 1.0, 0.0)
    counts = dot(matches.astype(bf16), upper)
    rank = jnp.sum(counts * matches, axis=0, keepdims=True).astype(jnp.int32) - 1
    slot = target * capacity + rank
    select = jnp.where(iota((slots, links), 0) == slot, 1.0, 0.0).astype(bf16)
    columns[0:channels, :] = dot(grid()[...], repeat).astype(bf16)
    columns[width - EXTRA : width, :] = extra[...].astype(bf16)
    store(0, dot(select, columns[...], 1, 1).astype(bf16))


def side_kernel(loads, store, pieces, turned, table):
    features, embed, edge_first, start, link_receiver, update_start, lists = loads
    owned, width = start.target.shape
    edges = features.target.shape[1]
    degree = edges // owned
    devices, slots = lists.target.shape[1:]
    pieces[...] = jnp.zeros_like(pieces)
    turned[...] = jnp.zeros_like(turned)
    table[...] = jnp.zeros_like(table)
    store_pieces(pieces, features()[...], LEFT_ORDER)
    turned[:, 0:EXTRA] = jnp.transpose(pieces[...])
    store_pieces(table, embed()[...], RIGHT_ORDER)
    matrix = table[...].astype(bf16)
    for j in range(degree):
        left = turned[pl.ds(j, owned, stride=degree), :].astype(bf16)
        edge_state = normalize(silu(dot(left, matrix))).astype(bf16)
        store(0, edge_state, j)
        store(1, dot(edge_state, edge_first()[...]).astype(bf16), j)
    store(2, dot(start()[...], link_receiver()[...]).astype(bf16))
    store(3, dot(start()[...], update_start()[...]))
    lists = lists()[0]
    rows = devices * slots
    row = iota((rows, 1), 0)
    picks = jnp.where(iota((rows, devices), 1) == row // slots, 1.0, 0.0).astype(bf16)
    high = dot(picks, (lists >> 4).astype(f32).astype(bf16))
    low = dot(picks, (lists & 15).astype(f32).astype(bf16))
    chosen = jnp.where(iota((rows, slots), 1) == row % slots, high * 16.0 + low, 0.0)
    column = jnp.sum(chosen, axis=1, keepdims=True).astype(jnp.int32)
    store(4, jnp.where(iota((rows, owned), 1) == column, 1.0, 0.0).astype(bf16))


def update(state, summand, second, gain):
    hidden = silu(summand).astype(bf16)
    return (state.astype(f32) + gain * normalize(dot(hidden, second))).astype(bf16)


def send(store, base, state, sender, select):
    sent = dot(state, sender).astype(bf16)
    store(base, dot(select, sent).astype(bf16))
    store(base + 1, sent)


def link_kernel(loads, store, first, table, messages):
    (
        terms,
        embed_first,
        embed_second,
        link_embed,
        link_sender,
        link_edge,
        receiver,
        link_second,
        base,
        update_first,
        update_second,
        gain,
        start,
        sender_first,
        select,
    ) = loads
    owned, width = start.target.shape
    slots = terms.target.shape[0]
    channels = embed_first.target.shape[0]
    tail = table.shape[0]
    first[...] = jnp.zeros_like(first)
    table[...] = jnp.zeros_like(table)
    lanes = iota((8, tail), 1)
    weights = jnp.where(
        lanes == tail - EXTRA + 24, 16.0, jnp.where(lanes == tail - EXTRA + 25, 1.0, 0.0)
    ).astype(bf16)
    chunk = 256
    first[0:channels, :] = embed_first()[...]
    store_pieces(table, link_embed()[...], RIGHT_ORDER, tail - EXTRA)
    matrix = table[...].astype(bf16)
    terms = terms()
    for begin in range(0, slots, chunk):
        rows = slice(begin, begin + chunk)
        extra = terms[rows, width - tail :]
        hidden = silu(dot(terms[rows, :], first[...])).astype(bf16)
        grid_state = normalize(dot(hidden, embed_second()[...])).astype(bf16)
        sender = dot(grid_state, link_sender()[...]).astype(bf16).astype(f32)
        link_state = normalize(silu(dot(extra, matrix))).astype(bf16)
        link_terms = (sender + dot(link_state, link_edge()[...])).astype(bf16)
        parts = extra.astype(f32)
        node = (
            parts[:, tail - EXTRA + 24 : tail - EXTRA + 25] * 16.0
            + parts[:, tail - EXTRA + 25 : tail - EXTRA + 26]
        ).astype(jnp.int32)
        pick = jnp.where(iota((chunk, owned), 1) == node - 1, 1.0, 0.0).astype(bf16)
        summand = link_terms.astype(f32) + dot(pick, receiver()[...])
        message = normalize(dot(silu(summand).astype(bf16), link_second()[...]))
        messages[rows, :] = message.astype(bf16)
    nodes = dot(weights, terms[:, width - tail :], 1, 1)[0:1, :].astype(jnp.int32)
    collect = jnp.where(iota((owned, slots), 0) == nodes - 1, 1.0, 0.0).astype(bf16)
    summed = dot(collect, messages[...]).astype(bf16)
    summand = base()[...] + dot(summed, update_first()[...])
    state = update(start()[...], summand, update_second()[...], gain()[0:1, :])
    store(0, state)
    send(store, 1, state, sender_first()[...], select()[...])


def local_kernel(step, last, loads, store, summands, kept, edges):
    senders, state, receiver_first, sent = loads[:4]
    parts = loads[5 if step else 4]
    degree, owned = senders.target.shape
    columns = jnp.transpose(senders()[...].astype(f32)).astype(jnp.int32)
    kept[...] = dot(state()[...], receiver_first()[...]).astype(bf16).astype(f32)

    def lead(j):
        local = jnp.where(iota((owned, owned), 1) == columns[:, j : j + 1], 1.0, 0.0)
        summand = dot(local.astype(bf16), sent()[...])
        if step:
            target = edges.at[j]
            old, message = parts[j](), loads[6][j]()
            for begin in range(0, owned, CHUNK):
                some = slice(begin, begin + CHUNK)
                edge_state = old[some, :].astype(f32) + message[some, :].astype(f32)
                target[some, :] = edge_state.astype(bf16)
            if not last:
                store(1, target[...], j)
            summand = summand + dot(target[...], loads[4]()[...])
        summands[j % 2] = summand

    def tail(j):
        def fill(target):
            for begin in range(0, owned, CHUNK):
                some = slice(begin, begin + CHUNK)
                summand = summands[j % 2, some, :] + kept[some, :]
                if not step:
                    summand = summand + parts[j]()[some, :].astype(f32)
                target[some, :] = summand.astype(bf16)

        store(0, fill, j)

    lead(0)
    for j in range(degree):
        if j + 1 < degree:
            lead(j + 1)
        tail(j)


def edge_kernel(step, last, loads, store, summands, hiddens, results, total):
    senders, incoming, second, sums = loads[:4]
    (state, state_first, summed_first, update_second, gain) = loads[4:9]
    degree, owned = senders.target.shape
    rows = incoming.target.shape[0]
    columns = jnp.transpose((senders()[...] - owned).astype(f32)).astype(jnp.int32)

    def lead(j):
        pick = jnp.where(iota((owned, rows), 1) == columns[:, j : j + 1], 1.0, 0.0)
        summands[j % 2] = dot(pick.astype(bf16), incoming()[...])

    def middle(j):
        part = sums[j]()
        for begin in range(0, owned, CHUNK):
            some = slice(begin, begin + CHUNK)
            summand = part[some, :].astype(f32) + summands[j % 2, some, :]
            hiddens[j % 2, some, :] = silu(summand).astype(bf16)
        results[j % 2] = dot(hiddens[j % 2], second()[...])

    def tail(j):
        def fill(target):
            for begin in range(0, owned, CHUNK):
                some = slice(begin, begin + CHUNK)
                message = normalize(results[j % 2, some, :]).astype(bf16)
                if target is not None:
                    target[some, :] = message
                message = message.astype(f32)
                total[some, :] = message if j == 0 else total[some, :] + message

        if last:
            fill(None)
        else:
            store(3, fill, j)

    lead(0)
    middle(0)
    for j in range(degree):
        if j + 1 < degree:
            lead(j + 1)
            middle(j + 1)
        tail(j)
    summand = dot(state()[...], state_first()[...]) + dot(
        total[...].astype(bf16), summed_first()[...]
    )
    state = update(
        state()[...], summand, update_second()[...], gain()[step + 1 : step + 2, :]
    )
    store(0, state)
    if not last:
        sender_first, select = loads[9:]
        send(store, 1, state, sender_first()[...], select()[...])


def body(
    grid_inputs,
    link_features,
    link_partition,
    link_node,
    mesh_start,
    edge_features,
    edge_senders,
    halo_lists,
    embed_first,
    embed_second,
    link_embed,
    link_first,
    link_second,
    update_first,
    update_second,
    edge_embed,
    process_first,
    process_second,
    process_update_first,
    process_update_second,
    update_gain,
):
    owned, width = mesh_start.shape
    devices = lax.axis_size("rows")
    cells = grid_inputs.shape[1]
    links = cells * link_partition.shape[1]
    slots = 2 * links
    degree = edge_senders.shape[1]
    edges = owned * degree
    halo_slots = halo_lists.shape[2]
    halo_rows = devices * halo_slots
    senders = edge_senders.T

    def exchange(values):
        values = values.reshape(devices, -1, width)
        return lax.all_to_all(values, "rows", split_axis=0, concat_axis=0, tiled=True).reshape(
            -1, width
        )

    sending = [((halo_rows, width), bf16, 0), ((owned, width), bf16, 0)]
    (packed,) = run(
        functools.partial(pack_kernel, devices),
        "pack",
        [((slots, width), bf16, 0)],
        (grid_inputs, link_features, link_partition.T, link_node.T),
        [pltpu.VMEM((width, links), bf16), pltpu.VMEM((EXTRA, links), f32)],
    )
    terms = exchange(packed)
    edge_state, parts, receiver, base, select = run(
        side_kernel,
        "side",
        [
            ((degree, owned, width), bf16, degree),
            ((degree, owned, width), bf16, degree),
            ((owned, width), bf16, 1),
            ((owned, width), f32, 1),
            ((halo_rows, owned), bf16, 1),
        ],
        (
            edge_features,
            edge_embed,
            (process_first, rows_of(2 * width, 3 * width, 0), 1),
            mesh_start,
            (link_first, rows_of(width, 2 * width), 1),
            (update_first, rows_of(0, width), 1),
            halo_lists,
        ),
        [
            pltpu.VMEM((EXTRA, edges), f32),
            pltpu.VMEM((edges, 128), f32),
            pltpu.VMEM((128, width), f32),
        ],
        flops=10**10,
    )
    state, outgoing, sent = run(
        link_kernel,
        "link",
        [((owned, width), bf16, 0)] + sending,
        (
            (terms, None, 0),
            embed_first,
            embed_second,
            link_embed,
            (link_first, rows_of(0, width), 1),
            (link_first, rows_of(2 * width, 3 * width), 1),
            receiver,
            link_second,
            base,
            (update_first, rows_of(width, 2 * width), 1),
            update_second,
            update_gain,
            mesh_start,
            (process_first, rows_of(0, width, 0), 1),
            select,
        ),
        [
            pltpu.VMEM((width, width), bf16),
            pltpu.VMEM((128, width), f32),
            pltpu.VMEM((slots, width), bf16),
        ],
    )
    steps = process_first.shape[0]
    for step in range(steps):
        last = step + 1 == steps
        incoming = exchange(outgoing)
        extra = []
        if step:
            extra = [(process_first, rows_of(2 * width, 3 * width, step), 1)]
            parts = edge_state
        (sums, *later) = run(
            functools.partial(local_kernel, step, last),
            f"local{step}",
            [((degree, owned, width), bf16, degree)] * (1 if last or step == 0 else 2),
            [
                senders,
                (state, None, 0),
                (process_first, rows_of(width, 2 * width, step), 1),
                (sent, None, 0),
            ]
            + extra
            + [(parts, piece_of, degree)]
            + ([(message, piece_of, degree)] if step else []),
            [
                pltpu.VMEM((2, owned, width), f32),
                pltpu.VMEM((owned, width), f32),
                pltpu.VMEM((degree, owned, width), bf16),
            ],
            flops=10**10,
        )
        if later:
            edge_state = later[0]
        outs = [((owned, width), bf16, 1 if last else 0)]
        extra = []
        if not last:
            outs += sending + [((degree, owned, width), bf16, degree)]
            extra = [(process_first, rows_of(0, width, step + 1), 1), select]
        results = run(
            functools.partial(edge_kernel, step, last),
            f"edge{step}",
            outs,
            [
                senders,
                (incoming, None, 0),
                (process_second, fixed(step), 1),
                (sums, piece_of, degree),
                (state, None, 0),
                (process_update_first, rows_of(0, width, step), 1),
                (process_update_first, rows_of(width, 2 * width, step), 1),
                (process_update_second, fixed(step), 1),
                update_gain,
            ]
            + extra,
            [
                pltpu.VMEM((2, owned, width), f32),
                pltpu.VMEM((2, owned, width), bf16),
                pltpu.VMEM((2, owned, width), f32),
                pltpu.VMEM((owned, width), f32),
            ],
        )
        if last:
            return results[0]
        state, outgoing, sent, message = results


def solution(mesh):
    return jax.shard_map(
        body,
        mesh=mesh,
        in_specs=(
            P(None, ("groups", "rows")),
            P(None, "rows"),
            P("rows", None),
            P("rows", None),
            P("rows", None),
            P(None, "rows"),
            P("rows", None),
            P("rows", None, None),
        )
        + (P(),) * 13,
        out_specs=P(("groups", "rows"), None),
        check_vma=False,
    )
```

```python
import functools

import jax
import jax.numpy as jnp
from jax import lax
from jax.experimental import pallas as pl
from jax.experimental.pallas import tpu as pltpu
from jax.sharding import PartitionSpec as P

epsilon = 1e-05
f32 = jnp.float32
bf16 = jnp.bfloat16
MIB = 2**20
EXTRA = 32
CHUNK = 32


def dot(left, right, left_dim=1, right_dim=0):
    return lax.dot_general(
        left, right, (((left_dim,), (right_dim,)), ((), ())), preferred_element_type=f32
    )


def silu(values):
    half = 0.5 * values
    return half + half * jnp.tanh(half)


def normalize(values):
    scale = 1.0 / values.shape[-1]
    center = values - jnp.sum(values, axis=-1, keepdims=True) * scale
    spread = jnp.sum(center * center, axis=-1, keepdims=True) * scale
    return center * lax.rsqrt(spread + epsilon)


def iota(shape, dim):
    return lax.broadcasted_iota(jnp.int32, shape, dim)


def split3(values):
    high = values.astype(bf16).astype(f32)
    rest = values - high
    middle = rest.astype(bf16).astype(f32)
    return high, middle, rest - middle


def store_pieces(ref, values, order, base=0):
    pieces = split3(values)
    rows = values.shape[0]
    for place, piece in enumerate(order):
        ref[base + place * rows : base + (place + 1) * rows, :] = pieces[piece]


LEFT_ORDER = (0, 0, 0, 1, 1, 2)
RIGHT_ORDER = (0, 1, 2, 0, 1, 0)


class Held:
    def __init__(self, target):
        self.target = target

    def __call__(self):
        return self.target


class Load:
    def __init__(self, source, target, semaphore):
        self.copy = pltpu.make_async_copy(source, target, semaphore)
        self.target = target
        self.waiting = True
        self.copy.start()

    def __call__(self):
        if self.waiting:
            self.copy.wait()
            self.waiting = False
        return self.target


def run(kernel, name, outs, args, scratch=(), flops=10**9):
    plans = []
    for arg in args:
        if not isinstance(arg, tuple):
            arg = (arg, None, 1)
        array, take, count = arg
        if take is None:
            shape = array.shape
        else:
            shape = jax.eval_shape(lambda x, take=take: take(x, 0), array).shape
        plans.append((array, take, count, shape))
    n_in, n_out = len(plans), len(outs)
    starts, total = [], 0
    for plan in plans:
        starts.append(total)
        total += plan[2]
    out_starts, out_total = [], 0
    for out in outs:
        out_starts.append(out_total)
        out_total += out[2]
    start_order = [(i, 0) for i in range(n_in) if plans[i][2] == 1]
    split = [i for i in range(n_in) if plans[i][2] > 1]
    if split:
        at = len([i for i in range(split[0]) if plans[i][2] == 1])
        pieces = [(i, piece) for piece in range(plans[split[0]][2]) for i in split]
        start_order[at:at] = pieces
    arrays, places = [], []
    for plan in plans:
        known = [i for i, array in enumerate(arrays) if array is plan[0]]
        if known:
            places.append(known[0])
        else:
            places.append(len(arrays))
            arrays.append(plan[0])

    def whole(*refs):
        ins = refs[: len(arrays)]
        out_refs = refs[len(arrays) : len(arrays) + n_out]
        rest = refs[len(arrays) + n_out :]
        in_vmem, out_vmem = rest[:n_in], rest[n_in : n_in + n_out]
        in_sems, out_sems = rest[n_in + n_out : n_in + n_out + 2]
        loads = [[None] * max(count, 1) for _, _, count, _ in plans]
        for i, (_, _, count, _) in enumerate(plans):
            if count == 0:
                loads[i][0] = Held(ins[places[i]])
        for i, piece in start_order:
            _, take, count, _ = plans[i]
            source = ins[places[i]]
            view = source if take is None else take(source.at, piece)
            target = in_vmem[i] if count == 1 else in_vmem[i].at[piece]
            loads[i][piece] = Load(view, target, in_sems.at[starts[i] + piece])
        loads = [pieces if len(pieces) > 1 else pieces[0] for pieces in loads]
        pending = []

        def store(i, value, piece=None):
            target = out_vmem[i] if piece is None else out_vmem[i].at[piece]
            out = out_refs[i] if piece is None else out_refs[i].at[piece]
            if outs[i][2] == 0:
                target = out
            if callable(value):
                value(target)
            else:
                target[...] = value
            if outs[i][2] == 0:
                return
            copy = pltpu.make_async_copy(target, out, out_sems.at[out_starts[i] + (piece or 0)])
            copy.start()
            pending.append(copy)

        kernel(loads, store, *rest[n_in + n_out + 2 :])
        for pieces in loads:
            for load in pieces if isinstance(pieces, list) else [pieces]:
                load()
        for copy in pending:
            copy.wait()

    hbm = pl.BlockSpec(memory_space=pltpu.HBM)
    vmem = pl.BlockSpec(memory_space=pltpu.VMEM)
    held = [
        any(place == i and plan[2] == 0 for place, plan in zip(places, plans))
        for i in range(len(arrays))
    ]

    def room(shape, dtype, count):
        if count == 0:
            return pltpu.VMEM((8, 128), f32)
        return pltpu.VMEM(shape if count == 1 else (count,) + shape, dtype)

    in_scratch = [room(shape, array.dtype, count) for array, _, count, shape in plans]
    return pl.pallas_call(
        whole,
        out_shape=[jax.ShapeDtypeStruct(out[0], out[1]) for out in outs],
        in_specs=[vmem if here else hbm for here in held],
        out_specs=[hbm if out[2] else vmem for out in outs],
        scratch_shapes=in_scratch
        + [room(out[0], out[1], min(out[2], 1)) for out in outs]
        + [
            pltpu.SemaphoreType.DMA((max(total, 1),)),
            pltpu.SemaphoreType.DMA((max(out_total, 1),)),
        ]
        + list(scratch),
        compiler_params=pltpu.CompilerParams(vmem_limit_bytes=56 * MIB),
        cost_estimate=pl.CostEstimate(flops=flops, bytes_accessed=8 * MIB, transcendentals=0),
        name=name,
    )(*arrays)


def rows_of(start, stop, step=None):
    if step is None:
        return lambda ref, i: ref[start:stop]
    return lambda ref, i: ref[step, start:stop]


def piece_of(ref, i):
    return ref[i]


def fixed(step):
    return lambda ref, i: ref[step]


def pack_kernel(devices, loads, store, columns, extra):
    grid, features, partition, node = loads
    channels, cells = grid.target.shape
    fanout = partition.target.shape[0]
    links = cells * fanout
    width = columns.shape[0]
    slots = 2 * links
    capacity = slots // devices
    place = iota((cells, links), 1)
    repeat = jnp.where(
        functools.reduce(
            jnp.logical_or,
            [place == iota((cells, links), 0) + k * cells for k in range(fanout)],
        ),
        1.0,
        0.0,
    ).astype(bf16)
    order = iota((links, links), 0)
    turn = iota((links, links), 1)
    upper = jnp.where(order <= turn, 1.0, 0.0).astype(bf16)
    spread = jnp.where(order == turn % cells * fanout + turn // cells, 1.0, 0.0).astype(bf16)
    extra[...] = jnp.zeros_like(extra)
    columns[width - EXTRA - 16 : width - EXTRA, :] = jnp.zeros((16, links), bf16)
    store_pieces(extra, features()[...], LEFT_ORDER)
    target = jnp.concatenate([partition()[k : k + 1, :] for k in range(fanout)], axis=1)
    nodes = jnp.concatenate([node()[k : k + 1, :] for k in range(fanout)], axis=1) + 1
    extra[...] = dot(extra[...].astype(bf16), spread)
    extra[24:25, :] = (nodes >> 4).astype(f32)
    extra[25:26, :] = (nodes & 15).astype(f32)
    matches = jnp.where(iota((devices, links), 0) == target, 1.0, 0.0)
    counts = dot(matches.astype(bf16), upper)
    rank = jnp.sum(counts * matches, axis=0, keepdims=True).astype(jnp.int32) - 1
    slot = target * capacity + rank
    select = jnp.where(iota((slots, links), 0) == slot, 1.0, 0.0).astype(bf16)
    columns[0:channels, :] = dot(grid()[...], repeat).astype(bf16)
    columns[width - EXTRA : width, :] = extra[...].astype(bf16)
    store(0, dot(select, columns[...], 1, 1).astype(bf16))


def side_kernel(loads, store, pieces, turned, table):
    features, embed, edge_first, start, link_receiver, update_start, lists = loads
    owned, width = start.target.shape
    edges = features.target.shape[1]
    degree = edges // owned
    devices, slots = lists.target.shape[1:]
    pieces[...] = jnp.zeros_like(pieces)
    turned[...] = jnp.zeros_like(turned)
    table[...] = jnp.zeros_like(table)
    store_pieces(pieces, features()[...], LEFT_ORDER)
    turned[:, 0:EXTRA] = jnp.transpose(pieces[...])
    store_pieces(table, embed()[...], RIGHT_ORDER)
    matrix = table[...].astype(bf16)
    for j in range(degree):
        left = turned[pl.ds(j, owned, stride=degree), :].astype(bf16)
        edge_state = normalize(silu(dot(left, matrix))).astype(bf16)
        store(0, edge_state, j)
        store(1, dot(edge_state, edge_first()[...]).astype(bf16), j)
    store(2, dot(start()[...], link_receiver()[...]).astype(bf16))
    store(3, dot(start()[...], update_start()[...]))
    lists = lists()[0]
    rows = devices * slots
    row = iota((rows, 1), 0)
    picks = jnp.where(iota((rows, devices), 1) == row // slots, 1.0, 0.0).astype(bf16)
    high = dot(picks, (lists >> 4).astype(f32).astype(bf16))
    low = dot(picks, (lists & 15).astype(f32).astype(bf16))
    chosen = jnp.where(iota((rows, slots), 1) == row % slots, high * 16.0 + low, 0.0)
    column = jnp.sum(chosen, axis=1, keepdims=True).astype(jnp.int32)
    store(4, jnp.where(iota((rows, owned), 1) == column, 1.0, 0.0).astype(bf16))


def update(state, summand, second, gain):
    hidden = silu(summand).astype(bf16)
    return (state.astype(f32) + gain * normalize(dot(hidden, second))).astype(bf16)


def send(store, base, state, sender, select):
    sent = dot(state, sender).astype(bf16)
    store(base, dot(select, sent).astype(bf16))
    store(base + 1, sent)


def link_kernel(loads, store, first, table, messages):
    (
        terms,
        embed_first,
        embed_second,
        link_embed,
        link_sender,
        link_edge,
        receiver,
        link_second,
        base,
        update_first,
        update_second,
        gain,
        start,
        sender_first,
        select,
    ) = loads
    owned, width = start.target.shape
    slots = terms.target.shape[0]
    channels = embed_first.target.shape[0]
    tail = table.shape[0]
    first[...] = jnp.zeros_like(first)
    table[...] = jnp.zeros_like(table)
    lanes = iota((8, tail), 1)
    weights = jnp.where(
        lanes == tail - EXTRA + 24, 16.0, jnp.where(lanes == tail - EXTRA + 25, 1.0, 0.0)
    ).astype(bf16)
    chunk = 256
    first[0:channels, :] = embed_first()[...]
    store_pieces(table, link_embed()[...], RIGHT_ORDER, tail - EXTRA)
    matrix = table[...].astype(bf16)
    terms = terms()
    for begin in range(0, slots, chunk):
        rows = slice(begin, begin + chunk)
        extra = terms[rows, width - tail :]
        hidden = silu(dot(terms[rows, :], first[...])).astype(bf16)
        grid_state = normalize(dot(hidden, embed_second()[...])).astype(bf16)
        sender = dot(grid_state, link_sender()[...]).astype(bf16).astype(f32)
        link_state = normalize(silu(dot(extra, matrix))).astype(bf16)
        link_terms = (sender + dot(link_state, link_edge()[...])).astype(bf16)
        parts = extra.astype(f32)
        node = (
            parts[:, tail - EXTRA + 24 : tail - EXTRA + 25] * 16.0
            + parts[:, tail - EXTRA + 25 : tail - EXTRA + 26]
        ).astype(jnp.int32)
        pick = jnp.where(iota((chunk, owned), 1) == node - 1, 1.0, 0.0).astype(bf16)
        summand = link_terms.astype(f32) + dot(pick, receiver()[...])
        message = normalize(dot(silu(summand).astype(bf16), link_second()[...]))
        messages[rows, :] = message.astype(bf16)
    nodes = dot(weights, terms[:, width - tail :], 1, 1)[0:1, :].astype(jnp.int32)
    collect = jnp.where(iota((owned, slots), 0) == nodes - 1, 1.0, 0.0).astype(bf16)
    summed = dot(collect, messages[...]).astype(bf16)
    summand = base()[...] + dot(summed, update_first()[...])
    state = update(start()[...], summand, update_second()[...], gain()[0:1, :])
    store(0, state)
    send(store, 1, state, sender_first()[...], select()[...])


def local_kernel(step, last, loads, store, summands, kept, edges):
    senders, state, receiver_first, sent = loads[:4]
    parts = loads[5 if step else 4]
    degree, owned = senders.target.shape
    columns = jnp.transpose(senders()[...].astype(f32)).astype(jnp.int32)
    kept[...] = dot(state()[...], receiver_first()[...]).astype(bf16).astype(f32)

    def lead(j):
        local = jnp.where(iota((owned, owned), 1) == columns[:, j : j + 1], 1.0, 0.0)
        summand = dot(local.astype(bf16), sent()[...])
        if step:
            target = edges.at[j]
            old, message = parts[j](), loads[6][j]()
            for begin in range(0, owned, CHUNK):
                some = slice(begin, begin + CHUNK)
                edge_state = old[some, :].astype(f32) + message[some, :].astype(f32)
                target[some, :] = edge_state.astype(bf16)
            if not last:
                store(1, target[...], j)
            summand = summand + dot(target[...], loads[4]()[...])
        summands[j % 2] = summand

    def tail(j):
        def fill(target):
            for begin in range(0, owned, CHUNK):
                some = slice(begin, begin + CHUNK)
                summand = summands[j % 2, some, :] + kept[some, :]
                if not step:
                    summand = summand + parts[j]()[some, :].astype(f32)
                target[some, :] = summand.astype(bf16)

        store(0, fill, j)

    lead(0)
    for j in range(degree):
        if j + 1 < degree:
            lead(j + 1)
        tail(j)


def edge_kernel(step, last, loads, store, summands, hiddens, results, total):
    senders, incoming, second, sums = loads[:4]
    (state, state_first, summed_first, update_second, gain) = loads[4:9]
    degree, owned = senders.target.shape
    rows = incoming.target.shape[0]
    columns = jnp.transpose((senders()[...] - owned).astype(f32)).astype(jnp.int32)

    def lead(j):
        pick = jnp.where(iota((owned, rows), 1) == columns[:, j : j + 1], 1.0, 0.0)
        summands[j % 2] = dot(pick.astype(bf16), incoming()[...])

    def middle(j):
        part = sums[j]()
        for begin in range(0, owned, CHUNK):
            some = slice(begin, begin + CHUNK)
            summand = part[some, :].astype(f32) + summands[j % 2, some, :]
            hiddens[j % 2, some, :] = silu(summand).astype(bf16)
        results[j % 2] = dot(hiddens[j % 2], second()[...])

    def tail(j):
        def fill(target):
            for begin in range(0, owned, CHUNK):
                some = slice(begin, begin + CHUNK)
                message = normalize(results[j % 2, some, :]).astype(bf16)
                if target is not None:
                    target[some, :] = message
                message = message.astype(f32)
                total[some, :] = message if j == 0 else total[some, :] + message

        if last:
            fill(None)
        else:
            store(3, fill, j)

    lead(0)
    middle(0)
    for j in range(degree):
        if j + 1 < degree:
            lead(j + 1)
            middle(j + 1)
        tail(j)
    summand = dot(state()[...], state_first()[...]) + dot(
        total[...].astype(bf16), summed_first()[...]
    )
    state = update(
        state()[...], summand, update_second()[...], gain()[step + 1 : step + 2, :]
    )
    store(0, state)
    if not last:
        sender_first, select = loads[9:]
        send(store, 1, state, sender_first()[...], select()[...])


def body(
    grid_inputs,
    link_features,
    link_partition,
    link_node,
    mesh_start,
    edge_features,
    edge_senders,
    halo_lists,
    embed_first,
    embed_second,
    link_embed,
    link_first,
    link_second,
    update_first,
    update_second,
    edge_embed,
    process_first,
    process_second,
    process_update_first,
    process_update_second,
    update_gain,
):
    owned, width = mesh_start.shape
    devices = lax.axis_size("rows")
    cells = grid_inputs.shape[1]
    links = cells * link_partition.shape[1]
    slots = 2 * links
    degree = edge_senders.shape[1]
    edges = owned * degree
    halo_slots = halo_lists.shape[2]
    halo_rows = devices * halo_slots
    senders = edge_senders.T

    def exchange(values):
        values = values.reshape(devices, -1, width)
        return lax.all_to_all(values, "rows", split_axis=0, concat_axis=0, tiled=True).reshape(
            -1, width
        )

    sending = [((halo_rows, width), bf16, 1), ((owned, width), bf16, 1)]
    (packed,) = run(
        functools.partial(pack_kernel, devices),
        "pack",
        [((slots, width), bf16, 1)],
        (grid_inputs, link_features, link_partition.T, link_node.T),
        [pltpu.VMEM((width, links), bf16), pltpu.VMEM((EXTRA, links), f32)],
    )
    terms = exchange(packed)
    edge_state, parts, receiver, base, select = run(
        side_kernel,
        "side",
        [
            ((degree, owned, width), bf16, degree),
            ((degree, owned, width), bf16, degree),
            ((owned, width), bf16, 1),
            ((owned, width), f32, 1),
            ((halo_rows, owned), bf16, 1),
        ],
        (
            edge_features,
            edge_embed,
            (process_first, rows_of(2 * width, 3 * width, 0), 1),
            mesh_start,
            (link_first, rows_of(width, 2 * width), 1),
            (update_first, rows_of(0, width), 1),
            halo_lists,
        ),
        [
            pltpu.VMEM((EXTRA, edges), f32),
            pltpu.VMEM((edges, 128), f32),
            pltpu.VMEM((128, width), f32),
        ],
        flops=10**10,
    )
    state, outgoing, sent = run(
        link_kernel,
        "link",
        [((owned, width), bf16, 1)] + sending,
        (
            (terms, None, 0),
            embed_first,
            embed_second,
            link_embed,
            (link_first, rows_of(0, width), 1),
            (link_first, rows_of(2 * width, 3 * width), 1),
            receiver,
            link_second,
            base,
            (update_first, rows_of(width, 2 * width), 1),
            update_second,
            update_gain,
            mesh_start,
            (process_first, rows_of(0, width, 0), 1),
            select,
        ),
        [
            pltpu.VMEM((width, width), bf16),
            pltpu.VMEM((128, width), f32),
            pltpu.VMEM((slots, width), bf16),
        ],
    )
    steps = process_first.shape[0]
    for step in range(steps):
        last = step + 1 == steps
        incoming = exchange(outgoing)
        extra = []
        if step:
            extra = [(process_first, rows_of(2 * width, 3 * width, step), 1)]
            parts = edge_state
        (sums, *later) = run(
            functools.partial(local_kernel, step, last),
            f"local{step}",
            [((degree, owned, width), bf16, degree)] * (1 if last or step == 0 else 2),
            [
                senders,
                state,
                (process_first, rows_of(width, 2 * width, step), 1),
                sent,
            ]
            + extra
            + [(parts, piece_of, degree)]
            + ([(message, piece_of, degree)] if step else []),
            [
                pltpu.VMEM((2, owned, width), f32),
                pltpu.VMEM((owned, width), f32),
                pltpu.VMEM((degree, owned, width), bf16),
            ],
            flops=10**10,
        )
        if later:
            edge_state = later[0]
        outs = [((owned, width), bf16, 1)]
        extra = []
        if not last:
            outs += sending + [((degree, owned, width), bf16, degree)]
            extra = [(process_first, rows_of(0, width, step + 1), 1), select]
        results = run(
            functools.partial(edge_kernel, step, last),
            f"edge{step}",
            outs,
            [
                senders,
                (incoming, None, 0),
                (process_second, fixed(step), 1),
                (sums, piece_of, degree),
                state,
                (process_update_first, rows_of(0, width, step), 1),
                (process_update_first, rows_of(width, 2 * width, step), 1),
                (process_update_second, fixed(step), 1),
                update_gain,
            ]
            + extra,
            [
                pltpu.VMEM((2, owned, width), f32),
                pltpu.VMEM((2, owned, width), bf16),
                pltpu.VMEM((2, owned, width), f32),
                pltpu.VMEM((owned, width), f32),
            ],
        )
        if last:
            return results[0]
        state, outgoing, sent, message = results


def solution(mesh):
    return jax.shard_map(
        body,
        mesh=mesh,
        in_specs=(
            P(None, ("groups", "rows")),
            P(None, "rows"),
            P("rows", None),
            P("rows", None),
            P("rows", None),
            P(None, "rows"),
            P("rows", None),
            P("rows", None, None),
        )
        + (P(),) * 13,
        out_specs=P(("groups", "rows"), None),
        check_vma=False,
    )
```

```python
import functools

import jax
import jax.numpy as jnp
from jax import lax
from jax.experimental import pallas as pl
from jax.experimental.pallas import tpu as pltpu
from jax.sharding import PartitionSpec as P

epsilon = 1e-05
f32 = jnp.float32
bf16 = jnp.bfloat16
MIB = 2**20
EXTRA = 32
CHUNK = 32


def dot(left, right, left_dim=1, right_dim=0):
    return lax.dot_general(
        left, right, (((left_dim,), (right_dim,)), ((), ())), preferred_element_type=f32
    )


def silu(values):
    half = 0.5 * values
    return half + half * jnp.tanh(half)


def silu16(values):
    half = (0.5 * values).astype(bf16)
    return half + half * jnp.tanh(half)


def normalize(values):
    scale = 1.0 / values.shape[-1]
    center = values - jnp.sum(values, axis=-1, keepdims=True) * scale
    spread = jnp.sum(center * center, axis=-1, keepdims=True) * scale
    return center * lax.rsqrt(spread + epsilon)


def iota(shape, dim):
    return lax.broadcasted_iota(jnp.int32, shape, dim)


def split3(values):
    high = values.astype(bf16).astype(f32)
    rest = values - high
    middle = rest.astype(bf16).astype(f32)
    return high, middle, rest - middle


def store_pieces(ref, values, order, base=0):
    pieces = split3(values)
    rows = values.shape[0]
    for place, piece in enumerate(order):
        ref[base + place * rows : base + (place + 1) * rows, :] = pieces[piece]


LEFT_ORDER = (0, 0, 0, 1, 1, 2)
RIGHT_ORDER = (0, 1, 2, 0, 1, 0)


class Load:
    def __init__(self, source, target, semaphore):
        self.copy = pltpu.make_async_copy(source, target, semaphore)
        self.target = target
        self.waiting = True
        self.copy.start()

    def __call__(self):
        if self.waiting:
            self.copy.wait()
            self.waiting = False
        return self.target


def run(kernel, name, outs, args, scratch=(), flops=10**9):
    plans = []
    for arg in args:
        if not isinstance(arg, tuple):
            arg = (arg, None, 1)
        array, take, count = arg
        if take is None:
            shape = array.shape
        else:
            shape = jax.eval_shape(lambda x, take=take: take(x, 0), array).shape
        plans.append((array, take, count, shape))
    n_in, n_out = len(plans), len(outs)
    starts, total = [], 0
    for plan in plans:
        starts.append(total)
        total += plan[2]
    out_starts, out_total = [], 0
    for out in outs:
        out_starts.append(out_total)
        out_total += out[2]
    start_order = [(i, 0) for i in range(n_in) if plans[i][2] == 1]
    split = [i for i in range(n_in) if plans[i][2] > 1]
    if split:
        at = len([i for i in range(split[0]) if plans[i][2] == 1])
        pieces = [(i, piece) for piece in range(plans[split[0]][2]) for i in split]
        start_order[at:at] = pieces
    arrays, places = [], []
    for plan in plans:
        known = [i for i, array in enumerate(arrays) if array is plan[0]]
        if known:
            places.append(known[0])
        else:
            places.append(len(arrays))
            arrays.append(plan[0])

    def whole(*refs):
        ins = refs[: len(arrays)]
        out_refs = refs[len(arrays) : len(arrays) + n_out]
        rest = refs[len(arrays) + n_out :]
        in_vmem, out_vmem = rest[:n_in], rest[n_in : n_in + n_out]
        in_sems, out_sems = rest[n_in + n_out : n_in + n_out + 2]
        loads = [[None] * count for _, _, count, _ in plans]
        for i, piece in start_order:
            _, take, count, _ = plans[i]
            source = ins[places[i]]
            view = source if take is None else take(source.at, piece)
            target = in_vmem[i] if count == 1 else in_vmem[i].at[piece]
            loads[i][piece] = Load(view, target, in_sems.at[starts[i] + piece])
        loads = [pieces if len(pieces) > 1 else pieces[0] for pieces in loads]
        pending, waiting = [], []

        def store(i, value, piece=None, hold=False):
            target = out_vmem[i] if piece is None else out_vmem[i].at[piece]
            out = out_refs[i] if piece is None else out_refs[i].at[piece]
            if callable(value):
                value(target)
            else:
                target[...] = value
            copy = pltpu.make_async_copy(target, out, out_sems.at[out_starts[i] + (piece or 0)])
            waiting.append(copy)
            if not hold:
                flush()

        def flush():
            for copy in waiting:
                copy.start()
            pending.extend(waiting)
            waiting.clear()

        store.flush = flush
        kernel(loads, store, *rest[n_in + n_out + 2 :])
        for pieces in loads:
            for load in pieces if isinstance(pieces, list) else [pieces]:
                load()
        flush()
        for copy in pending:
            copy.wait()

    spec = pl.BlockSpec(memory_space=pltpu.HBM)
    in_scratch = [
        pltpu.VMEM(shape if count == 1 else (count,) + shape, array.dtype)
        for array, _, count, shape in plans
    ]
    return pl.pallas_call(
        whole,
        out_shape=[jax.ShapeDtypeStruct(out[0], out[1]) for out in outs],
        in_specs=[spec] * len(arrays),
        out_specs=[spec] * n_out,
        scratch_shapes=in_scratch
        + [pltpu.VMEM(out[0], out[1]) for out in outs]
        + [pltpu.SemaphoreType.DMA((total,)), pltpu.SemaphoreType.DMA((out_total,))]
        + list(scratch),
        compiler_params=pltpu.CompilerParams(vmem_limit_bytes=60 * MIB),
        cost_estimate=pl.CostEstimate(flops=flops, bytes_accessed=8 * MIB, transcendentals=0),
        name=name,
    )(*arrays)


def rows_of(start, stop, step=None):
    if step is None:
        return lambda ref, i: ref[start:stop]
    return lambda ref, i: ref[step, start:stop]


def piece_of(ref, i):
    return ref[i]


def fixed(step):
    return lambda ref, i: ref[step]


def pack_kernel(devices, loads, store, columns, extra):
    grid, features, partition, node = loads
    channels, cells = grid.target.shape
    fanout = partition.target.shape[0]
    links = cells * fanout
    width = columns.shape[0]
    slots = 2 * links
    capacity = slots // devices
    place = iota((cells, links), 1)
    repeat = jnp.where(
        functools.reduce(
            jnp.logical_or,
            [place == iota((cells, links), 0) + k * cells for k in range(fanout)],
        ),
        1.0,
        0.0,
    ).astype(bf16)
    order = iota((links, links), 0)
    turn = iota((links, links), 1)
    upper = jnp.where(order <= turn, 1.0, 0.0).astype(bf16)
    spread = jnp.where(order == turn % cells * fanout + turn // cells, 1.0, 0.0).astype(bf16)
    extra[...] = jnp.zeros_like(extra)
    columns[width - EXTRA - 16 : width - EXTRA, :] = jnp.zeros((16, links), bf16)
    store_pieces(extra, features()[...], LEFT_ORDER)
    target = jnp.concatenate([partition()[k : k + 1, :] for k in range(fanout)], axis=1)
    nodes = jnp.concatenate([node()[k : k + 1, :] for k in range(fanout)], axis=1) + 1
    extra[...] = dot(extra[...].astype(bf16), spread)
    extra[24:25, :] = (nodes >> 4).astype(f32)
    extra[25:26, :] = (nodes & 15).astype(f32)
    matches = jnp.where(iota((devices, links), 0) == target, 1.0, 0.0)
    counts = dot(matches.astype(bf16), upper)
    rank = jnp.sum(counts * matches, axis=0, keepdims=True).astype(jnp.int32) - 1
    slot = target * capacity + rank
    select = jnp.where(iota((slots, links), 0) == slot, 1.0, 0.0).astype(bf16)
    columns[0:channels, :] = dot(grid()[...], repeat).astype(bf16)
    columns[width - EXTRA : width, :] = extra[...].astype(bf16)
    store(0, dot(select, columns[...], 1, 1).astype(bf16))


def side_kernel(loads, store, pieces, turned, table):
    features, embed, edge_first, start, link_receiver, update_start, lists = loads
    owned, width = start.target.shape
    edges = features.target.shape[1]
    degree = edges // owned
    devices, slots = lists.target.shape[1:]
    pieces[...] = jnp.zeros_like(pieces)
    turned[...] = jnp.zeros_like(turned)
    table[...] = jnp.zeros_like(table)
    store_pieces(pieces, features()[...], LEFT_ORDER)
    turned[:, 0:EXTRA] = jnp.transpose(pieces[...])
    store_pieces(table, embed()[...], RIGHT_ORDER)
    matrix = table[...].astype(bf16)
    for j in range(degree):
        left = turned[pl.ds(j, owned, stride=degree), :].astype(bf16)
        edge_state = normalize(silu(dot(left, matrix))).astype(bf16)
        store(0, edge_state, j)
        store(1, dot(edge_state, edge_first()[...]).astype(bf16), j)
    store(2, dot(start()[...], link_receiver()[...]).astype(bf16))
    store(3, dot(start()[...], update_start()[...]))
    lists = lists()[0]
    rows = devices * slots
    row = iota((rows, 1), 0)
    picks = jnp.where(iota((rows, devices), 1) == row // slots, 1.0, 0.0).astype(bf16)
    high = dot(picks, (lists >> 4).astype(f32).astype(bf16))
    low = dot(picks, (lists & 15).astype(f32).astype(bf16))
    chosen = jnp.where(iota((rows, slots), 1) == row % slots, high * 16.0 + low, 0.0)
    column = jnp.sum(chosen, axis=1, keepdims=True).astype(jnp.int32)
    store(4, jnp.where(iota((rows, owned), 1) == column, 1.0, 0.0).astype(bf16))


def update(state, summand, second, gain):
    hidden = silu(summand).astype(bf16)
    return (state.astype(f32) + gain * normalize(dot(hidden, second))).astype(bf16)


def send(store, base, state, sender, select):
    sent = dot(state, sender).astype(bf16)
    store(base, dot(select, sent).astype(bf16))
    store(base + 1, sent)


def link_kernel(loads, store, first, table, messages, hidden, edge_state, picks):
    (
        terms,
        embed_first,
        link_embed,
        embed_second,
        link_sender,
        link_edge,
        receiver,
        link_second,
        base,
        update_first,
        update_second,
        gain,
        start,
        sender_first,
        select,
    ) = loads
    owned, width = start.target.shape
    slots = terms.target.shape[0]
    channels = embed_first.target.shape[0]
    tail = table.shape[0]
    lanes = iota((8, tail), 1)
    weights = jnp.where(
        lanes == tail - EXTRA + 24, 16.0, jnp.where(lanes == tail - EXTRA + 25, 1.0, 0.0)
    ).astype(bf16)
    chunks = [slice(begin, begin + 128) for begin in range(0, slots, 128)]

    def each(values, function):
        parts = [values[i : i + CHUNK, :] for i in range(0, values.shape[0], CHUNK)]
        return jnp.concatenate([function(part).astype(bf16) for part in parts], axis=0)

    table[...] = jnp.zeros_like(table)
    first[channels // 16 * 16 :, :] = jnp.zeros((width - channels // 16 * 16, width), bf16)
    first[0:channels, :] = embed_first()[...]
    store_pieces(table, link_embed()[...], RIGHT_ORDER, tail - EXTRA)
    matrix = table[...].astype(bf16)
    terms = terms()
    for rows in chunks:
        hidden[rows, :] = each(dot(terms[rows, :], first[...]), silu)
        extra = terms[rows, width - tail :]
        edge_state[rows, :] = each(dot(extra, matrix), lambda x: normalize(silu(x)))
        parts = extra.astype(f32)
        node = (
            parts[:, tail - EXTRA + 24 : tail - EXTRA + 25] * 16.0
            + parts[:, tail - EXTRA + 25 : tail - EXTRA + 26]
        ).astype(jnp.int32)
        pick = jnp.where(iota((rows.stop - rows.start, owned), 1) == node - 1, 1.0, 0.0)
        picks[rows, :] = pick.astype(bf16)
    nodes = dot(weights, terms[:, width - tail :], 1, 1)[0:1, :].astype(jnp.int32)
    collect = jnp.where(iota((owned, slots), 0) == nodes - 1, 1.0, 0.0).astype(bf16)
    for load in (embed_second, link_sender, link_edge, receiver, link_second):
        load()
    for rows in chunks:
        hidden[rows, :] = each(dot(hidden[rows, :], embed_second()[...]), normalize)
    for rows in chunks:
        sender = dot(hidden[rows, :], link_sender()[...]).astype(bf16).astype(f32)
        link_terms = (sender + dot(edge_state[rows, :], link_edge()[...])).astype(bf16)
        summand = link_terms.astype(f32) + dot(picks[rows, :], receiver()[...])
        hidden[rows, :] = each(summand, silu)
    for rows in chunks:
        messages[rows, :] = each(dot(hidden[rows, :], link_second()[...]), normalize)
    for load in (base, update_first, update_second, gain, start, sender_first, select):
        load()
    summed = dot(collect, messages[...]).astype(bf16)
    summand = base()[...] + dot(summed, update_first()[...])
    state = update(start()[...], summand, update_second()[...], gain()[0:1, :])
    store(0, state)
    send(store, 1, state, sender_first()[...], select()[...])


def local_kernel(step, last, loads, store):
    senders, state, receiver_first, sent = loads[:4]
    parts = loads[5 if step else 4]
    degree, owned = senders.target.shape
    columns = jnp.transpose(senders()[...].astype(f32)).astype(jnp.int32)
    kept = dot(state()[...], receiver_first()[...]).astype(bf16).astype(f32)
    for j in range(degree):
        local = jnp.where(iota((owned, owned), 1) == columns[:, j : j + 1], 1.0, 0.0)
        part = parts[j]()[...]
        if step:
            edge_state = (part.astype(f32) + loads[6][j]()[...].astype(f32)).astype(bf16)
            if not last:
                store(1, edge_state, j)
            part = dot(edge_state, loads[4]()[...])
        part = dot(local.astype(bf16), sent()[...]) + part.astype(f32)
        store(0, (part + kept).astype(bf16), j)


def edge_kernel(step, last, loads, store, summands, hiddens, results, total):
    senders, incoming, second, sums = loads[:4]
    (state, state_first, summed_first, update_second, gain) = loads[4:9]
    degree, owned = senders.target.shape
    rows = incoming.target.shape[0]
    columns = jnp.transpose((senders()[...] - owned).astype(f32)).astype(jnp.int32)

    def lead(j):
        pick = jnp.where(iota((owned, rows), 1) == columns[:, j : j + 1], 1.0, 0.0)
        summands[j % 2] = dot(pick.astype(bf16), incoming()[...])

    def middle(j):
        if j in (0, 2):
            for load in sums[j : 2 if j == 0 else degree]:
                load()
        part = sums[j].target
        for begin in range(0, owned, CHUNK):
            some = slice(begin, begin + CHUNK)
            summand = part[some, :].astype(f32) + summands[j % 2, some, :]
            hiddens[j % 2, some, :] = silu16(summand)
        results[j % 2] = dot(hiddens[j % 2], second()[...])

    def tail(j):
        def fill(target):
            for begin in range(0, owned, CHUNK):
                some = slice(begin, begin + CHUNK)
                message = normalize(results[j % 2, some, :]).astype(bf16)
                if target is not None:
                    target[some, :] = message
                message = message.astype(f32)
                total[some, :] = message if j == 0 else total[some, :] + message

        if last:
            fill(None)
        else:
            store(3, fill, j, j % 4 != 3)

    lead(0)
    middle(0)
    for j in range(degree):
        if j + 1 < degree:
            lead(j + 1)
            middle(j + 1)
        tail(j)
    summand = dot(state()[...], state_first()[...]) + dot(
        total[...].astype(bf16), summed_first()[...]
    )
    state = update(
        state()[...], summand, update_second()[...], gain()[step + 1 : step + 2, :]
    )
    store(0, state)
    if not last:
        sender_first, select = loads[9:]
        send(store, 1, state, sender_first()[...], select()[...])


def body(
    grid_inputs,
    link_features,
    link_partition,
    link_node,
    mesh_start,
    edge_features,
    edge_senders,
    halo_lists,
    embed_first,
    embed_second,
    link_embed,
    link_first,
    link_second,
    update_first,
    update_second,
    edge_embed,
    process_first,
    process_second,
    process_update_first,
    process_update_second,
    update_gain,
):
    owned, width = mesh_start.shape
    devices = lax.axis_size("rows")
    cells = grid_inputs.shape[1]
    links = cells * link_partition.shape[1]
    slots = 2 * links
    degree = edge_senders.shape[1]
    edges = owned * degree
    halo_slots = halo_lists.shape[2]
    halo_rows = devices * halo_slots
    senders = edge_senders.T

    def exchange(values):
        values = values.reshape(devices, -1, width)
        return lax.all_to_all(values, "rows", split_axis=0, concat_axis=0, tiled=True).reshape(
            -1, width
        )

    sending = [((halo_rows, width), bf16, 1), ((owned, width), bf16, 1)]
    (packed,) = run(
        functools.partial(pack_kernel, devices),
        "pack",
        [((slots, width), bf16, 1)],
        (grid_inputs, link_features, link_partition.T, link_node.T),
        [pltpu.VMEM((width, links), bf16), pltpu.VMEM((EXTRA, links), f32)],
    )
    terms = exchange(packed)
    edge_state, parts, receiver, base, select = run(
        side_kernel,
        "side",
        [
            ((degree, owned, width), bf16, degree),
            ((degree, owned, width), bf16, degree),
            ((owned, width), bf16, 1),
            ((owned, width), f32, 1),
            ((halo_rows, owned), bf16, 1),
        ],
        (
            edge_features,
            edge_embed,
            (process_first, rows_of(2 * width, 3 * width, 0), 1),
            mesh_start,
            (link_first, rows_of(width, 2 * width), 1),
            (update_first, rows_of(0, width), 1),
            halo_lists,
        ),
        [
            pltpu.VMEM((EXTRA, edges), f32),
            pltpu.VMEM((edges, 128), f32),
            pltpu.VMEM((128, width), f32),
        ],
        flops=10**10,
    )
    state, outgoing, sent = run(
        link_kernel,
        "link",
        [((owned, width), bf16, 1)] + sending,
        (
            terms,
            embed_first,
            link_embed,
            embed_second,
            (link_first, rows_of(0, width), 1),
            (link_first, rows_of(2 * width, 3 * width), 1),
            receiver,
            link_second,
            base,
            (update_first, rows_of(width, 2 * width), 1),
            update_second,
            update_gain,
            mesh_start,
            (process_first, rows_of(0, width, 0), 1),
            select,
        ),
        [
            pltpu.VMEM((width, width), bf16),
            pltpu.VMEM((128, width), f32),
            pltpu.VMEM((slots, width), bf16),
            pltpu.VMEM((slots, width), bf16),
            pltpu.VMEM((slots, width), bf16),
            pltpu.VMEM((slots, owned), bf16),
        ],
    )
    steps = process_first.shape[0]
    for step in range(steps):
        last = step + 1 == steps
        incoming = exchange(outgoing)
        extra = []
        if step:
            extra = [(process_first, rows_of(2 * width, 3 * width, step), 1)]
            parts = edge_state
        (sums, *kept) = run(
            functools.partial(local_kernel, step, last),
            f"local{step}",
            [((degree, owned, width), bf16, degree)] * (1 if last or step == 0 else 2),
            [
                senders,
                state,
                (process_first, rows_of(width, 2 * width, step), 1),
                sent,
            ]
            + extra
            + [(parts, piece_of, degree)]
            + ([(message, piece_of, degree)] if step else []),
            flops=10**10,
        )
        if kept:
            edge_state = kept[0]
        outs = [((owned, width), bf16, 1)]
        extra = []
        if not last:
            outs += sending + [((degree, owned, width), bf16, degree)]
            extra = [(process_first, rows_of(0, width, step + 1), 1), select]
        results = run(
            functools.partial(edge_kernel, step, last),
            f"edge{step}",
            outs,
            [
                senders,
                incoming,
                (process_second, fixed(step), 1),
                (sums, piece_of, degree),
                state,
                (process_update_first, rows_of(0, width, step), 1),
                (process_update_first, rows_of(width, 2 * width, step), 1),
                (process_update_second, fixed(step), 1),
                update_gain,
            ]
            + extra,
            [
                pltpu.VMEM((2, owned, width), f32),
                pltpu.VMEM((2, owned, width), bf16),
                pltpu.VMEM((2, owned, width), f32),
                pltpu.VMEM((owned, width), f32),
            ],
        )
        if last:
            return results[0]
        state, outgoing, sent, message = results


def solution(mesh):
    return jax.shard_map(
        body,
        mesh=mesh,
        in_specs=(
            P(None, ("groups", "rows")),
            P(None, "rows"),
            P("rows", None),
            P("rows", None),
            P("rows", None),
            P(None, "rows"),
            P("rows", None),
            P("rows", None, None),
        )
        + (P(),) * 13,
        out_specs=P(("groups", "rows"), None),
        check_vma=False,
    )
```

```python
import functools

import jax
import jax.numpy as jnp
from jax import lax
from jax.experimental import pallas as pl
from jax.experimental.pallas import tpu as pltpu
from jax.sharding import PartitionSpec as P

epsilon = 1e-05
f32 = jnp.float32
bf16 = jnp.bfloat16
MIB = 2**20
EXTRA = 32
CHUNK = 32


def dot(left, right, left_dim=1, right_dim=0):
    return lax.dot_general(
        left, right, (((left_dim,), (right_dim,)), ((), ())), preferred_element_type=f32
    )


def silu(values):
    half = 0.5 * values
    return half + half * jnp.tanh(half)


def normalize(values):
    scale = 1.0 / values.shape[-1]
    center = values - jnp.sum(values, axis=-1, keepdims=True) * scale
    spread = jnp.sum(center * center, axis=-1, keepdims=True) * scale
    return center * lax.rsqrt(spread + epsilon)


def iota(shape, dim):
    return lax.broadcasted_iota(jnp.int32, shape, dim)


def split3(values):
    high = values.astype(bf16).astype(f32)
    rest = values - high
    middle = rest.astype(bf16).astype(f32)
    return high, middle, rest - middle


def store_pieces(ref, values, order, base=0):
    pieces = split3(values)
    rows = values.shape[0]
    for place, piece in enumerate(order):
        ref[base + place * rows : base + (place + 1) * rows, :] = pieces[piece]


LEFT_ORDER = (0, 0, 0, 1, 1, 2)
RIGHT_ORDER = (0, 1, 2, 0, 1, 0)


class Load:
    def __init__(self, source, target, semaphore):
        self.copy = pltpu.make_async_copy(source, target, semaphore)
        self.target = target
        self.waiting = True
        self.copy.start()

    def __call__(self):
        if self.waiting:
            self.copy.wait()
            self.waiting = False
        return self.target


def run(kernel, name, outs, args, scratch=(), flops=10**9):
    plans = []
    for arg in args:
        if not isinstance(arg, tuple):
            arg = (arg, None, 1)
        array, take, count = arg
        if take is None:
            shape = array.shape
        else:
            shape = jax.eval_shape(lambda x, take=take: take(x, 0), array).shape
        plans.append((array, take, count, shape))
    n_in, n_out = len(plans), len(outs)
    starts, total = [], 0
    for plan in plans:
        starts.append(total)
        total += plan[2]
    out_starts, out_total = [], 0
    for out in outs:
        out_starts.append(out_total)
        out_total += out[2]
    start_order = [(i, 0) for i in range(n_in) if plans[i][2] == 1]
    split = [i for i in range(n_in) if plans[i][2] > 1]
    if split:
        at = len([i for i in range(split[0]) if plans[i][2] == 1])
        pieces = [(i, piece) for piece in range(plans[split[0]][2]) for i in split]
        start_order[at:at] = pieces
    arrays, places = [], []
    for plan in plans:
        known = [i for i, array in enumerate(arrays) if array is plan[0]]
        if known:
            places.append(known[0])
        else:
            places.append(len(arrays))
            arrays.append(plan[0])

    def whole(*refs):
        ins = refs[: len(arrays)]
        out_refs = refs[len(arrays) : len(arrays) + n_out]
        rest = refs[len(arrays) + n_out :]
        in_vmem, out_vmem = rest[:n_in], rest[n_in : n_in + n_out]
        in_sems, out_sems = rest[n_in + n_out : n_in + n_out + 2]
        loads = [[None] * count for _, _, count, _ in plans]
        for i, piece in start_order:
            _, take, count, _ = plans[i]
            source = ins[places[i]]
            view = source if take is None else take(source.at, piece)
            target = in_vmem[i] if count == 1 else in_vmem[i].at[piece]
            loads[i][piece] = Load(view, target, in_sems.at[starts[i] + piece])
        loads = [pieces if len(pieces) > 1 else pieces[0] for pieces in loads]
        pending, waiting = [], []

        def store(i, value, piece=None, hold=False):
            target = out_vmem[i] if piece is None else out_vmem[i].at[piece]
            out = out_refs[i] if piece is None else out_refs[i].at[piece]
            if callable(value):
                value(target)
            else:
                target[...] = value
            copy = pltpu.make_async_copy(target, out, out_sems.at[out_starts[i] + (piece or 0)])
            waiting.append(copy)
            if not hold:
                flush()

        def flush():
            for copy in waiting:
                copy.start()
            pending.extend(waiting)
            waiting.clear()

        store.flush = flush
        kernel(loads, store, *rest[n_in + n_out + 2 :])
        for pieces in loads:
            for load in pieces if isinstance(pieces, list) else [pieces]:
                load()
        flush()
        for copy in pending:
            copy.wait()

    spec = pl.BlockSpec(memory_space=pltpu.HBM)
    in_scratch = [
        pltpu.VMEM(shape if count == 1 else (count,) + shape, array.dtype)
        for array, _, count, shape in plans
    ]
    return pl.pallas_call(
        whole,
        out_shape=[jax.ShapeDtypeStruct(out[0], out[1]) for out in outs],
        in_specs=[spec] * len(arrays),
        out_specs=[spec] * n_out,
        scratch_shapes=in_scratch
        + [pltpu.VMEM(out[0], out[1]) for out in outs]
        + [pltpu.SemaphoreType.DMA((total,)), pltpu.SemaphoreType.DMA((out_total,))]
        + list(scratch),
        compiler_params=pltpu.CompilerParams(vmem_limit_bytes=60 * MIB),
        cost_estimate=pl.CostEstimate(flops=flops, bytes_accessed=8 * MIB, transcendentals=0),
        name=name,
    )(*arrays)


def rows_of(start, stop, step=None):
    if step is None:
        return lambda ref, i: ref[start:stop]
    return lambda ref, i: ref[step, start:stop]


def piece_of(ref, i):
    return ref[i]


def fixed(step):
    return lambda ref, i: ref[step]


def pack_kernel(devices, loads, store, columns, extra):
    grid, features, partition, node = loads
    channels, cells = grid.target.shape
    fanout = partition.target.shape[0]
    links = cells * fanout
    width = columns.shape[0]
    slots = 2 * links
    capacity = slots // devices
    place = iota((cells, links), 1)
    repeat = jnp.where(
        functools.reduce(
            jnp.logical_or,
            [place == iota((cells, links), 0) + k * cells for k in range(fanout)],
        ),
        1.0,
        0.0,
    ).astype(bf16)
    order = iota((links, links), 0)
    turn = iota((links, links), 1)
    upper = jnp.where(order <= turn, 1.0, 0.0).astype(bf16)
    spread = jnp.where(order == turn % cells * fanout + turn // cells, 1.0, 0.0).astype(bf16)
    extra[...] = jnp.zeros_like(extra)
    columns[width - EXTRA - 16 : width - EXTRA, :] = jnp.zeros((16, links), bf16)
    store_pieces(extra, features()[...], LEFT_ORDER)
    target = jnp.concatenate([partition()[k : k + 1, :] for k in range(fanout)], axis=1)
    nodes = jnp.concatenate([node()[k : k + 1, :] for k in range(fanout)], axis=1) + 1
    extra[...] = dot(extra[...].astype(bf16), spread)
    extra[24:25, :] = (nodes >> 4).astype(f32)
    extra[25:26, :] = (nodes & 15).astype(f32)
    matches = jnp.where(iota((devices, links), 0) == target, 1.0, 0.0)
    counts = dot(matches.astype(bf16), upper)
    rank = jnp.sum(counts * matches, axis=0, keepdims=True).astype(jnp.int32) - 1
    slot = target * capacity + rank
    select = jnp.where(iota((slots, links), 0) == slot, 1.0, 0.0).astype(bf16)
    columns[0:channels, :] = dot(grid()[...], repeat).astype(bf16)
    columns[width - EXTRA : width, :] = extra[...].astype(bf16)
    store(0, dot(select, columns[...], 1, 1).astype(bf16))


def side_kernel(sizes, gather, loads, store, pieces, turned, table):
    features, embed, edge_first, start, link_receiver, update_start, lists = loads
    owned, width = start.target.shape
    edges = features.target.shape[1]
    degree = edges // owned
    devices, far, slots = sizes
    pieces[...] = jnp.zeros_like(pieces)
    turned[...] = jnp.zeros_like(turned)
    table[...] = jnp.zeros_like(table)
    store_pieces(pieces, features()[...], LEFT_ORDER)
    turned[:, 0:EXTRA] = jnp.transpose(pieces[...])
    store_pieces(table, embed()[...], RIGHT_ORDER)
    matrix = table[...].astype(bf16)
    for j in range(degree):
        left = turned[pl.ds(j, owned, stride=degree), :].astype(bf16)
        edge_state = normalize(silu(dot(left, matrix))).astype(bf16)
        store(0, edge_state, j)
        store(1, dot(edge_state, edge_first()[...]).astype(bf16), j)
    store(2, dot(start()[...], link_receiver()[...]).astype(bf16))
    store(3, dot(start()[...], update_start()[...]))
    lists = lists()[0]
    rows = devices * far + (2 * slots if gather else 0)
    reader, place = outgoing_slots(rows, devices, far, slots)
    picks = jnp.where(iota((rows, devices), 1) == reader, 1.0, 0.0).astype(bf16)
    high = dot(picks, (lists >> 4).astype(f32).astype(bf16))
    low = dot(picks, (lists & 15).astype(f32).astype(bf16))
    chosen = jnp.where(iota((rows, slots), 1) == place, high * 16.0 + low, 0.0)
    column = jnp.sum(chosen, axis=1, keepdims=True).astype(jnp.int32)
    store(4, jnp.where(iota((rows, owned), 1) == column, 1.0, 0.0).astype(bf16))


def neighbours(devices):
    me = lax.axis_index("rows")
    return (me + devices - 1) % devices, (me + 1) % devices


def outgoing_slots(rows, devices, far, slots):
    before, after = neighbours(devices)
    row = iota((rows, 1), 0)
    near = row - devices * far
    reader = jnp.where(near < 0, row // far, jnp.where(near < slots, after, before))
    return reader, jnp.where(near < 0, row % far, near % slots)


def gathered_rows(rows, devices, far, slots):
    me = lax.axis_index("rows")
    before, after = neighbours(devices)
    each = devices * far + 2 * slots
    row = iota((rows, 1), 0)
    near = row - devices * far
    from_far = row // far * each + me * far + row % far
    from_before = before * each + devices * far + near
    from_after = after * each + devices * far + near
    found = jnp.where(near < 0, from_far, jnp.where(near < slots, from_before, from_after))
    return jnp.where(near < 2 * slots, found, -1)


def halo_index(senders, owned, devices, far, slots):
    if far == slots:
        return senders - owned
    before, after = neighbours(devices)
    halo = senders - owned
    owner = halo // slots
    place = halo % slots
    index = owner * far + place
    index = jnp.where(owner == before, devices * far + place, index)
    index = jnp.where(owner == after, devices * far + slots + place, index)
    return jnp.where(halo < 0, -1, index)


def update(state, summand, second, gain):
    hidden = silu(summand).astype(bf16)
    return (state.astype(f32) + gain * normalize(dot(hidden, second))).astype(bf16)


def send(store, base, state, sender, select):
    sent = dot(state, sender).astype(bf16)
    store(base, dot(select, sent).astype(bf16))
    store(base + 1, sent)


def link_kernel(loads, store, first, table, messages, hidden, edge_state, picks):
    (
        terms,
        embed_first,
        link_embed,
        embed_second,
        link_sender,
        link_edge,
        receiver,
        link_second,
        base,
        update_first,
        update_second,
        gain,
        start,
        sender_first,
        select,
    ) = loads
    owned, width = start.target.shape
    slots = terms.target.shape[0]
    channels = embed_first.target.shape[0]
    tail = table.shape[0]
    lanes = iota((8, tail), 1)
    weights = jnp.where(
        lanes == tail - EXTRA + 24, 16.0, jnp.where(lanes == tail - EXTRA + 25, 1.0, 0.0)
    ).astype(bf16)
    chunks = [slice(begin, begin + 128) for begin in range(0, slots, 128)]

    def each(values, function):
        parts = [values[i : i + CHUNK, :] for i in range(0, values.shape[0], CHUNK)]
        return jnp.concatenate([function(part).astype(bf16) for part in parts], axis=0)

    table[...] = jnp.zeros_like(table)
    first[channels // 16 * 16 :, :] = jnp.zeros((width - channels // 16 * 16, width), bf16)
    first[0:channels, :] = embed_first()[...]
    store_pieces(table, link_embed()[...], RIGHT_ORDER, tail - EXTRA)
    matrix = table[...].astype(bf16)
    terms = terms()
    for rows in chunks:
        hidden[rows, :] = each(dot(terms[rows, :], first[...]), silu)
        extra = terms[rows, width - tail :]
        edge_state[rows, :] = each(dot(extra, matrix), lambda x: normalize(silu(x)))
        parts = extra.astype(f32)
        node = (
            parts[:, tail - EXTRA + 24 : tail - EXTRA + 25] * 16.0
            + parts[:, tail - EXTRA + 25 : tail - EXTRA + 26]
        ).astype(jnp.int32)
        pick = jnp.where(iota((rows.stop - rows.start, owned), 1) == node - 1, 1.0, 0.0)
        picks[rows, :] = pick.astype(bf16)
    nodes = dot(weights, terms[:, width - tail :], 1, 1)[0:1, :].astype(jnp.int32)
    collect = jnp.where(iota((owned, slots), 0) == nodes - 1, 1.0, 0.0).astype(bf16)
    for load in (embed_second, link_sender, link_edge, receiver, link_second):
        load()
    for rows in chunks:
        hidden[rows, :] = each(dot(hidden[rows, :], embed_second()[...]), normalize)
    for rows in chunks:
        sender = dot(hidden[rows, :], link_sender()[...]).astype(bf16).astype(f32)
        link_terms = (sender + dot(edge_state[rows, :], link_edge()[...])).astype(bf16)
        summand = link_terms.astype(f32) + dot(picks[rows, :], receiver()[...])
        hidden[rows, :] = each(summand, silu)
    for rows in chunks:
        messages[rows, :] = each(dot(hidden[rows, :], link_second()[...]), normalize)
    for load in (base, update_first, update_second, gain, start, sender_first, select):
        load()
    summed = dot(collect, messages[...]).astype(bf16)
    summand = base()[...] + dot(summed, update_first()[...])
    state = update(start()[...], summand, update_second()[...], gain()[0:1, :])
    store(0, state)
    send(store, 1, state, sender_first()[...], select()[...])


def local_kernel(step, last, loads, store):
    senders, state, receiver_first, sent = loads[:4]
    parts = loads[5 if step else 4]
    degree, owned = senders.target.shape
    columns = jnp.transpose(senders()[...].astype(f32)).astype(jnp.int32)
    kept = dot(state()[...], receiver_first()[...]).astype(bf16).astype(f32)
    for j in range(degree):
        local = jnp.where(iota((owned, owned), 1) == columns[:, j : j + 1], 1.0, 0.0)
        part = parts[j]()[...]
        if step:
            edge_state = (part.astype(f32) + loads[6][j]()[...].astype(f32)).astype(bf16)
            if not last:
                store(1, edge_state, j)
            part = dot(edge_state, loads[4]()[...])
        part = dot(local.astype(bf16), sent()[...]) + part.astype(f32)
        store(0, (part + kept).astype(bf16), j)


def edge_kernel(step, last, sizes, loads, store, summands, hiddens, results, total, table):
    senders, incoming, second, sums = loads[:4]
    (state, state_first, summed_first, update_second, gain) = loads[4:9]
    degree, owned = senders.target.shape
    devices, far, slots = sizes
    rows = table.shape[0]
    index = halo_index(senders()[...], owned, *sizes)
    columns = jnp.transpose(index.astype(f32)).astype(jnp.int32)
    count = incoming.target.shape[0]
    if count == rows:
        table[...] = incoming()[...]
    else:
        found = gathered_rows(rows, *sizes)
        collect = jnp.where(iota((rows, count), 1) == found, 1.0, 0.0).astype(bf16)
        table[...] = dot(collect, incoming()[...]).astype(bf16)

    def lead(j):
        pick = jnp.where(iota((owned, rows), 1) == columns[:, j : j + 1], 1.0, 0.0)
        summands[j % 2] = dot(pick.astype(bf16), table[...])

    def middle(j):
        part = sums[j]()
        for begin in range(0, owned, CHUNK):
            some = slice(begin, begin + CHUNK)
            summand = part[some, :].astype(f32) + summands[j % 2, some, :]
            hiddens[j % 2, some, :] = silu(summand).astype(bf16)
        results[j % 2] = dot(hiddens[j % 2], second()[...])

    def tail(j):
        def fill(target):
            for begin in range(0, owned, CHUNK):
                some = slice(begin, begin + CHUNK)
                message = normalize(results[j % 2, some, :]).astype(bf16)
                if target is not None:
                    target[some, :] = message
                message = message.astype(f32)
                total[some, :] = message if j == 0 else total[some, :] + message

        if last:
            fill(None)
        else:
            store(3, fill, j)

    lead(0)
    middle(0)
    for j in range(degree):
        if j + 1 < degree:
            lead(j + 1)
            middle(j + 1)
        tail(j)
    summand = dot(state()[...], state_first()[...]) + dot(
        total[...].astype(bf16), summed_first()[...]
    )
    state = update(
        state()[...], summand, update_second()[...], gain()[step + 1 : step + 2, :]
    )
    store(0, state)
    if not last:
        sender_first, select = loads[9:]
        send(store, 1, state, sender_first()[...], select()[...])


def body(
    grid_inputs,
    link_features,
    link_partition,
    link_node,
    mesh_start,
    edge_features,
    edge_senders,
    halo_lists,
    embed_first,
    embed_second,
    link_embed,
    link_first,
    link_second,
    update_first,
    update_second,
    edge_embed,
    process_first,
    process_second,
    process_update_first,
    process_update_second,
    update_gain,
):
    owned, width = mesh_start.shape
    devices = lax.axis_size("rows")
    cells = grid_inputs.shape[1]
    links = cells * link_partition.shape[1]
    slots = 2 * links
    degree = edge_senders.shape[1]
    edges = owned * degree
    halo_slots = halo_lists.shape[2]
    gather = devices <= 32
    far = 4 if gather else halo_slots
    sizes = (devices, far, halo_slots)
    halo_rows = devices * far + (2 * halo_slots if gather else 0)
    senders = edge_senders.T

    def exchange(values):
        values = values.reshape(devices, -1, width)
        return lax.all_to_all(values, "rows", split_axis=0, concat_axis=0, tiled=True).reshape(
            -1, width
        )

    sending = [((halo_rows, width), bf16, 1), ((owned, width), bf16, 1)]
    (packed,) = run(
        functools.partial(pack_kernel, devices),
        "pack",
        [((slots, width), bf16, 1)],
        (grid_inputs, link_features, link_partition.T, link_node.T),
        [pltpu.VMEM((width, links), bf16), pltpu.VMEM((EXTRA, links), f32)],
    )
    terms = exchange(packed)
    edge_state, parts, receiver, base, select = run(
        functools.partial(side_kernel, sizes, gather),
        "side",
        [
            ((degree, owned, width), bf16, degree),
            ((degree, owned, width), bf16, degree),
            ((owned, width), bf16, 1),
            ((owned, width), f32, 1),
            ((halo_rows, owned), bf16, 1),
        ],
        (
            edge_features,
            edge_embed,
            (process_first, rows_of(2 * width, 3 * width, 0), 1),
            mesh_start,
            (link_first, rows_of(width, 2 * width), 1),
            (update_first, rows_of(0, width), 1),
            halo_lists,
        ),
        [
            pltpu.VMEM((EXTRA, edges), f32),
            pltpu.VMEM((edges, 128), f32),
            pltpu.VMEM((128, width), f32),
        ],
        flops=10**10,
    )
    state, outgoing, sent = run(
        link_kernel,
        "link",
        [((owned, width), bf16, 1)] + sending,
        (
            terms,
            embed_first,
            link_embed,
            embed_second,
            (link_first, rows_of(0, width), 1),
            (link_first, rows_of(2 * width, 3 * width), 1),
            receiver,
            link_second,
            base,
            (update_first, rows_of(width, 2 * width), 1),
            update_second,
            update_gain,
            mesh_start,
            (process_first, rows_of(0, width, 0), 1),
            select,
        ),
        [
            pltpu.VMEM((width, width), bf16),
            pltpu.VMEM((128, width), f32),
            pltpu.VMEM((slots, width), bf16),
            pltpu.VMEM((slots, width), bf16),
            pltpu.VMEM((slots, width), bf16),
            pltpu.VMEM((slots, owned), bf16),
        ],
    )
    steps = process_first.shape[0]
    for step in range(steps):
        last = step + 1 == steps
        if gather:
            incoming = lax.all_gather(outgoing, "rows", axis=0, tiled=True)
        else:
            incoming = exchange(outgoing)
        extra = []
        if step:
            extra = [(process_first, rows_of(2 * width, 3 * width, step), 1)]
            parts = edge_state
        (sums, *kept) = run(
            functools.partial(local_kernel, step, last),
            f"local{step}",
            [((degree, owned, width), bf16, degree)] * (1 if last or step == 0 else 2),
            [
                senders,
                state,
                (process_first, rows_of(width, 2 * width, step), 1),
                sent,
            ]
            + extra
            + [(parts, piece_of, degree)]
            + ([(message, piece_of, degree)] if step else []),
            flops=10**10,
        )
        if kept:
            edge_state = kept[0]
        outs = [((owned, width), bf16, 1)]
        extra = []
        if not last:
            outs += sending + [((degree, owned, width), bf16, degree)]
            extra = [(process_first, rows_of(0, width, step + 1), 1), select]
        results = run(
            functools.partial(edge_kernel, step, last, sizes),
            f"edge{step}",
            outs,
            [
                senders,
                incoming,
                (process_second, fixed(step), 1),
                (sums, piece_of, degree),
                state,
                (process_update_first, rows_of(0, width, step), 1),
                (process_update_first, rows_of(width, 2 * width, step), 1),
                (process_update_second, fixed(step), 1),
                update_gain,
            ]
            + extra,
            [
                pltpu.VMEM((2, owned, width), f32),
                pltpu.VMEM((2, owned, width), bf16),
                pltpu.VMEM((2, owned, width), f32),
                pltpu.VMEM((owned, width), f32),
                pltpu.VMEM((-(-halo_rows // 128) * 128, width), bf16),
            ],
        )
        if last:
            return results[0]
        state, outgoing, sent, message = results


def solution(mesh):
    return jax.shard_map(
        body,
        mesh=mesh,
        in_specs=(
            P(None, ("groups", "rows")),
            P(None, "rows"),
            P("rows", None),
            P("rows", None),
            P("rows", None),
            P(None, "rows"),
            P("rows", None),
            P("rows", None, None),
        )
        + (P(),) * 13,
        out_specs=P(("groups", "rows"), None),
        check_vma=False,
    )
```

```python
import functools

import jax
import jax.numpy as jnp
from jax import lax
from jax.experimental import pallas as pl
from jax.experimental.pallas import tpu as pltpu
from jax.sharding import PartitionSpec as P

epsilon = 1e-05
f32 = jnp.float32
bf16 = jnp.bfloat16
MIB = 2**20
EXTRA = 32
CHUNK = 32


def dot(left, right, left_dim=1, right_dim=0):
    return lax.dot_general(
        left, right, (((left_dim,), (right_dim,)), ((), ())), preferred_element_type=f32
    )


def silu(values):
    half = 0.5 * values
    return half + half * jnp.tanh(half)


def normalize(values):
    scale = 1.0 / values.shape[-1]
    center = values - jnp.sum(values, axis=-1, keepdims=True) * scale
    spread = jnp.sum(center * center, axis=-1, keepdims=True) * scale
    return center * lax.rsqrt(spread + epsilon)


def each(values, function):
    parts = [values[i : i + CHUNK, :] for i in range(0, values.shape[0], CHUNK)]
    return jnp.concatenate([function(part).astype(bf16) for part in parts], axis=0)


def one_hot(columns, block, count):
    rows = slice(block * CHUNK, (block + 1) * CHUNK)
    lanes = iota((CHUNK, count), 1)
    picks = [
        jnp.where(lanes == columns[rows, j : j + 1], 1.0, 0.0).astype(bf16)
        for j in range(columns.shape[1])
    ]
    return jnp.concatenate(picks, axis=0)


def iota(shape, dim):
    return lax.broadcasted_iota(jnp.int32, shape, dim)


def split3(values):
    high = values.astype(bf16).astype(f32)
    rest = values - high
    middle = rest.astype(bf16).astype(f32)
    return high, middle, rest - middle


def store_pieces(ref, values, order, base=0):
    pieces = split3(values)
    rows = values.shape[0]
    for place, piece in enumerate(order):
        ref[base + place * rows : base + (place + 1) * rows, :] = pieces[piece]


LEFT_ORDER = (0, 0, 0, 1, 1, 2)
RIGHT_ORDER = (0, 1, 2, 0, 1, 0)


class Load:
    def __init__(self, source, target, semaphore):
        self.copy = pltpu.make_async_copy(source, target, semaphore)
        self.target = target
        self.waiting = True
        self.copy.start()

    def __call__(self):
        if self.waiting:
            self.copy.wait()
            self.waiting = False
        return self.target


def run(kernel, name, outs, args, scratch=(), flops=10**9, reuse=None):
    plans = []
    for arg in args:
        if not isinstance(arg, tuple):
            arg = (arg, None, 1)
        array, take, count = arg
        if take is None:
            shape = array.shape
        else:
            shape = jax.eval_shape(lambda x, take=take: take(x, 0), array).shape
        plans.append((array, take, count, shape))
    n_in, n_out = len(plans), len(outs)
    spare = [] if reuse is None else [plans[reuse][0]]
    starts, total = [], 0
    for plan in plans:
        starts.append(total)
        total += plan[2]
    out_starts, out_total = [], 0
    for out in outs:
        out_starts.append(out_total)
        out_total += out[2]
    start_order = [(i, 0) for i in range(n_in) if plans[i][2] == 1]
    split = [i for i in range(n_in) if plans[i][2] > 1]
    if split:
        at = len([i for i in range(split[0]) if plans[i][2] == 1])
        pieces = [(i, piece) for piece in range(plans[split[0]][2]) for i in split]
        start_order[at:at] = pieces
    arrays, places = [], []
    for plan in plans:
        known = [i for i, array in enumerate(arrays) if array is plan[0]]
        if known:
            places.append(known[0])
        else:
            places.append(len(arrays))
            arrays.append(plan[0])

    def whole(*refs):
        ins = refs[: len(arrays)]
        out_refs = refs[len(arrays) : len(arrays) + n_out]
        rest = refs[len(arrays) + n_out + len(spare) :]
        in_vmem, out_vmem = rest[:n_in], rest[n_in : n_in + n_out]
        in_sems, out_sems = rest[n_in + n_out : n_in + n_out + 2]
        loads = [[None] * count for _, _, count, _ in plans]
        for i, piece in start_order:
            _, take, count, _ = plans[i]
            source = ins[places[i]]
            view = source if take is None else take(source.at, piece)
            target = in_vmem[i] if count == 1 else in_vmem[i].at[piece]
            loads[i][piece] = Load(view, target, in_sems.at[starts[i] + piece])
        loads = [pieces if len(pieces) > 1 else pieces[0] for pieces in loads]
        pending, waiting = [], []

        def store(i, value, piece=None, hold=False):
            target = out_vmem[i] if piece is None else out_vmem[i].at[piece]
            out = out_refs[i] if piece is None else out_refs[i].at[piece]
            if callable(value):
                value(target)
            else:
                target[...] = value
            copy = pltpu.make_async_copy(target, out, out_sems.at[out_starts[i] + (piece or 0)])
            waiting.append(copy)
            if not hold:
                flush()

        def flush():
            for copy in waiting:
                copy.start()
            pending.extend(waiting)
            waiting.clear()

        store.flush = flush
        kernel(loads, store, *rest[n_in + n_out + 2 :])
        for pieces in loads:
            for load in pieces if isinstance(pieces, list) else [pieces]:
                load()
        flush()
        for copy in pending:
            copy.wait()

    spec = pl.BlockSpec(memory_space=pltpu.HBM)
    in_scratch = [
        pltpu.VMEM(shape if count == 1 else (count,) + shape, array.dtype)
        for array, _, count, shape in plans
    ]
    results = pl.pallas_call(
        whole,
        out_shape=[jax.ShapeDtypeStruct(out[0], out[1]) for out in outs]
        + [jax.ShapeDtypeStruct(array.shape, array.dtype) for array in spare],
        in_specs=[spec] * len(arrays),
        out_specs=[spec] * (n_out + len(spare)),
        input_output_aliases={places[reuse]: n_out} if spare else {},
        scratch_shapes=in_scratch
        + [pltpu.VMEM(out[0], out[1]) for out in outs]
        + [pltpu.SemaphoreType.DMA((total,)), pltpu.SemaphoreType.DMA((out_total,))]
        + list(scratch),
        compiler_params=pltpu.CompilerParams(vmem_limit_bytes=60 * MIB),
        cost_estimate=pl.CostEstimate(flops=flops, bytes_accessed=8 * MIB, transcendentals=0),
        name=name,
    )(*arrays)
    return results[:n_out]


def rows_of(start, stop, step=None):
    if step is None:
        return lambda ref, i: ref[start:stop]
    return lambda ref, i: ref[step, start:stop]


def piece_of(ref, i):
    return ref[i]


def fixed(step):
    return lambda ref, i: ref[step]


def pack_kernel(devices, loads, store, columns, extra):
    grid, features, partition, node = loads
    channels, cells = grid.target.shape
    fanout = partition.target.shape[0]
    links = cells * fanout
    width = columns.shape[0]
    slots = 2 * links
    capacity = slots // devices
    place = iota((cells, links), 1)
    repeat = jnp.where(
        functools.reduce(
            jnp.logical_or,
            [place == iota((cells, links), 0) + k * cells for k in range(fanout)],
        ),
        1.0,
        0.0,
    ).astype(bf16)
    order = iota((links, links), 0)
    turn = iota((links, links), 1)
    upper = jnp.where(order <= turn, 1.0, 0.0).astype(bf16)
    spread = jnp.where(order == turn % cells * fanout + turn // cells, 1.0, 0.0).astype(bf16)
    extra[...] = jnp.zeros_like(extra)
    columns[width - EXTRA - 16 : width - EXTRA, :] = jnp.zeros((16, links), bf16)
    store_pieces(extra, features()[...], LEFT_ORDER)
    target = jnp.concatenate([partition()[k : k + 1, :] for k in range(fanout)], axis=1)
    nodes = jnp.concatenate([node()[k : k + 1, :] for k in range(fanout)], axis=1) + 1
    extra[...] = dot(extra[...].astype(bf16), spread)
    extra[24:25, :] = (nodes >> 4).astype(f32)
    extra[25:26, :] = (nodes & 15).astype(f32)
    matches = jnp.where(iota((devices, links), 0) == target, 1.0, 0.0)
    counts = dot(matches.astype(bf16), upper)
    rank = jnp.sum(counts * matches, axis=0, keepdims=True).astype(jnp.int32) - 1
    slot = target * capacity + rank
    select = jnp.where(iota((slots, links), 0) == slot, 1.0, 0.0).astype(bf16)
    columns[0:channels, :] = dot(grid()[...], repeat).astype(bf16)
    columns[width - EXTRA : width, :] = extra[...].astype(bf16)
    store(0, dot(select, columns[...], 1, 1).astype(bf16))


def side_kernel(loads, store, pieces, turned, table):
    features, embed, edge_first, start, link_receiver, update_start, lists = loads
    owned, width = start.target.shape
    edges = features.target.shape[1]
    degree = edges // owned
    devices, slots = lists.target.shape[1:]
    pieces[...] = jnp.zeros_like(pieces)
    turned[...] = jnp.zeros_like(turned)
    table[...] = jnp.zeros_like(table)
    store_pieces(pieces, features()[...], LEFT_ORDER)
    turned[:, 0:EXTRA] = jnp.transpose(pieces[...])
    store_pieces(table, embed()[...], RIGHT_ORDER)
    matrix = table[...].astype(bf16)
    for block in range(owned // CHUNK):
        base = block * CHUNK * degree
        left = jnp.concatenate(
            [turned[pl.ds(base + j, CHUNK, stride=degree), :] for j in range(degree)], axis=0
        )
        linear = dot(left.astype(bf16), matrix)
        edge_state = each(linear, lambda x: normalize(silu(x)))
        store(0, edge_state, block)
        store(1, dot(edge_state, edge_first()[...]).astype(bf16), block)
    store(2, dot(start()[...], link_receiver()[...]).astype(bf16))
    store(3, dot(start()[...], update_start()[...]))
    lists = lists()[0]
    rows = devices * slots
    row = iota((rows, 1), 0)
    picks = jnp.where(iota((rows, devices), 1) == row // slots, 1.0, 0.0).astype(bf16)
    high = dot(picks, (lists >> 4).astype(f32).astype(bf16))
    low = dot(picks, (lists & 15).astype(f32).astype(bf16))
    chosen = jnp.where(iota((rows, slots), 1) == row % slots, high * 16.0 + low, 0.0)
    column = jnp.sum(chosen, axis=1, keepdims=True).astype(jnp.int32)
    store(4, jnp.where(iota((rows, owned), 1) == column, 1.0, 0.0).astype(bf16))


def update(state, summand, second, gain):
    hidden = silu(summand).astype(bf16)
    return (state.astype(f32) + gain * normalize(dot(hidden, second))).astype(bf16)


def send(store, base, state, sender, select):
    sent = dot(state, sender).astype(bf16)
    store(base, dot(select, sent).astype(bf16))
    store(base + 1, sent)


def link_kernel(loads, store, first, table, messages, hidden, edge_state, picks):
    (
        terms,
        embed_first,
        link_embed,
        embed_second,
        link_sender,
        link_edge,
        receiver,
        link_second,
        base,
        update_first,
        update_second,
        gain,
        start,
        sender_first,
        select,
    ) = loads
    owned, width = start.target.shape
    slots = terms.target.shape[0]
    channels = embed_first.target.shape[0]
    tail = table.shape[0]
    lanes = iota((8, tail), 1)
    weights = jnp.where(
        lanes == tail - EXTRA + 24, 16.0, jnp.where(lanes == tail - EXTRA + 25, 1.0, 0.0)
    ).astype(bf16)
    chunks = [slice(begin, begin + 128) for begin in range(0, slots, 128)]

    table[...] = jnp.zeros_like(table)
    first[channels // 16 * 16 :, :] = jnp.zeros((width - channels // 16 * 16, width), bf16)
    first[0:channels, :] = embed_first()[...]
    store_pieces(table, link_embed()[...], RIGHT_ORDER, tail - EXTRA)
    matrix = table[...].astype(bf16)
    terms = terms()
    for rows in chunks:
        hidden[rows, :] = each(dot(terms[rows, :], first[...]), silu)
        extra = terms[rows, width - tail :]
        edge_state[rows, :] = each(dot(extra, matrix), lambda x: normalize(silu(x)))
        parts = extra.astype(f32)
        node = (
            parts[:, tail - EXTRA + 24 : tail - EXTRA + 25] * 16.0
            + parts[:, tail - EXTRA + 25 : tail - EXTRA + 26]
        ).astype(jnp.int32)
        pick = jnp.where(iota((rows.stop - rows.start, owned), 1) == node - 1, 1.0, 0.0)
        picks[rows, :] = pick.astype(bf16)
    nodes = dot(weights, terms[:, width - tail :], 1, 1)[0:1, :].astype(jnp.int32)
    collect = jnp.where(iota((owned, slots), 0) == nodes - 1, 1.0, 0.0).astype(bf16)
    for load in (embed_second, link_sender, link_edge, receiver, link_second):
        load()
    for rows in chunks:
        hidden[rows, :] = each(dot(hidden[rows, :], embed_second()[...]), normalize)
    for rows in chunks:
        sender = dot(hidden[rows, :], link_sender()[...]).astype(bf16).astype(f32)
        link_terms = (sender + dot(edge_state[rows, :], link_edge()[...])).astype(bf16)
        summand = link_terms.astype(f32) + dot(picks[rows, :], receiver()[...])
        hidden[rows, :] = each(summand, silu)
    for rows in chunks:
        messages[rows, :] = each(dot(hidden[rows, :], link_second()[...]), normalize)
    for load in (base, update_first, update_second, gain, start, sender_first, select):
        load()
    summed = dot(collect, messages[...]).astype(bf16)
    summand = base()[...] + dot(summed, update_first()[...])
    state = update(start()[...], summand, update_second()[...], gain()[0:1, :])
    store(0, state)
    send(store, 1, state, sender_first()[...], select()[...])


def local_kernel(step, last, loads, store, kept):
    senders, state, receiver_first, sent = loads[:4]
    parts = loads[5 if step else 4]
    degree, owned = senders.target.shape
    columns = jnp.transpose(senders()[...].astype(f32)).astype(jnp.int32)
    kept[...] = dot(state()[...], receiver_first()[...]).astype(bf16).astype(f32)
    for block in range(owned // CHUNK):
        summand = dot(one_hot(columns, block, owned), sent()[...])
        part = parts[block]()[...]
        if step:
            message = loads[6][block]()[...]
            edge_state = (part.astype(f32) + message.astype(f32)).astype(bf16)
            if not last:
                store(1, edge_state, block)
            summand = summand + dot(edge_state, loads[4]()[...])
        receiver = kept[block * CHUNK : (block + 1) * CHUNK, :]

        def finish(j):
            rows = slice(j * CHUNK, (j + 1) * CHUNK)
            values = summand[rows, :] + receiver
            if not step:
                values = values + part[rows, :].astype(f32)
            return values.astype(bf16)

        store(0, jnp.concatenate([finish(j) for j in range(degree)], axis=0), block)


def edge_kernel(step, last, loads, store, summands, hiddens, results, total):
    senders, incoming, second, sums = loads[:4]
    (state, state_first, summed_first, update_second, gain) = loads[4:9]
    degree, owned = senders.target.shape
    blocks = owned // CHUNK
    rows = incoming.target.shape[0]
    columns = jnp.transpose((senders()[...] - owned).astype(f32)).astype(jnp.int32)

    def lead(block):
        summands[block % 2] = dot(one_hot(columns, block, rows), incoming()[...])

    def middle(block):
        part = sums[block]()
        for j in range(degree):
            some = slice(j * CHUNK, (j + 1) * CHUNK)
            summand = part[some, :].astype(f32) + summands[block % 2, some, :]
            hiddens[block % 2, some, :] = silu(summand).astype(bf16)
        results[block % 2] = dot(hiddens[block % 2], second()[...])

    def tail(block):
        def fill(target):
            added = jnp.zeros((CHUNK, total.shape[1]), f32)
            for j in range(degree):
                some = slice(j * CHUNK, (j + 1) * CHUNK)
                message = normalize(results[block % 2, some, :])
                if target is not None:
                    message = message.astype(bf16)
                    target[some, :] = message
                added = added + message.astype(f32)
            total[block * CHUNK : (block + 1) * CHUNK, :] = added.astype(bf16)

        if last:
            fill(None)
        else:
            store(3, fill, block, block % 3 != 2)

    lead(0)
    middle(0)
    for block in range(blocks):
        if block + 1 < blocks:
            lead(block + 1)
            middle(block + 1)
        tail(block)
    summand = dot(state()[...], state_first()[...]) + dot(total[...], summed_first()[...])
    state = update(
        state()[...], summand, update_second()[...], gain()[step + 1 : step + 2, :]
    )
    store(0, state)
    if not last:
        sender_first, select = loads[9:]
        send(store, 1, state, sender_first()[...], select()[...])


def body(
    grid_inputs,
    link_features,
    link_partition,
    link_node,
    mesh_start,
    edge_features,
    edge_senders,
    halo_lists,
    embed_first,
    embed_second,
    link_embed,
    link_first,
    link_second,
    update_first,
    update_second,
    edge_embed,
    process_first,
    process_second,
    process_update_first,
    process_update_second,
    update_gain,
):
    owned, width = mesh_start.shape
    devices = lax.axis_size("rows")
    cells = grid_inputs.shape[1]
    links = cells * link_partition.shape[1]
    slots = 2 * links
    degree = edge_senders.shape[1]
    edges = owned * degree
    blocks = owned // CHUNK
    edge_shape = (blocks, CHUNK * degree, width)
    halo_slots = halo_lists.shape[2]
    halo_rows = devices * halo_slots
    senders = edge_senders.T

    def exchange(values):
        values = values.reshape(devices, -1, width)
        return lax.all_to_all(values, "rows", split_axis=0, concat_axis=0, tiled=True).reshape(
            -1, width
        )

    sending = [((halo_rows, width), bf16, 1), ((owned, width), bf16, 1)]
    (packed,) = run(
        functools.partial(pack_kernel, devices),
        "pack",
        [((slots, width), bf16, 1)],
        (grid_inputs, link_features, link_partition.T, link_node.T),
        [pltpu.VMEM((width, links), bf16), pltpu.VMEM((EXTRA, links), f32)],
    )
    terms = exchange(packed)
    edge_state, parts, receiver, base, select = run(
        side_kernel,
        "side",
        [
            (edge_shape, bf16, blocks),
            (edge_shape, bf16, blocks),
            ((owned, width), bf16, 1),
            ((owned, width), f32, 1),
            ((halo_rows, owned), bf16, 1),
        ],
        (
            edge_features,
            edge_embed,
            (process_first, rows_of(2 * width, 3 * width, 0), 1),
            mesh_start,
            (link_first, rows_of(width, 2 * width), 1),
            (update_first, rows_of(0, width), 1),
            halo_lists,
        ),
        [
            pltpu.VMEM((EXTRA, edges), f32),
            pltpu.VMEM((edges, 128), f32),
            pltpu.VMEM((128, width), f32),
        ],
        flops=10**10,
    )
    state, outgoing, sent = run(
        link_kernel,
        "link",
        [((owned, width), bf16, 1)] + sending,
        (
            terms,
            embed_first,
            link_embed,
            embed_second,
            (link_first, rows_of(0, width), 1),
            (link_first, rows_of(2 * width, 3 * width), 1),
            receiver,
            link_second,
            base,
            (update_first, rows_of(width, 2 * width), 1),
            update_second,
            update_gain,
            mesh_start,
            (process_first, rows_of(0, width, 0), 1),
            select,
        ),
        [
            pltpu.VMEM((width, width), bf16),
            pltpu.VMEM((128, width), f32),
            pltpu.VMEM((slots, width), bf16),
            pltpu.VMEM((slots, width), bf16),
            pltpu.VMEM((slots, width), bf16),
            pltpu.VMEM((slots, owned), bf16),
        ],
        reuse=0,
    )
    steps = process_first.shape[0]
    for step in range(steps):
        last = step + 1 == steps
        incoming = exchange(outgoing)
        extra = []
        if step:
            extra = [(process_first, rows_of(2 * width, 3 * width, step), 1)]
            parts = edge_state
        (sums, *kept) = run(
            functools.partial(local_kernel, step, last),
            f"local{step}",
            [(edge_shape, bf16, blocks)] * (1 if last or step == 0 else 2),
            [
                senders,
                state,
                (process_first, rows_of(width, 2 * width, step), 1),
                sent,
            ]
            + extra
            + [(parts, piece_of, blocks)]
            + ([(message, piece_of, blocks)] if step else []),
            [pltpu.VMEM((owned, width), f32)],
            flops=10**10,
        )
        if kept:
            edge_state = kept[0]
        outs = [((owned, width), bf16, 1)]
        extra = []
        if not last:
            outs += sending + [(edge_shape, bf16, blocks)]
            extra = [(process_first, rows_of(0, width, step + 1), 1), select]
        results = run(
            functools.partial(edge_kernel, step, last),
            f"edge{step}",
            outs,
            [
                senders,
                incoming,
                (process_second, fixed(step), 1),
                (sums, piece_of, blocks),
                state,
                (process_update_first, rows_of(0, width, step), 1),
                (process_update_first, rows_of(width, 2 * width, step), 1),
                (process_update_second, fixed(step), 1),
                update_gain,
            ]
            + extra,
            [
                pltpu.VMEM((2,) + edge_shape[1:], f32),
                pltpu.VMEM((2,) + edge_shape[1:], bf16),
                pltpu.VMEM((2,) + edge_shape[1:], f32),
                pltpu.VMEM((owned, width), bf16),
            ],
            reuse=1,
        )
        if last:
            return results[0]
        state, outgoing, sent, message = results


def solution(mesh):
    return jax.shard_map(
        body,
        mesh=mesh,
        in_specs=(
            P(None, ("groups", "rows")),
            P(None, "rows"),
            P("rows", None),
            P("rows", None),
            P("rows", None),
            P(None, "rows"),
            P("rows", None),
            P("rows", None, None),
        )
        + (P(),) * 13,
        out_specs=P(("groups", "rows"), None),
        check_vma=False,
    )
```

```python
import functools

import jax
import jax.numpy as jnp
from jax import lax
from jax.experimental import pallas as pl
from jax.experimental.pallas import tpu as pltpu
from jax.sharding import PartitionSpec as P

epsilon = 1e-05
f32 = jnp.float32
bf16 = jnp.bfloat16
MIB = 2**20
EXTRA = 32
CHUNK = 32
EDGE_GROUP = 2
LOCAL_GROUP = 4


def dot(left, right, left_dim=1, right_dim=0):
    return lax.dot_general(
        left, right, (((left_dim,), (right_dim,)), ((), ())), preferred_element_type=f32
    )


def silu(values):
    half = 0.5 * values
    return half + half * jnp.tanh(half)


def normalize(values):
    scale = 1.0 / values.shape[-1]
    center = values - jnp.sum(values, axis=-1, keepdims=True) * scale
    spread = jnp.sum(center * center, axis=-1, keepdims=True) * scale
    return center * lax.rsqrt(spread + epsilon)


def one_hot(columns, group, count):
    lanes = iota((columns.shape[0], count), 1)
    picks = [jnp.where(lanes == columns[:, j : j + 1], 1.0, 0.0).astype(bf16) for j in group]
    return jnp.concatenate(picks, axis=0)


def groups_of(degree, size):
    return [range(begin, begin + size) for begin in range(0, degree, size)]


def iota(shape, dim):
    return lax.broadcasted_iota(jnp.int32, shape, dim)


def split3(values):
    high = values.astype(bf16).astype(f32)
    rest = values - high
    middle = rest.astype(bf16).astype(f32)
    return high, middle, rest - middle


def store_pieces(ref, values, order, base=0):
    pieces = split3(values)
    rows = values.shape[0]
    for place, piece in enumerate(order):
        ref[base + place * rows : base + (place + 1) * rows, :] = pieces[piece]


LEFT_ORDER = (0, 0, 0, 1, 1, 2)
RIGHT_ORDER = (0, 1, 2, 0, 1, 0)


class Load:
    def __init__(self, source, target, semaphore):
        self.copy = pltpu.make_async_copy(source, target, semaphore)
        self.target = target
        self.waiting = True
        self.copy.start()

    def __call__(self):
        if self.waiting:
            self.copy.wait()
            self.waiting = False
        return self.target


def run(kernel, name, outs, args, scratch=(), flops=10**9):
    plans = []
    for arg in args:
        if not isinstance(arg, tuple):
            arg = (arg, None, 1)
        array, take, count = arg
        if take is None:
            shape = array.shape
        else:
            shape = jax.eval_shape(lambda x, take=take: take(x, 0), array).shape
        plans.append((array, take, count, shape))
    n_in, n_out = len(plans), len(outs)
    starts, total = [], 0
    for plan in plans:
        starts.append(total)
        total += plan[2]
    out_starts, out_total = [], 0
    for out in outs:
        out_starts.append(out_total)
        out_total += out[2]
    start_order = [(i, 0) for i in range(n_in) if plans[i][2] == 1]
    split = [i for i in range(n_in) if plans[i][2] > 1]
    if split:
        at = len([i for i in range(split[0]) if plans[i][2] == 1])
        pieces = [(i, piece) for piece in range(plans[split[0]][2]) for i in split]
        start_order[at:at] = pieces
    arrays, places = [], []
    for plan in plans:
        known = [i for i, array in enumerate(arrays) if array is plan[0]]
        if known:
            places.append(known[0])
        else:
            places.append(len(arrays))
            arrays.append(plan[0])

    def whole(*refs):
        ins = refs[: len(arrays)]
        out_refs = refs[len(arrays) : len(arrays) + n_out]
        rest = refs[len(arrays) + n_out :]
        in_vmem, out_vmem = rest[:n_in], rest[n_in : n_in + n_out]
        in_sems, out_sems = rest[n_in + n_out : n_in + n_out + 2]
        loads = [[None] * count for _, _, count, _ in plans]
        for i, piece in start_order:
            _, take, count, _ = plans[i]
            source = ins[places[i]]
            view = source if take is None else take(source.at, piece)
            target = in_vmem[i] if count == 1 else in_vmem[i].at[piece]
            loads[i][piece] = Load(view, target, in_sems.at[starts[i] + piece])
        loads = [pieces if len(pieces) > 1 else pieces[0] for pieces in loads]
        pending = []

        def start(i, piece):
            target = out_vmem[i] if piece is None else out_vmem[i].at[piece]
            out = out_refs[i] if piece is None else out_refs[i].at[piece]
            copy = pltpu.make_async_copy(target, out, out_sems.at[out_starts[i] + (piece or 0)])
            copy.start()
            pending.append(copy)

        def store(i, value, piece=None):
            target = out_vmem[i] if piece is None else out_vmem[i].at[piece]
            if callable(value):
                value(target)
            else:
                target[...] = value
            start(i, piece)

        def many(i, fill, pieces):
            fill([out_vmem[i].at[piece] for piece in pieces])
            for piece in pieces:
                start(i, piece)

        store.many = many
        kernel(loads, store, *rest[n_in + n_out + 2 :])
        for pieces in loads:
            for load in pieces if isinstance(pieces, list) else [pieces]:
                load()
        for copy in pending:
            copy.wait()

    spec = pl.BlockSpec(memory_space=pltpu.HBM)
    in_scratch = [
        pltpu.VMEM(shape if count == 1 else (count,) + shape, array.dtype)
        for array, _, count, shape in plans
    ]
    return pl.pallas_call(
        whole,
        out_shape=[jax.ShapeDtypeStruct(out[0], out[1]) for out in outs],
        in_specs=[spec] * len(arrays),
        out_specs=[spec] * n_out,
        scratch_shapes=in_scratch
        + [pltpu.VMEM(out[0], out[1]) for out in outs]
        + [pltpu.SemaphoreType.DMA((total,)), pltpu.SemaphoreType.DMA((out_total,))]
        + list(scratch),
        compiler_params=pltpu.CompilerParams(vmem_limit_bytes=60 * MIB),
        cost_estimate=pl.CostEstimate(flops=flops, bytes_accessed=8 * MIB, transcendentals=0),
        name=name,
    )(*arrays)


def rows_of(start, stop, step=None):
    if step is None:
        return lambda ref, i: ref[start:stop]
    return lambda ref, i: ref[step, start:stop]


def piece_of(ref, i):
    return ref[i]


def fixed(step):
    return lambda ref, i: ref[step]


def pack_kernel(devices, loads, store, columns, extra):
    grid, features, partition, node = loads
    channels, cells = grid.target.shape
    fanout = partition.target.shape[0]
    links = cells * fanout
    width = columns.shape[0]
    slots = 2 * links
    capacity = slots // devices
    place = iota((cells, links), 1)
    repeat = jnp.where(
        functools.reduce(
            jnp.logical_or,
            [place == iota((cells, links), 0) + k * cells for k in range(fanout)],
        ),
        1.0,
        0.0,
    ).astype(bf16)
    order = iota((links, links), 0)
    turn = iota((links, links), 1)
    upper = jnp.where(order <= turn, 1.0, 0.0).astype(bf16)
    spread = jnp.where(order == turn % cells * fanout + turn // cells, 1.0, 0.0).astype(bf16)
    extra[...] = jnp.zeros_like(extra)
    columns[width - EXTRA - 16 : width - EXTRA, :] = jnp.zeros((16, links), bf16)
    store_pieces(extra, features()[...], LEFT_ORDER)
    target = jnp.concatenate([partition()[k : k + 1, :] for k in range(fanout)], axis=1)
    nodes = jnp.concatenate([node()[k : k + 1, :] for k in range(fanout)], axis=1) + 1
    extra[...] = dot(extra[...].astype(bf16), spread)
    extra[24:25, :] = (nodes >> 4).astype(f32)
    extra[25:26, :] = (nodes & 15).astype(f32)
    matches = jnp.where(iota((devices, links), 0) == target, 1.0, 0.0)
    counts = dot(matches.astype(bf16), upper)
    rank = jnp.sum(counts * matches, axis=0, keepdims=True).astype(jnp.int32) - 1
    slot = target * capacity + rank
    select = jnp.where(iota((slots, links), 0) == slot, 1.0, 0.0).astype(bf16)
    columns[0:channels, :] = dot(grid()[...], repeat).astype(bf16)
    columns[width - EXTRA : width, :] = extra[...].astype(bf16)
    store(0, dot(select, columns[...], 1, 1).astype(bf16))


def side_kernel(loads, store, pieces, turned, table):
    features, embed, edge_first, start, link_receiver, update_start, lists = loads
    owned, width = start.target.shape
    edges = features.target.shape[1]
    degree = edges // owned
    devices, slots = lists.target.shape[1:]
    pieces[...] = jnp.zeros_like(pieces)
    turned[...] = jnp.zeros_like(turned)
    table[...] = jnp.zeros_like(table)
    store_pieces(pieces, features()[...], LEFT_ORDER)
    turned[:, 0:EXTRA] = jnp.transpose(pieces[...])
    store_pieces(table, embed()[...], RIGHT_ORDER)
    matrix = table[...].astype(bf16)
    for j in range(degree):
        left = turned[pl.ds(j, owned, stride=degree), :].astype(bf16)
        edge_state = normalize(silu(dot(left, matrix))).astype(bf16)
        store(0, edge_state, j)
        store(1, dot(edge_state, edge_first()[...]).astype(bf16), j)
    store(2, dot(start()[...], link_receiver()[...]).astype(bf16))
    store(3, dot(start()[...], update_start()[...]))
    lists = lists()[0]
    rows = devices * slots
    row = iota((rows, 1), 0)
    picks = jnp.where(iota((rows, devices), 1) == row // slots, 1.0, 0.0).astype(bf16)
    high = dot(picks, (lists >> 4).astype(f32).astype(bf16))
    low = dot(picks, (lists & 15).astype(f32).astype(bf16))
    chosen = jnp.where(iota((rows, slots), 1) == row % slots, high * 16.0 + low, 0.0)
    column = jnp.sum(chosen, axis=1, keepdims=True).astype(jnp.int32)
    store(4, jnp.where(iota((rows, owned), 1) == column, 1.0, 0.0).astype(bf16))


def update(state, summand, second, gain):
    hidden = silu(summand).astype(bf16)
    return (state.astype(f32) + gain * normalize(dot(hidden, second))).astype(bf16)


def send(store, base, state, sender, select):
    sent = dot(state, sender).astype(bf16)
    store(base, dot(select, sent).astype(bf16))
    store(base + 1, sent)


def link_kernel(loads, store, first, table, messages, hidden, edge_state, picks):
    (
        terms,
        embed_first,
        link_embed,
        embed_second,
        link_sender,
        link_edge,
        receiver,
        link_second,
        base,
        update_first,
        update_second,
        gain,
        start,
        sender_first,
        select,
    ) = loads
    owned, width = start.target.shape
    slots = terms.target.shape[0]
    channels = embed_first.target.shape[0]
    tail = table.shape[0]
    lanes = iota((8, tail), 1)
    weights = jnp.where(
        lanes == tail - EXTRA + 24, 16.0, jnp.where(lanes == tail - EXTRA + 25, 1.0, 0.0)
    ).astype(bf16)
    chunks = [slice(begin, begin + 256) for begin in range(0, slots, 256)]

    def each(values, function):
        parts = [values[i : i + CHUNK, :] for i in range(0, values.shape[0], CHUNK)]
        return jnp.concatenate([function(part).astype(bf16) for part in parts], axis=0)

    table[...] = jnp.zeros_like(table)
    first[channels // 16 * 16 :, :] = jnp.zeros((width - channels // 16 * 16, width), bf16)
    first[0:channels, :] = embed_first()[...]
    store_pieces(table, link_embed()[...], RIGHT_ORDER, tail - EXTRA)
    matrix = table[...].astype(bf16)
    terms = terms()
    for rows in chunks:
        hidden[rows, :] = each(dot(terms[rows, :], first[...]), silu)
        extra = terms[rows, width - tail :]
        edge_state[rows, :] = each(dot(extra, matrix), lambda x: normalize(silu(x)))
        parts = extra.astype(f32)
        node = (
            parts[:, tail - EXTRA + 24 : tail - EXTRA + 25] * 16.0
            + parts[:, tail - EXTRA + 25 : tail - EXTRA + 26]
        ).astype(jnp.int32)
        pick = jnp.where(iota((rows.stop - rows.start, owned), 1) == node - 1, 1.0, 0.0)
        picks[rows, :] = pick.astype(bf16)
    nodes = dot(weights, terms[:, width - tail :], 1, 1)[0:1, :].astype(jnp.int32)
    collect = jnp.where(iota((owned, slots), 0) == nodes - 1, 1.0, 0.0).astype(bf16)
    for load in (embed_second, link_sender, link_edge, receiver, link_second):
        load()
    for rows in chunks:
        hidden[rows, :] = each(dot(hidden[rows, :], embed_second()[...]), normalize)
    for rows in chunks:
        sender = dot(hidden[rows, :], link_sender()[...]).astype(bf16).astype(f32)
        link_terms = (sender + dot(edge_state[rows, :], link_edge()[...])).astype(bf16)
        summand = link_terms.astype(f32) + dot(picks[rows, :], receiver()[...])
        hidden[rows, :] = each(summand, silu)
    for rows in chunks:
        messages[rows, :] = each(dot(hidden[rows, :], link_second()[...]), normalize)
    for load in (base, update_first, update_second, gain, start, sender_first, select):
        load()
    summed = dot(collect, messages[...]).astype(bf16)
    summand = base()[...] + dot(summed, update_first()[...])
    state = update(start()[...], summand, update_second()[...], gain()[0:1, :])
    store(0, state)
    send(store, 1, state, sender_first()[...], select()[...])


def local_kernel(step, last, loads, store, summands, kept):
    senders, state, receiver_first, sent = loads[:4]
    parts = loads[5 if step else 4]
    degree, owned = senders.target.shape
    groups = groups_of(degree, LOCAL_GROUP)
    columns = jnp.transpose(senders()[...].astype(f32)).astype(jnp.int32)
    kept[...] = dot(state()[...], receiver_first()[...]).astype(bf16).astype(f32)
    for group in groups:
        summands[...] = dot(one_hot(columns, group, owned), sent()[...])
        olds = [parts[j]() for j in group]
        if step:
            states = [
                (olds[i][...].astype(f32) + loads[6][j]()[...].astype(f32)).astype(bf16)
                for i, j in enumerate(group)
            ]
            if not last:
                for i, j in enumerate(group):
                    store(1, states[i], j)
            summands[...] += dot(jnp.concatenate(states, axis=0), loads[4]()[...])
        for i, j in enumerate(group):

            def fill(target):
                for begin in range(0, owned, CHUNK):
                    some = slice(begin, begin + CHUNK)
                    values = summands[i * owned + begin : i * owned + begin + CHUNK, :]
                    values = values + kept[some, :]
                    if not step:
                        values = values + olds[i][some, :].astype(f32)
                    target[some, :] = values.astype(bf16)

            store(0, fill, j)


def edge_kernel(step, last, loads, store, summands, hiddens, results, total):
    senders, incoming, second, sums = loads[:4]
    (state, state_first, summed_first, update_second, gain) = loads[4:9]
    degree, owned = senders.target.shape
    rows = incoming.target.shape[0]
    groups = groups_of(degree, EDGE_GROUP)
    columns = jnp.transpose((senders()[...] - owned).astype(f32)).astype(jnp.int32)

    def lead(g):
        summands[g % 2] = dot(one_hot(columns, groups[g], rows), incoming()[...])

    def middle(g):
        for i, j in enumerate(groups[g]):
            part = sums[j]()
            for begin in range(0, owned, CHUNK):
                some = slice(i * owned + begin, i * owned + begin + CHUNK)
                summand = part[begin : begin + CHUNK, :].astype(f32) + summands[g % 2, some, :]
                hiddens[g % 2, some, :] = silu(summand).astype(bf16)
        results[g % 2] = dot(hiddens[g % 2], second()[...])

    def tail(g):
        group = groups[g]

        def fill(targets):
            for begin in range(0, owned, CHUNK):
                here = slice(begin, begin + CHUNK)
                added = total[here, :] if g else None
                for i, j in enumerate(group):
                    some = slice(i * owned + begin, i * owned + begin + CHUNK)
                    message = normalize(results[g % 2, some, :])
                    if targets is not None:
                        message = message.astype(bf16)
                        targets[i][here, :] = message
                        message = message.astype(f32)
                    added = message if added is None else added + message
                total[here, :] = added

        if last:
            fill(None)
        else:
            store.many(3, fill, group)

    lead(0)
    middle(0)
    for g in range(len(groups)):
        if g + 1 < len(groups):
            lead(g + 1)
            middle(g + 1)
        tail(g)
    summand = dot(state()[...], state_first()[...]) + dot(
        total[...].astype(bf16), summed_first()[...]
    )
    state = update(
        state()[...], summand, update_second()[...], gain()[step + 1 : step + 2, :]
    )
    store(0, state)
    if not last:
        sender_first, select = loads[9:]
        send(store, 1, state, sender_first()[...], select()[...])


def body(
    grid_inputs,
    link_features,
    link_partition,
    link_node,
    mesh_start,
    edge_features,
    edge_senders,
    halo_lists,
    embed_first,
    embed_second,
    link_embed,
    link_first,
    link_second,
    update_first,
    update_second,
    edge_embed,
    process_first,
    process_second,
    process_update_first,
    process_update_second,
    update_gain,
):
    owned, width = mesh_start.shape
    devices = lax.axis_size("rows")
    cells = grid_inputs.shape[1]
    links = cells * link_partition.shape[1]
    slots = 2 * links
    degree = edge_senders.shape[1]
    edges = owned * degree
    halo_slots = halo_lists.shape[2]
    halo_rows = devices * halo_slots
    senders = edge_senders.T

    def exchange(values):
        values = values.reshape(devices, -1, width)
        return lax.all_to_all(values, "rows", split_axis=0, concat_axis=0, tiled=True).reshape(
            -1, width
        )

    sending = [((halo_rows, width), bf16, 1), ((owned, width), bf16, 1)]
    (packed,) = run(
        functools.partial(pack_kernel, devices),
        "pack",
        [((slots, width), bf16, 1)],
        (grid_inputs, link_features, link_partition.T, link_node.T),
        [pltpu.VMEM((width, links), bf16), pltpu.VMEM((EXTRA, links), f32)],
    )
    terms = exchange(packed)
    edge_state, parts, receiver, base, select = run(
        side_kernel,
        "side",
        [
            ((degree, owned, width), bf16, degree),
            ((degree, owned, width), bf16, degree),
            ((owned, width), bf16, 1),
            ((owned, width), f32, 1),
            ((halo_rows, owned), bf16, 1),
        ],
        (
            edge_features,
            edge_embed,
            (process_first, rows_of(2 * width, 3 * width, 0), 1),
            mesh_start,
            (link_first, rows_of(width, 2 * width), 1),
            (update_first, rows_of(0, width), 1),
            halo_lists,
        ),
        [
            pltpu.VMEM((EXTRA, edges), f32),
            pltpu.VMEM((edges, 128), f32),
            pltpu.VMEM((128, width), f32),
        ],
        flops=10**10,
    )
    state, outgoing, sent = run(
        link_kernel,
        "link",
        [((owned, width), bf16, 1)] + sending,
        (
            terms,
            embed_first,
            link_embed,
            embed_second,
            (link_first, rows_of(0, width), 1),
            (link_first, rows_of(2 * width, 3 * width), 1),
            receiver,
            link_second,
            base,
            (update_first, rows_of(width, 2 * width), 1),
            update_second,
            update_gain,
            mesh_start,
            (process_first, rows_of(0, width, 0), 1),
            select,
        ),
        [
            pltpu.VMEM((width, width), bf16),
            pltpu.VMEM((128, width), f32),
            pltpu.VMEM((slots, width), bf16),
            pltpu.VMEM((slots, width), bf16),
            pltpu.VMEM((slots, width), bf16),
            pltpu.VMEM((slots, owned), bf16),
        ],
    )
    steps = process_first.shape[0]
    for step in range(steps):
        last = step + 1 == steps
        incoming = exchange(outgoing)
        extra = []
        if step:
            extra = [(process_first, rows_of(2 * width, 3 * width, step), 1)]
            parts = edge_state
        (sums, *kept) = run(
            functools.partial(local_kernel, step, last),
            f"local{step}",
            [((degree, owned, width), bf16, degree)] * (1 if last or step == 0 else 2),
            [
                senders,
                state,
                (process_first, rows_of(width, 2 * width, step), 1),
                sent,
            ]
            + extra
            + [(parts, piece_of, degree)]
            + ([(message, piece_of, degree)] if step else []),
            [
                pltpu.VMEM((LOCAL_GROUP * owned, width), f32),
                pltpu.VMEM((owned, width), f32),
            ],
            flops=10**10,
        )
        if kept:
            edge_state = kept[0]
        outs = [((owned, width), bf16, 1)]
        extra = []
        if not last:
            outs += sending + [((degree, owned, width), bf16, degree)]
            extra = [(process_first, rows_of(0, width, step + 1), 1), select]
        results = run(
            functools.partial(edge_kernel, step, last),
            f"edge{step}",
            outs,
            [
                senders,
                incoming,
                (process_second, fixed(step), 1),
                (sums, piece_of, degree),
                state,
                (process_update_first, rows_of(0, width, step), 1),
                (process_update_first, rows_of(width, 2 * width, step), 1),
                (process_update_second, fixed(step), 1),
                update_gain,
            ]
            + extra,
            [
                pltpu.VMEM((2, EDGE_GROUP * owned, width), f32),
                pltpu.VMEM((2, EDGE_GROUP * owned, width), bf16),
                pltpu.VMEM((2, EDGE_GROUP * owned, width), f32),
                pltpu.VMEM((owned, width), f32),
            ],
        )
        if last:
            return results[0]
        state, outgoing, sent, message = results


def solution(mesh):
    return jax.shard_map(
        body,
        mesh=mesh,
        in_specs=(
            P(None, ("groups", "rows")),
            P(None, "rows"),
            P("rows", None),
            P("rows", None),
            P("rows", None),
            P(None, "rows"),
            P("rows", None),
            P("rows", None, None),
        )
        + (P(),) * 13,
        out_specs=P(("groups", "rows"), None),
        check_vma=False,
    )
```

```python
import functools

import jax
import jax.numpy as jnp
from jax import lax
from jax.experimental import pallas as pl
from jax.experimental.pallas import tpu as pltpu
from jax.sharding import PartitionSpec as P

epsilon = 1e-05
f32 = jnp.float32
bf16 = jnp.bfloat16
MIB = 2**20
EXTRA = 32
CHUNK = 32


def dot(left, right, left_dim=1, right_dim=0):
    return lax.dot_general(
        left, right, (((left_dim,), (right_dim,)), ((), ())), preferred_element_type=f32
    )


def silu(values):
    half = 0.5 * values
    return half + half * jnp.tanh(half)


def silu_of_half(half):
    return half + half * jnp.tanh(half)


def centred(weights):
    values = weights.astype(f32)
    mean = jnp.sum(values, axis=-1, keepdims=True) * (1.0 / values.shape[-1])
    return (values - mean).astype(bf16)


def scale_rows(values):
    spread = jnp.sum(values * values, axis=-1, keepdims=True) * (1.0 / values.shape[-1])
    return values * lax.rsqrt(spread + epsilon)


def normalize(values):
    scale = 1.0 / values.shape[-1]
    center = values - jnp.sum(values, axis=-1, keepdims=True) * scale
    spread = jnp.sum(center * center, axis=-1, keepdims=True) * scale
    return center * lax.rsqrt(spread + epsilon)


def iota(shape, dim):
    return lax.broadcasted_iota(jnp.int32, shape, dim)


def split3(values):
    high = values.astype(bf16).astype(f32)
    rest = values - high
    middle = rest.astype(bf16).astype(f32)
    return high, middle, rest - middle


def store_pieces(ref, values, order, base=0):
    pieces = split3(values)
    rows = values.shape[0]
    for place, piece in enumerate(order):
        ref[base + place * rows : base + (place + 1) * rows, :] = pieces[piece]


LEFT_ORDER = (0, 0, 0, 1, 1, 2)
RIGHT_ORDER = (0, 1, 2, 0, 1, 0)


class Load:
    def __init__(self, source, target, semaphore):
        self.copy = pltpu.make_async_copy(source, target, semaphore)
        self.target = target
        self.waiting = True
        self.copy.start()

    def __call__(self):
        if self.waiting:
            self.copy.wait()
            self.waiting = False
        return self.target


def run(kernel, name, outs, args, scratch=(), flops=10**9):
    plans = []
    for arg in args:
        if not isinstance(arg, tuple):
            arg = (arg, None, 1)
        array, take, count = arg
        if take is None:
            shape = array.shape
        else:
            shape = jax.eval_shape(lambda x, take=take: take(x, 0), array).shape
        plans.append((array, take, count, shape))
    n_in, n_out = len(plans), len(outs)
    starts, total = [], 0
    for plan in plans:
        starts.append(total)
        total += plan[2]
    out_starts, out_total = [], 0
    for out in outs:
        out_starts.append(out_total)
        out_total += out[2]
    start_order = [(i, 0) for i in range(n_in) if plans[i][2] == 1]
    split = [i for i in range(n_in) if plans[i][2] > 1]
    if split:
        at = len([i for i in range(split[0]) if plans[i][2] == 1])
        pieces = [(i, piece) for piece in range(plans[split[0]][2]) for i in split]
        start_order[at:at] = pieces
    arrays, places = [], []
    for plan in plans:
        known = [i for i, array in enumerate(arrays) if array is plan[0]]
        if known:
            places.append(known[0])
        else:
            places.append(len(arrays))
            arrays.append(plan[0])

    def whole(*refs):
        ins = refs[: len(arrays)]
        out_refs = refs[len(arrays) : len(arrays) + n_out]
        rest = refs[len(arrays) + n_out :]
        in_vmem, out_vmem = rest[:n_in], rest[n_in : n_in + n_out]
        in_sems, out_sems = rest[n_in + n_out : n_in + n_out + 2]
        loads = [[None] * count for _, _, count, _ in plans]
        for i, piece in start_order:
            _, take, count, _ = plans[i]
            source = ins[places[i]]
            view = source if take is None else take(source.at, piece)
            target = in_vmem[i] if count == 1 else in_vmem[i].at[piece]
            loads[i][piece] = Load(view, target, in_sems.at[starts[i] + piece])
        loads = [pieces if len(pieces) > 1 else pieces[0] for pieces in loads]
        pending, waiting = [], []

        def store(i, value, piece=None, hold=False):
            target = out_vmem[i] if piece is None else out_vmem[i].at[piece]
            out = out_refs[i] if piece is None else out_refs[i].at[piece]
            if callable(value):
                value(target)
            else:
                target[...] = value
            copy = pltpu.make_async_copy(target, out, out_sems.at[out_starts[i] + (piece or 0)])
            waiting.append(copy)
            if not hold:
                flush()

        def flush():
            for copy in waiting:
                copy.start()
            pending.extend(waiting)
            waiting.clear()

        store.flush = flush
        kernel(loads, store, *rest[n_in + n_out + 2 :])
        for pieces in loads:
            for load in pieces if isinstance(pieces, list) else [pieces]:
                load()
        flush()
        for copy in pending:
            copy.wait()

    spec = pl.BlockSpec(memory_space=pltpu.HBM)
    in_scratch = [
        pltpu.VMEM(shape if count == 1 else (count,) + shape, array.dtype)
        for array, _, count, shape in plans
    ]
    return pl.pallas_call(
        whole,
        out_shape=[jax.ShapeDtypeStruct(out[0], out[1]) for out in outs],
        in_specs=[spec] * len(arrays),
        out_specs=[spec] * n_out,
        scratch_shapes=in_scratch
        + [pltpu.VMEM(out[0], out[1]) for out in outs]
        + [pltpu.SemaphoreType.DMA((total,)), pltpu.SemaphoreType.DMA((out_total,))]
        + list(scratch),
        compiler_params=pltpu.CompilerParams(vmem_limit_bytes=60 * MIB),
        cost_estimate=pl.CostEstimate(flops=flops, bytes_accessed=8 * MIB, transcendentals=0),
        name=name,
    )(*arrays)


def rows_of(start, stop, step=None):
    if step is None:
        return lambda ref, i: ref[start:stop]
    return lambda ref, i: ref[step, start:stop]


def piece_of(ref, i):
    return ref[i]


def fixed(step):
    return lambda ref, i: ref[step]


def pack_kernel(devices, loads, store, columns, extra):
    grid, features, partition, node = loads
    channels, cells = grid.target.shape
    fanout = partition.target.shape[0]
    links = cells * fanout
    width = columns.shape[0]
    slots = 2 * links
    capacity = slots // devices
    place = iota((cells, links), 1)
    repeat = jnp.where(
        functools.reduce(
            jnp.logical_or,
            [place == iota((cells, links), 0) + k * cells for k in range(fanout)],
        ),
        1.0,
        0.0,
    ).astype(bf16)
    order = iota((links, links), 0)
    turn = iota((links, links), 1)
    upper = jnp.where(order <= turn, 1.0, 0.0).astype(bf16)
    spread = jnp.where(order == turn % cells * fanout + turn // cells, 1.0, 0.0).astype(bf16)
    extra[...] = jnp.zeros_like(extra)
    columns[width - EXTRA - 16 : width - EXTRA, :] = jnp.zeros((16, links), bf16)
    store_pieces(extra, features()[...], LEFT_ORDER)
    target = jnp.concatenate([partition()[k : k + 1, :] for k in range(fanout)], axis=1)
    nodes = jnp.concatenate([node()[k : k + 1, :] for k in range(fanout)], axis=1) + 1
    extra[...] = dot(extra[...].astype(bf16), spread)
    extra[24:25, :] = (nodes >> 4).astype(f32)
    extra[25:26, :] = (nodes & 15).astype(f32)
    matches = jnp.where(iota((devices, links), 0) == target, 1.0, 0.0)
    counts = dot(matches.astype(bf16), upper)
    rank = jnp.sum(counts * matches, axis=0, keepdims=True).astype(jnp.int32) - 1
    slot = target * capacity + rank
    select = jnp.where(iota((slots, links), 0) == slot, 1.0, 0.0).astype(bf16)
    columns[0:channels, :] = dot(grid()[...], repeat).astype(bf16)
    columns[width - EXTRA : width, :] = extra[...].astype(bf16)
    store(0, dot(select, columns[...], 1, 1).astype(bf16))


def side_kernel(loads, store, pieces, turned, table):
    features, embed, edge_first, start, link_receiver, update_start, lists = loads[:7]
    singles, stacks = loads[7:10], loads[10:]
    owned, width = start.target.shape
    edges = features.target.shape[1]
    degree = edges // owned
    devices, slots = lists.target.shape[1:]
    pieces[...] = jnp.zeros_like(pieces)
    turned[...] = jnp.zeros_like(turned)
    table[...] = jnp.zeros_like(table)
    store_pieces(pieces, features()[...], LEFT_ORDER)
    turned[:, 0:EXTRA] = jnp.transpose(pieces[...])
    store_pieces(table, embed()[...], RIGHT_ORDER)
    matrix = table[...].astype(bf16)
    for j in range(degree):
        left = turned[pl.ds(j, owned, stride=degree), :].astype(bf16)
        edge_state = normalize(silu(dot(left, matrix))).astype(bf16)
        store(0, edge_state, j)
        store(1, (0.5 * dot(edge_state, edge_first()[...])).astype(bf16), j)
    store(2, dot(start()[...], link_receiver()[...]).astype(bf16))
    store(3, dot(start()[...], update_start()[...]))
    lists = lists()[0]
    rows = devices * slots
    row = iota((rows, 1), 0)
    picks = jnp.where(iota((rows, devices), 1) == row // slots, 1.0, 0.0).astype(bf16)
    high = dot(picks, (lists >> 4).astype(f32).astype(bf16))
    low = dot(picks, (lists & 15).astype(f32).astype(bf16))
    chosen = jnp.where(iota((rows, slots), 1) == row % slots, high * 16.0 + low, 0.0)
    column = jnp.sum(chosen, axis=1, keepdims=True).astype(jnp.int32)
    store(4, jnp.where(iota((rows, owned), 1) == column, 1.0, 0.0).astype(bf16))
    for place, load in enumerate(singles):
        store(5 + place, centred(load()[...]))
    for place, load in enumerate(stacks):
        weights = load()[...]
        store(8 + place, jnp.stack([centred(part) for part in weights], axis=0))


def update(state, summand, second, gain):
    hidden = silu(summand).astype(bf16)
    return (state.astype(f32) + gain * scale_rows(dot(hidden, second))).astype(bf16)


def send(store, base, state, sender, select):
    sent = dot(state, sender).astype(bf16) * 0.5
    store(base, dot(select, sent).astype(bf16))
    store(base + 1, sent)


def link_kernel(loads, store, first, table, messages, hidden, edge_state, picks):
    (
        terms,
        embed_first,
        link_embed,
        embed_second,
        link_sender,
        link_edge,
        receiver,
        link_second,
        base,
        update_first,
        update_second,
        gain,
        start,
        sender_first,
        select,
    ) = loads
    owned, width = start.target.shape
    slots = terms.target.shape[0]
    channels = embed_first.target.shape[0]
    tail = table.shape[0]
    lanes = iota((8, tail), 1)
    weights = jnp.where(
        lanes == tail - EXTRA + 24, 16.0, jnp.where(lanes == tail - EXTRA + 25, 1.0, 0.0)
    ).astype(bf16)
    chunks = [slice(begin, begin + 128) for begin in range(0, slots, 128)]

    def each(values, function):
        parts = [values[i : i + CHUNK, :] for i in range(0, values.shape[0], CHUNK)]
        return jnp.concatenate([function(part).astype(bf16) for part in parts], axis=0)

    table[...] = jnp.zeros_like(table)
    first[channels // 16 * 16 :, :] = jnp.zeros((width - channels // 16 * 16, width), bf16)
    first[0:channels, :] = embed_first()[...]
    store_pieces(table, link_embed()[...], RIGHT_ORDER, tail - EXTRA)
    matrix = table[...].astype(bf16)
    terms = terms()
    for rows in chunks:
        hidden[rows, :] = each(dot(terms[rows, :], first[...]), silu)
        extra = terms[rows, width - tail :]
        edge_state[rows, :] = each(dot(extra, matrix), lambda x: normalize(silu(x)))
        parts = extra.astype(f32)
        node = (
            parts[:, tail - EXTRA + 24 : tail - EXTRA + 25] * 16.0
            + parts[:, tail - EXTRA + 25 : tail - EXTRA + 26]
        ).astype(jnp.int32)
        pick = jnp.where(iota((rows.stop - rows.start, owned), 1) == node - 1, 1.0, 0.0)
        picks[rows, :] = pick.astype(bf16)
    nodes = dot(weights, terms[:, width - tail :], 1, 1)[0:1, :].astype(jnp.int32)
    collect = jnp.where(iota((owned, slots), 0) == nodes - 1, 1.0, 0.0).astype(bf16)
    for load in (embed_second, link_sender, link_edge, receiver, link_second):
        load()
    for rows in chunks:
        hidden[rows, :] = each(dot(hidden[rows, :], embed_second()[...]), scale_rows)
    for rows in chunks:
        sender = dot(hidden[rows, :], link_sender()[...]).astype(bf16).astype(f32)
        link_terms = (sender + dot(edge_state[rows, :], link_edge()[...])).astype(bf16)
        summand = link_terms.astype(f32) + dot(picks[rows, :], receiver()[...])
        hidden[rows, :] = each(summand, silu)
    for rows in chunks:
        messages[rows, :] = each(dot(hidden[rows, :], link_second()[...]), scale_rows)
    for load in (base, update_first, update_second, gain, start, sender_first, select):
        load()
    summed = dot(collect, messages[...]).astype(bf16)
    summand = base()[...] + dot(summed, update_first()[...])
    state = update(start()[...], summand, update_second()[...], gain()[0:1, :])
    store(0, state)
    send(store, 1, state, sender_first()[...], select()[...])


def local_kernel(step, last, loads, store):
    senders, state, receiver_first, sent = loads[:4]
    parts = loads[5 if step else 4]
    degree, owned = senders.target.shape
    columns = jnp.transpose(senders()[...].astype(f32)).astype(jnp.int32)
    kept = 0.5 * dot(state()[...], receiver_first()[...]).astype(bf16).astype(f32)
    if step:
        edge_first = loads[4]()[...] * 0.5
    for j in range(degree):
        local = jnp.where(iota((owned, owned), 1) == columns[:, j : j + 1], 1.0, 0.0)
        part = parts[j]()[...]
        if step:
            edge_state = (part.astype(f32) + loads[6][j]()[...].astype(f32)).astype(bf16)
            if not last:
                store(1, edge_state, j)
            part = dot(edge_state, edge_first)
        part = dot(local.astype(bf16), sent()[...]) + part.astype(f32)
        store(0, (part + kept).astype(bf16), j)


def edge_kernel(step, last, loads, store, summands, hiddens, results, total):
    senders, incoming, second, sums = loads[:4]
    (state, state_first, summed_first, update_second, gain) = loads[4:9]
    degree, owned = senders.target.shape
    rows = incoming.target.shape[0]
    columns = jnp.transpose((senders()[...] - owned).astype(f32)).astype(jnp.int32)

    def lead(j):
        pick = jnp.where(iota((owned, rows), 1) == columns[:, j : j + 1], 1.0, 0.0)
        summands[j % 2] = dot(pick.astype(bf16), incoming()[...])

    def middle(j):
        part = sums[j]()
        for begin in range(0, owned, CHUNK):
            some = slice(begin, begin + CHUNK)
            summand = part[some, :].astype(f32) + summands[j % 2, some, :]
            hiddens[j % 2, some, :] = silu_of_half(summand).astype(bf16)
        results[j % 2] = dot(hiddens[j % 2], second()[...])

    def tail(j):
        def fill(target):
            for begin in range(0, owned, CHUNK):
                some = slice(begin, begin + CHUNK)
                message = scale_rows(results[j % 2, some, :])
                if target is not None:
                    message = message.astype(bf16)
                    target[some, :] = message
                    message = message.astype(f32)
                total[some, :] = message if j == 0 else total[some, :] + message

        if last:
            fill(None)
        else:
            store(3, fill, j)

    lead(0)
    middle(0)
    for j in range(degree):
        if j + 1 < degree:
            lead(j + 1)
            middle(j + 1)
        tail(j)
    summand = dot(state()[...], state_first()[...]) + dot(
        total[...].astype(bf16), summed_first()[...]
    )
    state = update(
        state()[...], summand, update_second()[...], gain()[step + 1 : step + 2, :]
    )
    store(0, state)
    if not last:
        sender_first, select = loads[9:]
        send(store, 1, state, sender_first()[...], select()[...])


def body(
    grid_inputs,
    link_features,
    link_partition,
    link_node,
    mesh_start,
    edge_features,
    edge_senders,
    halo_lists,
    embed_first,
    embed_second,
    link_embed,
    link_first,
    link_second,
    update_first,
    update_second,
    edge_embed,
    process_first,
    process_second,
    process_update_first,
    process_update_second,
    update_gain,
):
    owned, width = mesh_start.shape
    devices = lax.axis_size("rows")
    cells = grid_inputs.shape[1]
    links = cells * link_partition.shape[1]
    slots = 2 * links
    degree = edge_senders.shape[1]
    edges = owned * degree
    halo_slots = halo_lists.shape[2]
    halo_rows = devices * halo_slots
    senders = edge_senders.T

    def exchange(values):
        values = values.reshape(devices, -1, width)
        return lax.all_to_all(values, "rows", split_axis=0, concat_axis=0, tiled=True).reshape(
            -1, width
        )

    sending = [((halo_rows, width), bf16, 1), ((owned, width), bf16, 1)]
    (packed,) = run(
        functools.partial(pack_kernel, devices),
        "pack",
        [((slots, width), bf16, 1)],
        (grid_inputs, link_features, link_partition.T, link_node.T),
        [pltpu.VMEM((width, links), bf16), pltpu.VMEM((EXTRA, links), f32)],
    )
    terms = exchange(packed)
    steps = process_first.shape[0]
    singles = (embed_second, link_second, update_second)
    stacks = (process_second, process_update_second)
    edge_state, parts, receiver, base, select, *seconds = run(
        side_kernel,
        "side",
        [
            ((degree, owned, width), bf16, degree),
            ((degree, owned, width), bf16, degree),
            ((owned, width), bf16, 1),
            ((owned, width), f32, 1),
            ((halo_rows, owned), bf16, 1),
        ]
        + [(array.shape, bf16, 1) for array in singles + stacks],
        (
            edge_features,
            edge_embed,
            (process_first, rows_of(2 * width, 3 * width, 0), 1),
            mesh_start,
            (link_first, rows_of(width, 2 * width), 1),
            (update_first, rows_of(0, width), 1),
            halo_lists,
        )
        + singles
        + stacks,
        [
            pltpu.VMEM((EXTRA, edges), f32),
            pltpu.VMEM((edges, 128), f32),
            pltpu.VMEM((128, width), f32),
        ],
        flops=10**10,
    )
    embed_second, link_second, update_second, process_second, process_update_second = seconds
    state, outgoing, sent = run(
        link_kernel,
        "link",
        [((owned, width), bf16, 1)] + sending,
        (
            terms,
            embed_first,
            link_embed,
            embed_second,
            (link_first, rows_of(0, width), 1),
            (link_first, rows_of(2 * width, 3 * width), 1),
            receiver,
            link_second,
            base,
            (update_first, rows_of(width, 2 * width), 1),
            update_second,
            update_gain,
            mesh_start,
            (process_first, rows_of(0, width, 0), 1),
            select,
        ),
        [
            pltpu.VMEM((width, width), bf16),
            pltpu.VMEM((128, width), f32),
            pltpu.VMEM((slots, width), bf16),
            pltpu.VMEM((slots, width), bf16),
            pltpu.VMEM((slots, width), bf16),
            pltpu.VMEM((slots, owned), bf16),
        ],
    )
    for step in range(steps):
        last = step + 1 == steps
        incoming = exchange(outgoing)
        extra = []
        if step:
            extra = [(process_first, rows_of(2 * width, 3 * width, step), 1)]
            parts = edge_state
        (sums, *kept) = run(
            functools.partial(local_kernel, step, last),
            f"local{step}",
            [((degree, owned, width), bf16, degree)] * (1 if last or step == 0 else 2),
            [
                senders,
                state,
                (process_first, rows_of(width, 2 * width, step), 1),
                sent,
            ]
            + extra
            + [(parts, piece_of, degree)]
            + ([(message, piece_of, degree)] if step else []),
            flops=10**10,
        )
        if kept:
            edge_state = kept[0]
        outs = [((owned, width), bf16, 1)]
        extra = []
        if not last:
            outs += sending + [((degree, owned, width), bf16, degree)]
            extra = [(process_first, rows_of(0, width, step + 1), 1), select]
        results = run(
            functools.partial(edge_kernel, step, last),
            f"edge{step}",
            outs,
            [
                senders,
                incoming,
                (process_second, fixed(step), 1),
                (sums, piece_of, degree),
                state,
                (process_update_first, rows_of(0, width, step), 1),
                (process_update_first, rows_of(width, 2 * width, step), 1),
                (process_update_second, fixed(step), 1),
                update_gain,
            ]
            + extra,
            [
                pltpu.VMEM((2, owned, width), f32),
                pltpu.VMEM((2, owned, width), bf16),
                pltpu.VMEM((2, owned, width), f32),
                pltpu.VMEM((owned, width), f32),
            ],
        )
        if last:
            return results[0]
        state, outgoing, sent, message = results


def solution(mesh):
    return jax.shard_map(
        body,
        mesh=mesh,
        in_specs=(
            P(None, ("groups", "rows")),
            P(None, "rows"),
            P("rows", None),
            P("rows", None),
            P("rows", None),
            P(None, "rows"),
            P("rows", None),
            P("rows", None, None),
        )
        + (P(),) * 13,
        out_specs=P(("groups", "rows"), None),
        check_vma=False,
    )
```

```python
import functools

import jax
import jax.numpy as jnp
from jax import lax
from jax.experimental import pallas as pl
from jax.experimental.pallas import tpu as pltpu
from jax.sharding import PartitionSpec as P

epsilon = 1e-05
f32 = jnp.float32
bf16 = jnp.bfloat16
MIB = 2**20
EXTRA = 32
CHUNK = 32


def dot(left, right, left_dim=1, right_dim=0):
    return lax.dot_general(
        left, right, (((left_dim,), (right_dim,)), ((), ())), preferred_element_type=f32
    )


def silu(values):
    half = 0.5 * values
    return half + half * jnp.tanh(half)


def silu_of_half(half):
    return half + half * jnp.tanh(half)


def centred(weights):
    values = weights.astype(f32)
    mean = jnp.sum(values, axis=-1, keepdims=True) * (1.0 / values.shape[-1])
    return (values - mean).astype(bf16)


def scale_rows(values):
    spread = jnp.sum(values * values, axis=-1, keepdims=True) * (1.0 / values.shape[-1])
    return values * lax.rsqrt(spread + epsilon)


def normalize(values):
    scale = 1.0 / values.shape[-1]
    center = values - jnp.sum(values, axis=-1, keepdims=True) * scale
    spread = jnp.sum(center * center, axis=-1, keepdims=True) * scale
    return center * lax.rsqrt(spread + epsilon)


def iota(shape, dim):
    return lax.broadcasted_iota(jnp.int32, shape, dim)


def split3(values):
    high = values.astype(bf16).astype(f32)
    rest = values - high
    middle = rest.astype(bf16).astype(f32)
    return high, middle, rest - middle


def store_pieces(ref, values, order, base=0):
    pieces = split3(values)
    rows = values.shape[0]
    for place, piece in enumerate(order):
        ref[base + place * rows : base + (place + 1) * rows, :] = pieces[piece]


LEFT_ORDER = (0, 0, 0, 1, 1, 2)
RIGHT_ORDER = (0, 1, 2, 0, 1, 0)


class Load:
    def __init__(self, source, target, semaphore):
        self.copy = pltpu.make_async_copy(source, target, semaphore)
        self.target = target
        self.waiting = True
        self.copy.start()

    def __call__(self):
        if self.waiting:
            self.copy.wait()
            self.waiting = False
        return self.target


def run(kernel, name, outs, args, scratch=(), flops=10**9):
    plans = []
    for arg in args:
        if not isinstance(arg, tuple):
            arg = (arg, None, 1)
        array, take, count = arg
        if take is None:
            shape = array.shape
        else:
            shape = jax.eval_shape(lambda x, take=take: take(x, 0), array).shape
        plans.append((array, take, count, shape))
    n_in, n_out = len(plans), len(outs)
    starts, total = [], 0
    for plan in plans:
        starts.append(total)
        total += plan[2]
    out_starts, out_total = [], 0
    for out in outs:
        out_starts.append(out_total)
        out_total += out[2]
    start_order = [(i, 0) for i in range(n_in) if plans[i][2] == 1]
    split = [i for i in range(n_in) if plans[i][2] > 1]
    if split:
        at = len([i for i in range(split[0]) if plans[i][2] == 1])
        pieces = [(i, piece) for piece in range(plans[split[0]][2]) for i in split]
        start_order[at:at] = pieces
    arrays, places = [], []
    for plan in plans:
        known = [i for i, array in enumerate(arrays) if array is plan[0]]
        if known:
            places.append(known[0])
        else:
            places.append(len(arrays))
            arrays.append(plan[0])

    def whole(*refs):
        ins = refs[: len(arrays)]
        out_refs = refs[len(arrays) : len(arrays) + n_out]
        rest = refs[len(arrays) + n_out :]
        in_vmem, out_vmem = rest[:n_in], rest[n_in : n_in + n_out]
        in_sems, out_sems = rest[n_in + n_out : n_in + n_out + 2]
        loads = [[None] * count for _, _, count, _ in plans]
        for i, piece in start_order:
            _, take, count, _ = plans[i]
            source = ins[places[i]]
            view = source if take is None else take(source.at, piece)
            target = in_vmem[i] if count == 1 else in_vmem[i].at[piece]
            loads[i][piece] = Load(view, target, in_sems.at[starts[i] + piece])
        loads = [pieces if len(pieces) > 1 else pieces[0] for pieces in loads]
        pending, waiting = [], []

        def store(i, value, piece=None, hold=False):
            target = out_vmem[i] if piece is None else out_vmem[i].at[piece]
            out = out_refs[i] if piece is None else out_refs[i].at[piece]
            if callable(value):
                value(target)
            else:
                target[...] = value
            copy = pltpu.make_async_copy(target, out, out_sems.at[out_starts[i] + (piece or 0)])
            waiting.append(copy)
            if not hold:
                flush()

        def flush():
            for copy in waiting:
                copy.start()
            pending.extend(waiting)
            waiting.clear()

        store.flush = flush
        kernel(loads, store, *rest[n_in + n_out + 2 :])
        for pieces in loads:
            for load in pieces if isinstance(pieces, list) else [pieces]:
                load()
        flush()
        for copy in pending:
            copy.wait()

    spec = pl.BlockSpec(memory_space=pltpu.HBM)
    in_scratch = [
        pltpu.VMEM(shape if count == 1 else (count,) + shape, array.dtype)
        for array, _, count, shape in plans
    ]
    return pl.pallas_call(
        whole,
        out_shape=[jax.ShapeDtypeStruct(out[0], out[1]) for out in outs],
        in_specs=[spec] * len(arrays),
        out_specs=[spec] * n_out,
        scratch_shapes=in_scratch
        + [pltpu.VMEM(out[0], out[1]) for out in outs]
        + [pltpu.SemaphoreType.DMA((total,)), pltpu.SemaphoreType.DMA((out_total,))]
        + list(scratch),
        compiler_params=pltpu.CompilerParams(vmem_limit_bytes=60 * MIB),
        cost_estimate=pl.CostEstimate(flops=flops, bytes_accessed=8 * MIB, transcendentals=0),
        name=name,
    )(*arrays)


def rows_of(start, stop, step=None):
    if step is None:
        return lambda ref, i: ref[start:stop]
    return lambda ref, i: ref[step, start:stop]


def piece_of(ref, i):
    return ref[i]


def fixed(step):
    return lambda ref, i: ref[step]


def pack_kernel(devices, loads, store, columns, extra):
    grid, features, partition, node = loads
    channels, cells = grid.target.shape
    fanout = partition.target.shape[0]
    links = cells * fanout
    width = columns.shape[0]
    slots = 2 * links
    capacity = slots // devices
    place = iota((cells, links), 1)
    repeat = jnp.where(
        functools.reduce(
            jnp.logical_or,
            [place == iota((cells, links), 0) + k * cells for k in range(fanout)],
        ),
        1.0,
        0.0,
    ).astype(bf16)
    order = iota((links, links), 0)
    turn = iota((links, links), 1)
    upper = jnp.where(order <= turn, 1.0, 0.0).astype(bf16)
    spread = jnp.where(order == turn % cells * fanout + turn // cells, 1.0, 0.0).astype(bf16)
    extra[...] = jnp.zeros_like(extra)
    columns[width - EXTRA - 16 : width - EXTRA, :] = jnp.zeros((16, links), bf16)
    store_pieces(extra, features()[...], LEFT_ORDER)
    target = jnp.concatenate([partition()[k : k + 1, :] for k in range(fanout)], axis=1)
    nodes = jnp.concatenate([node()[k : k + 1, :] for k in range(fanout)], axis=1) + 1
    extra[...] = dot(extra[...].astype(bf16), spread)
    extra[24:25, :] = (nodes >> 4).astype(f32)
    extra[25:26, :] = (nodes & 15).astype(f32)
    matches = jnp.where(iota((devices, links), 0) == target, 1.0, 0.0)
    counts = dot(matches.astype(bf16), upper)
    rank = jnp.sum(counts * matches, axis=0, keepdims=True).astype(jnp.int32) - 1
    slot = target * capacity + rank
    select = jnp.where(iota((slots, links), 0) == slot, 1.0, 0.0).astype(bf16)
    columns[0:channels, :] = dot(grid()[...], repeat).astype(bf16)
    columns[width - EXTRA : width, :] = extra[...].astype(bf16)
    store(0, dot(select, columns[...], 1, 1).astype(bf16))


def side_kernel(loads, store, pieces, turned, table):
    features, embed, edge_first, start, link_receiver, update_start, lists = loads[:7]
    singles, stacks = loads[7:10], loads[10:]
    owned, width = start.target.shape
    edges = features.target.shape[1]
    degree = edges // owned
    devices, slots = lists.target.shape[1:]
    pieces[...] = jnp.zeros_like(pieces)
    turned[...] = jnp.zeros_like(turned)
    table[...] = jnp.zeros_like(table)
    store_pieces(pieces, features()[...], LEFT_ORDER)
    turned[:, 0:EXTRA] = jnp.transpose(pieces[...])
    store_pieces(table, embed()[...], RIGHT_ORDER)
    matrix = table[...].astype(bf16)
    for j in range(degree):
        left = turned[pl.ds(j, owned, stride=degree), :].astype(bf16)
        edge_state = normalize(silu(dot(left, matrix))).astype(bf16)
        store(0, edge_state, j)
        store(1, (0.5 * dot(edge_state, edge_first()[...])).astype(bf16), j)
    store(2, dot(start()[...], link_receiver()[...]).astype(bf16))
    store(3, dot(start()[...], update_start()[...]))
    lists = lists()[0]
    rows = devices * slots
    row = iota((rows, 1), 0)
    picks = jnp.where(iota((rows, devices), 1) == row // slots, 1.0, 0.0).astype(bf16)
    high = dot(picks, (lists >> 4).astype(f32).astype(bf16))
    low = dot(picks, (lists & 15).astype(f32).astype(bf16))
    chosen = jnp.where(iota((rows, slots), 1) == row % slots, high * 16.0 + low, 0.0)
    column = jnp.sum(chosen, axis=1, keepdims=True).astype(jnp.int32)
    store(4, jnp.where(iota((rows, owned), 1) == column, 1.0, 0.0).astype(bf16))
    for place, load in enumerate(singles):
        store(5 + place, centred(load()[...]))
    for place, load in enumerate(stacks):
        weights = load()[...]
        store(8 + place, jnp.stack([centred(part) for part in weights], axis=0))


def update(state, summand, second, gain):
    hidden = silu(summand).astype(bf16)
    return (state.astype(f32) + gain * scale_rows(dot(hidden, second))).astype(bf16)


def send(store, base, state, sender, select):
    sent = dot(state, sender).astype(bf16) * 0.5
    store(base, dot(select, sent).astype(bf16))
    store(base + 1, sent)


def link_kernel(loads, store, first, table, messages, hidden, edge_state, picks):
    (
        terms,
        embed_first,
        link_embed,
        embed_second,
        link_sender,
        link_edge,
        receiver,
        link_second,
        base,
        update_first,
        update_second,
        gain,
        start,
        sender_first,
        select,
    ) = loads
    owned, width = start.target.shape
    slots = terms.target.shape[0]
    channels = embed_first.target.shape[0]
    tail = table.shape[0]
    lanes = iota((8, tail), 1)
    weights = jnp.where(
        lanes == tail - EXTRA + 24, 16.0, jnp.where(lanes == tail - EXTRA + 25, 1.0, 0.0)
    ).astype(bf16)
    chunks = [slice(begin, begin + 128) for begin in range(0, slots, 128)]

    def each(values, function):
        parts = [values[i : i + CHUNK, :] for i in range(0, values.shape[0], CHUNK)]
        return jnp.concatenate([function(part).astype(bf16) for part in parts], axis=0)

    table[...] = jnp.zeros_like(table)
    first[channels // 16 * 16 :, :] = jnp.zeros((width - channels // 16 * 16, width), bf16)
    first[0:channels, :] = embed_first()[...]
    store_pieces(table, link_embed()[...], RIGHT_ORDER, tail - EXTRA)
    matrix = table[...].astype(bf16)
    terms = terms()
    for rows in chunks:
        hidden[rows, :] = each(dot(terms[rows, :], first[...]), silu)
        extra = terms[rows, width - tail :]
        edge_state[rows, :] = each(dot(extra, matrix), lambda x: normalize(silu(x)))
        parts = extra.astype(f32)
        node = (
            parts[:, tail - EXTRA + 24 : tail - EXTRA + 25] * 16.0
            + parts[:, tail - EXTRA + 25 : tail - EXTRA + 26]
        ).astype(jnp.int32)
        pick = jnp.where(iota((rows.stop - rows.start, owned), 1) == node - 1, 1.0, 0.0)
        picks[rows, :] = pick.astype(bf16)
    nodes = dot(weights, terms[:, width - tail :], 1, 1)[0:1, :].astype(jnp.int32)
    collect = jnp.where(iota((owned, slots), 0) == nodes - 1, 1.0, 0.0).astype(bf16)
    for load in (embed_second, link_sender, link_edge, receiver, link_second):
        load()
    for rows in chunks:
        hidden[rows, :] = each(dot(hidden[rows, :], embed_second()[...]), scale_rows)
    for rows in chunks:
        sender = dot(hidden[rows, :], link_sender()[...]).astype(bf16).astype(f32)
        link_terms = (sender + dot(edge_state[rows, :], link_edge()[...])).astype(bf16)
        summand = link_terms.astype(f32) + dot(picks[rows, :], receiver()[...])
        hidden[rows, :] = each(summand, silu)
    for rows in chunks:
        messages[rows, :] = each(dot(hidden[rows, :], link_second()[...]), scale_rows)
    for load in (base, update_first, update_second, gain, start, sender_first, select):
        load()
    summed = dot(collect, messages[...]).astype(bf16)
    summand = base()[...] + dot(summed, update_first()[...])
    state = update(start()[...], summand, update_second()[...], gain()[0:1, :])
    store(0, state)
    send(store, 1, state, sender_first()[...], select()[...])


def local_kernel(step, last, loads, store):
    senders, state, receiver_first, sent = loads[:4]
    parts = loads[5 if step else 4]
    degree, owned = senders.target.shape
    columns = jnp.transpose(senders()[...].astype(f32)).astype(jnp.int32)
    kept = 0.5 * dot(state()[...], receiver_first()[...]).astype(bf16).astype(f32)
    if step:
        edge_first = loads[4]()[...] * 0.5
    for j in range(degree):
        local = jnp.where(iota((owned, owned), 1) == columns[:, j : j + 1], 1.0, 0.0)
        part = parts[j]()[...]
        if step:
            edge_state = (part.astype(f32) + loads[6][j]()[...].astype(f32)).astype(bf16)
            if not last:
                store(1, edge_state, j)
            part = dot(edge_state, edge_first)
        part = dot(local.astype(bf16), sent()[...]) + part.astype(f32)
        store(0, (part + kept).astype(bf16), j)


def edge_kernel(step, last, loads, store, summands, hiddens, results, total):
    senders, incoming, second, sums = loads[:4]
    (state, state_first, summed_first, update_second, gain) = loads[4:9]
    degree, owned = senders.target.shape
    rows = incoming.target.shape[0]
    columns = jnp.transpose((senders()[...] - owned).astype(f32)).astype(jnp.int32)

    def lead(j):
        pick = jnp.where(iota((owned, rows), 1) == columns[:, j : j + 1], 1.0, 0.0)
        summands[j % 2] = dot(pick.astype(bf16), incoming()[...])

    def middle(j):
        if j in (0, 2):
            for load in sums[j : 2 if j == 0 else degree]:
                load()
        if j == 4:
            for load in loads[4:]:
                load()
        part = sums[j].target
        for begin in range(0, owned, CHUNK):
            some = slice(begin, begin + CHUNK)
            summand = part[some, :].astype(f32) + summands[j % 2, some, :]
            hiddens[j % 2, some, :] = silu_of_half(summand).astype(bf16)
        results[j % 2] = dot(hiddens[j % 2], second()[...])

    def tail(j):
        def fill(target):
            for begin in range(0, owned, CHUNK):
                some = slice(begin, begin + CHUNK)
                message = scale_rows(results[j % 2, some, :])
                if target is not None:
                    message = message.astype(bf16)
                    target[some, :] = message
                    message = message.astype(f32)
                total[some, :] = message if j == 0 else total[some, :] + message

        if last:
            fill(None)
        else:
            store(3, fill, j, j % 4 != 3)

    lead(0)
    middle(0)
    for j in range(degree):
        if j + 1 < degree:
            lead(j + 1)
            middle(j + 1)
        tail(j)
    summand = dot(state()[...], state_first()[...]) + dot(
        total[...].astype(bf16), summed_first()[...]
    )
    state = update(
        state()[...], summand, update_second()[...], gain()[step + 1 : step + 2, :]
    )
    store(0, state)
    if not last:
        sender_first, select = loads[9:]
        send(store, 1, state, sender_first()[...], select()[...])


def body(
    grid_inputs,
    link_features,
    link_partition,
    link_node,
    mesh_start,
    edge_features,
    edge_senders,
    halo_lists,
    embed_first,
    embed_second,
    link_embed,
    link_first,
    link_second,
    update_first,
    update_second,
    edge_embed,
    process_first,
    process_second,
    process_update_first,
    process_update_second,
    update_gain,
):
    owned, width = mesh_start.shape
    devices = lax.axis_size("rows")
    cells = grid_inputs.shape[1]
    links = cells * link_partition.shape[1]
    slots = 2 * links
    degree = edge_senders.shape[1]
    edges = owned * degree
    halo_slots = halo_lists.shape[2]
    halo_rows = devices * halo_slots
    senders = edge_senders.T

    def exchange(values):
        values = values.reshape(devices, -1, width)
        return lax.all_to_all(values, "rows", split_axis=0, concat_axis=0, tiled=True).reshape(
            -1, width
        )

    sending = [((halo_rows, width), bf16, 1), ((owned, width), bf16, 1)]
    (packed,) = run(
        functools.partial(pack_kernel, devices),
        "pack",
        [((slots, width), bf16, 1)],
        (grid_inputs, link_features, link_partition.T, link_node.T),
        [pltpu.VMEM((width, links), bf16), pltpu.VMEM((EXTRA, links), f32)],
    )
    terms = exchange(packed)
    steps = process_first.shape[0]
    singles = (embed_second, link_second, update_second)
    stacks = (process_second, process_update_second)
    edge_state, parts, receiver, base, select, *seconds = run(
        side_kernel,
        "side",
        [
            ((degree, owned, width), bf16, degree),
            ((degree, owned, width), bf16, degree),
            ((owned, width), bf16, 1),
            ((owned, width), f32, 1),
            ((halo_rows, owned), bf16, 1),
        ]
        + [(array.shape, bf16, 1) for array in singles + stacks],
        (
            edge_features,
            edge_embed,
            (process_first, rows_of(2 * width, 3 * width, 0), 1),
            mesh_start,
            (link_first, rows_of(width, 2 * width), 1),
            (update_first, rows_of(0, width), 1),
            halo_lists,
        )
        + singles
        + stacks,
        [
            pltpu.VMEM((EXTRA, edges), f32),
            pltpu.VMEM((edges, 128), f32),
            pltpu.VMEM((128, width), f32),
        ],
        flops=10**10,
    )
    embed_second, link_second, update_second, process_second, process_update_second = seconds
    state, outgoing, sent = run(
        link_kernel,
        "link",
        [((owned, width), bf16, 1)] + sending,
        (
            terms,
            embed_first,
            link_embed,
            embed_second,
            (link_first, rows_of(0, width), 1),
            (link_first, rows_of(2 * width, 3 * width), 1),
            receiver,
            link_second,
            base,
            (update_first, rows_of(width, 2 * width), 1),
            update_second,
            update_gain,
            mesh_start,
            (process_first, rows_of(0, width, 0), 1),
            select,
        ),
        [
            pltpu.VMEM((width, width), bf16),
            pltpu.VMEM((128, width), f32),
            pltpu.VMEM((slots, width), bf16),
            pltpu.VMEM((slots, width), bf16),
            pltpu.VMEM((slots, width), bf16),
            pltpu.VMEM((slots, owned), bf16),
        ],
    )
    for step in range(steps):
        last = step + 1 == steps
        incoming = exchange(outgoing)
        extra = []
        if step:
            extra = [(process_first, rows_of(2 * width, 3 * width, step), 1)]
            parts = edge_state
        (sums, *kept) = run(
            functools.partial(local_kernel, step, last),
            f"local{step}",
            [((degree, owned, width), bf16, degree)] * (1 if last or step == 0 else 2),
            [
                senders,
                state,
                (process_first, rows_of(width, 2 * width, step), 1),
                sent,
            ]
            + extra
            + [(parts, piece_of, degree)]
            + ([(message, piece_of, degree)] if step else []),
            flops=10**10,
        )
        if kept:
            edge_state = kept[0]
        outs = [((owned, width), bf16, 1)]
        extra = []
        if not last:
            outs += sending + [((degree, owned, width), bf16, degree)]
            extra = [(process_first, rows_of(0, width, step + 1), 1), select]
        results = run(
            functools.partial(edge_kernel, step, last),
            f"edge{step}",
            outs,
            [
                senders,
                incoming,
                (process_second, fixed(step), 1),
                (sums, piece_of, degree),
                state,
                (process_update_first, rows_of(0, width, step), 1),
                (process_update_first, rows_of(width, 2 * width, step), 1),
                (process_update_second, fixed(step), 1),
                update_gain,
            ]
            + extra,
            [
                pltpu.VMEM((2, owned, width), f32),
                pltpu.VMEM((2, owned, width), bf16),
                pltpu.VMEM((2, owned, width), f32),
                pltpu.VMEM((owned, width), f32),
            ],
        )
        if last:
            return results[0]
        state, outgoing, sent, message = results


def solution(mesh):
    return jax.shard_map(
        body,
        mesh=mesh,
        in_specs=(
            P(None, ("groups", "rows")),
            P(None, "rows"),
            P("rows", None),
            P("rows", None),
            P("rows", None),
            P(None, "rows"),
            P("rows", None),
            P("rows", None, None),
        )
        + (P(),) * 13,
        out_specs=P(("groups", "rows"), None),
        check_vma=False,
    )
```
